256 devices in a mesh: ctx: 32 (over x_lo, z, core), chan: 8 (over x_hi, y).
Axes of the slice: x: 4 (x_hi: 2, x_lo: 2; x = x_hi * 2 + x_lo), y: 4, z: 8, core: 2. Of those that a mesh axis runs over, the one named last changes fastest.
Arguments:
- x_in: bfloat16 [32768, 2048], P('ctx', 'chan'), may hold values from -6 to 6
- conv_weight: float32 [4, 2048], replicated, may hold values from -3 to 3
- proj_weight: bfloat16 [2048, 320], replicated, may hold values from -0.125 to 0.125
- dt_bias: float32 [64], replicated, may hold values from -3 to 0
- decay_log: float32 [64], replicated, may hold values from -20 to -2, as said below
- skip_gain: float32 [64], replicated, may hold values from 0.5 to 1.5
- norm_gain: float32 [2048], P('chan'), may hold values from 0.5 to 1.5
- out_weight: bfloat16 [2048, 2048], P('chan'), may hold values from -0.125 to 0.125
Outputs:
- mixed: bfloat16 [32768, 2048], P('ctx', 'chan')
The draws below stay inside these ranges and needn't reach their ends.
Inputs may be any that keep to these rules, and one draw needn't show every extreme that they name: A head's decay rate is exp(decay_log).
All inputs are finite; a program needn't handle non-finite values.
Results may differ from the reference program's by a relative error of at most 0.0076.
The reference program's roundings to bfloat16 on the way count: a program that leaves them out, or rounds other values in their place, can miss the bound.
Values may be sent and summed in bfloat16 or wider, within the bound.
A program may use at most 128 MiB of HBM per device.

```python
import math
import jax
import jax.numpy as jnp
from jax import lax

H = 64
N = 128
KW = 4
D = 2048
SEQ = 32768


def draw_decay_log(key, part):
    key = jax.random.fold_in(key, 7)
    pick_key, slow_key, fast_key = jax.random.split(key, 3)
    share = 5
    slow = jax.random.randint(pick_key, (H,), 0, 10) < share
    slow_rate = jnp.exp(jax.random.uniform(slow_key, (H,), jnp.float32, math.log(0.05), math.log(2.0))) / SEQ
    fast_rate = jnp.exp(jax.random.uniform(fast_key, (H,), jnp.float32, math.log(0.03), math.log(0.1)))
    return jnp.log(jnp.where(slow, slow_rate, fast_rate)).astype(jnp.float32)


def shard_levels(own_key, extent, cuts, low, high):
    factor_of, own = 1.0, jax.random.fold_in(own_key, 6)
    for axis_at, shards_of in cuts:
        heights = jnp.exp(jax.random.uniform(jax.random.fold_in(own, axis_at), (shards_of,), jnp.float32, low / len(cuts), high / len(cuts)))
        factor_of = factor_of * jnp.repeat(heights, extent[axis_at] // shards_of).reshape([-1 if axis == axis_at else 1 for axis in range(len(extent))])
    return factor_of


def scatter_about(own_key, shape, width, reach, cuts=(), dtype=jnp.bfloat16):
    array = width * jax.random.normal(own_key, shape, jnp.float32)
    if cuts:
        array = array * shard_levels(own_key, shape, cuts, -0.22, 0.18)
    return jnp.clip(array, -reach, reach).astype(dtype)


def setup_inputs(seed: int = 0) -> dict:
    key_list = jax.random.split(jax.random.key(seed), 9)
    return {
        "x_in": scatter_about(key_list[0], (SEQ, D), 1.0, 6.0, ((0, 32), (1, 8))),
        "conv_weight": scatter_about(key_list[1], (KW, D), 0.5, 3.0, (), jnp.float32),
        "proj_weight": scatter_about(key_list[2], (D, 2 * N + H), D ** -0.5, 0.125),
        "dt_bias": jnp.clip(jax.random.uniform(key_list[3], (H,), jnp.float32, -3.0, 0.0), -3.0, 0.0),
        "decay_log": draw_decay_log(jax.random.fold_in(key_list[8], 71), 0),
        "skip_gain": jnp.clip(jax.random.uniform(key_list[5], (H,), jnp.float32, 0.5, 1.5), 0.5, 1.5),
        "norm_gain": jnp.clip(1.0 + 0.1 * jax.random.normal(key_list[6], (D,), jnp.float32), 0.5, 1.5),
        "out_weight": scatter_about(key_list[7], (D, D), D ** -0.5, 0.125, ((0, 8),)),
    }


def block_scan(conv_out, b_rows, c_rows, rates, decay):
    seq_len, heads = rates.shape
    head_dim = conv_out.shape[1] // heads
    block_len = min(256, seq_len)
    block_count = seq_len // block_len
    x_blocks = conv_out.reshape(block_count, block_len, heads, head_dim)
    b_blocks = b_rows.reshape(block_count, block_len, -1)
    c_blocks = c_rows.reshape(block_count, block_len, -1)
    a_blocks = (rates * decay[None, :]).reshape(block_count, block_len, heads)
    dt_blocks = rates.reshape(block_count, block_len, heads)
    lower = jnp.arange(block_len)[:, None] >= jnp.arange(block_len)[None, :]

    def advance(carry, item):
        carried = carry
        x_block, b_block, c_block, a_block, dt_block = item
        x_wide = x_block.astype(jnp.float32)
        cumul = jnp.cumsum(a_block, axis=0)
        scores = lax.dot_general(c_block, b_block, (((1,), (1,)), ((), ())), preferred_element_type=jnp.float32)
        segment = cumul[:, None, :] - cumul[None, :, :]
        weights = jnp.exp(jnp.where(lower[:, :, None], segment, -jnp.inf))
        weights = scores[:, :, None] * weights * dt_block[None, :, :]
        inner = jnp.einsum('tsh,shp->thp', weights, x_wide, precision=lax.Precision.HIGHEST)
        c_wide = c_block.astype(jnp.float32)
        outer = jnp.exp(cumul)[:, :, None] * jnp.einsum('tn,hnp->thp', c_wide, carried, precision=lax.Precision.HIGHEST)
        tail = jnp.exp(cumul[-1][None, :] - cumul) * dt_block
        b_wide = b_block.astype(jnp.float32)
        fresh = jnp.einsum('sn,shp->hnp', b_wide, x_wide * tail[:, :, None], precision=lax.Precision.HIGHEST)
        updated = jnp.exp(cumul[-1])[:, None, None] * carried + fresh
        return (updated, inner + outer)
    start_state = jnp.zeros((heads, b_rows.shape[1], head_dim), jnp.float32)
    final_state, outputs = lax.scan(advance, start_state, (x_blocks, b_blocks, c_blocks, a_blocks, dt_blocks))
    return outputs.reshape(seq_len, heads, head_dim)

def branch(source, conv_weight, proj_weight, dt_bias, decay_log, skip_gain):
    seq_len, channels = source.shape
    padded = jnp.concatenate([jnp.zeros((KW - 1, channels), jnp.bfloat16), source], 0)
    summed = jnp.zeros((seq_len, channels), jnp.float32)
    for tap_index in range(KW):
        summed = summed + conv_weight[tap_index][None, :] * padded[tap_index:tap_index + seq_len].astype(jnp.float32)
    conv_out = jax.nn.silu(summed).astype(jnp.bfloat16)
    proj = jnp.dot(conv_out, proj_weight, preferred_element_type=jnp.float32)
    b_rows = proj[:, :N].astype(jnp.bfloat16)
    c_rows = proj[:, N:2 * N].astype(jnp.bfloat16)
    rates = jax.nn.softplus(proj[:, 2 * N:] + dt_bias[None, :])
    decay = -jnp.exp(decay_log)
    scanned = block_scan(conv_out, b_rows, c_rows, rates, decay)
    heads = rates.shape[1]
    skipped = skip_gain[None, :, None] * conv_out.reshape(seq_len, heads, channels // heads).astype(jnp.float32)
    return (scanned + skipped).reshape(seq_len, channels)

def reference(x_in, conv_weight, proj_weight, dt_bias, decay_log, skip_gain, norm_gain, out_weight):
    forward_out = branch(x_in, conv_weight, proj_weight, dt_bias, decay_log, skip_gain)
    mirrored = jnp.flip(x_in, (0, 1))
    reverse_out = jnp.flip(branch(mirrored, conv_weight, proj_weight, dt_bias, decay_log, skip_gain), (0, 1))
    combined = forward_out + reverse_out
    squares = lax.optimization_barrier(jnp.sum(combined * combined, axis=1)) / combined.shape[1]
    normed = (combined * lax.rsqrt(squares + 1e-05)[:, None] * norm_gain[None, :]).astype(jnp.bfloat16)
    return jnp.dot(normed, out_weight, preferred_element_type=jnp.float32).astype(jnp.bfloat16)
```

```python
import functools

import jax
import jax.numpy as jnp
from jax import lax
from jax.experimental import pallas as pl
from jax.experimental.pallas import tpu as pltpu
from jax.sharding import PartitionSpec as P

F32 = jnp.float32
BF16 = jnp.bfloat16
MESH = pl.DeviceIdType.MESH
EPS = 1e-05
GROUP = 4


def mm(a, b, dims=((1,), (0,)), **kw):
    return lax.dot_general(a, b, (dims, ((), ())), preferred_element_type=F32, **kw)


def silu(v):
    return v / (1.0 + jnp.exp(-v))


def iota(shape, axis):
    return lax.broadcasted_iota(jnp.int32, shape, axis)


def kernel(
    dims,
    x_ref, cw_ref, pw_ref, prm_ref, gain_ref, w_ref, out_ref,
    xpad, xe, cbuf, cwr, xf, xr, bc, dtout, dtin, cumr, cumc, ldr, fresh, dch, yacc,
    mcat, xbd, emat, sxs, sxr, sys_, syr, stin, comb_s, comb_r, gall, wbuf, acc, obs, obr,
    xa_s, xa_r, ha_s, ha_r, g_s, g_r, w_s, w_r, wf_s, wf_r, bc_s, bc_r, dt_s, dt_r,
    sx_s, sx_r, sy_s, sy_r, cb_s, cb_r, ob_s, ob_r,
):
    NC, NJ, T, CW, D, N, HL, PP = dims
    SR = T // NJ
    HALVES = CW // 128
    RB = T // GROUP
    WC = GROUP * CW
    i = lax.axis_index("ctx")
    j = lax.axis_index("chan")
    prev_i = lax.rem(i + NC - 1, NC)
    next_i = lax.rem(i + 1, NC)
    core = lax.rem(i, 2)
    sib = i + 1 - 2 * core
    xh = j // GROUP
    yy = lax.rem(j, GROUP)

    def at(ci, cj):
        return {"ctx": ci, "chan": cj}

    def to(k):
        return lax.rem(j + k, NJ)

    def frm(k):
        return lax.rem(j + NJ - k, NJ)

    def rcopy(src, dst, ss, rs, dev):
        return pltpu.make_async_remote_copy(
            src_ref=src, dst_ref=dst, send_sem=ss, recv_sem=rs, device_id=dev, device_id_type=MESH
        )

    barrier = pltpu.get_barrier_semaphore()

    def hail(dev):
        pl.semaphore_signal(barrier, inc=1, device_id=dev, device_id_type=MESH)

    for k in range(1, NJ):
        hail(at(i, to(k)))

    def hail_ctx(k, c):
        hail(at(lax.rem(i + k, NC), j))
        return c

    lax.fori_loop(1, NC, hail_ctx, 0)

    @pl.when(j == 0)
    def _():
        for q in range(NJ):
            hail(at(prev_i, q))

    @pl.when(j == NJ - 1)
    def _():
        for q in range(NJ):
            hail(at(next_i, q))

    def win(jd):
        return pl.multiple_of(jnp.clip(SR * jd - 16, 0, T - SR - 32), 16)

    xpad[16:16 + T, :] = x_ref[...]
    xe[j, 16:SR + 48, :] = x_ref[pl.ds(win(j), SR + 32), :]
    gall[j] = gain_ref[...]
    wbuf[j] = w_ref[:, pl.ds(pl.multiple_of(xh * WC, 128), WC)]
    anti = iota((CW, CW), 0) + iota((CW, CW), 1) == CW - 1
    anti_f = jnp.where(anti, 1.0, 0.0).astype(F32)
    anti_b = anti_f.astype(BF16)
    for b in range(NJ):
        cwr[:, b * CW:(b + 1) * CW] = mm(
            cw_ref[:, (NJ - 1 - b) * CW:(NJ - b) * CW], anti_f, precision=lax.Precision.HIGHEST
        )
    er = lax.rem(iota((6 * HL, 2 * CW), 0), 2 * HL)
    ec = iota((6 * HL, 2 * CW), 1)
    head_of = ec // (CW // HL)
    target = jnp.where(head_of < HL, head_of, 3 * HL - 1 - head_of)
    emat[...] = jnp.where(er == target, 1.0, 0.0).astype(BF16)

    def expand(rows):
        hi = rows.astype(BF16)
        rest = rows - hi.astype(F32)
        mid = rest.astype(BF16)
        low = (rest - mid.astype(F32)).astype(BF16)
        return mm(jnp.concatenate([hi, mid, low], axis=0), emat[...], ((0,), (0,)))

    pl.semaphore_wait(barrier, NJ - 1 + NC - 1 + 2)

    def xa(k, jd):
        return rcopy(
            x_ref.at[pl.ds(win(jd), SR + 32), :], xe.at[j, pl.ds(16, SR + 32), :],
            xa_s.at[k], xa_r.at[k], at(i, jd),
        )

    def xa_in(k):
        return rcopy(
            x_ref.at[pl.ds(0, SR + 32), :], xe.at[frm(k), pl.ds(16, SR + 32), :],
            xa_s.at[k], xa_r.at[k], at(i, frm(k)),
        )

    lastrows, firstrows = x_ref.at[pl.ds(T - 16, 16), :], x_ref.at[pl.ds(0, 16), :]
    halo = [
        rcopy(lastrows, xpad.at[pl.ds(0, 16), :], ha_s.at[0], ha_r.at[0], at(next_i, j)),
        rcopy(firstrows, xpad.at[pl.ds(16 + T, 16), :], ha_s.at[1], ha_r.at[1], at(prev_i, j)),
    ]
    slab_pre = rcopy(
        lastrows, xe.at[j, pl.ds(0, 16), :], ha_s.at[2], ha_r.at[2 + j], at(next_i, 0)
    )
    slab_post = rcopy(
        firstrows, xe.at[j, pl.ds(SR + 48, 16), :], ha_s.at[3], ha_r.at[2 + j], at(prev_i, NJ - 1)
    )
    slab_pre.start()
    slab_post.start()
    for k in range(1, NJ):
        xa(k, to(k)).start()
    for h in halo:
        h.start()
    gains = [
        rcopy(gall.at[j], gall.at[j], g_s.at[k], g_r.at[k], at(i, to(k))) for k in range(1, NJ)
    ]
    for g in gains:
        g.start()

    def conv_pair(taps, rtaps):
        vf = taps[0:1, :] * cbuf[13:13 + SR, :]
        vr = rtaps[0:1, :] * cbuf[19:19 + SR, :]
        for k in range(1, 4):
            vf = vf + taps[k:k + 1, :] * cbuf[13 + k:13 + k + SR, :]
            vr = vr + rtaps[k:k + 1, :] * cbuf[19 - k:19 - k + SR, :]
        return silu(vf).astype(BF16), silu(vr).astype(BF16)

    own_cols = pl.ds(pl.multiple_of(j * CW, 128), CW)

    def own_conv(c, carry):
        rows = pl.ds(pl.multiple_of(c * SR, 16), SR)
        cbuf[...] = xpad[pl.ds(pl.multiple_of(c * SR, 16), SR + 32), :].astype(F32)
        f, r = conv_pair(cw_ref[:, own_cols], cwr[:, own_cols])
        xf[rows, :] = f
        xr[rows, :] = r
        return carry

    lax.fori_loop(1, NJ - 1, own_conv, 0)

    @pl.when(j == 0)
    def _():
        for q in range(NJ):
            rcopy(
                lastrows, xe.at[q, pl.ds(0, 16), :], ha_s.at[2], ha_r.at[2 + q], at(prev_i, q)
            ).wait_recv()

    @pl.when(j == NJ - 1)
    def _():
        for q in range(NJ):
            rcopy(
                firstrows, xe.at[q, pl.ds(SR + 48, 16), :], ha_s.at[3], ha_r.at[2 + q],
                at(next_i, q),
            ).wait_recv()

    @pl.when(jnp.logical_and(i == 0, j == 0))
    def _():
        for q in range(NJ):
            xe[q, 0:16, :] = jnp.zeros((16, CW), BF16)

    @pl.when(jnp.logical_and(i == NC - 1, j == NJ - 1))
    def _():
        for q in range(NJ):
            xe[q, SR + 48:SR + 64, :] = jnp.zeros((16, CW), BF16)

    start = pl.multiple_of(SR * j - win(j), 16)

    def slab(k, carry):
        pf, pr = carry

        @pl.when(k > 0)
        def _():
            xa_in(k).wait_recv()

        b = frm(k)
        cols = pl.ds(pl.multiple_of(b * CW, 128), CW)
        cbuf[...] = xe[b, pl.ds(start, SR + 32), :].astype(F32)
        f, r = conv_pair(cw_ref[:, cols], cwr[:, cols])
        flipped = mm(r, anti_b).astype(BF16)
        pf = pf + mm(f, pw_ref[pl.ds(pl.multiple_of(b * CW, 128), CW), :])
        pr = pr + mm(flipped, pw_ref[pl.ds(pl.multiple_of((NJ - 1 - b) * CW, 128), CW), :])
        return pf, pr

    wide = pw_ref.shape[1]
    pf, pr = lax.fori_loop(
        0, NJ, slab, (jnp.zeros((SR, wide), F32), jnp.zeros((SR, wide), F32))
    )
    bc[j, :, 0:2 * N] = pf[:, 0:2 * N].astype(BF16)
    bc[j, :, 2 * N:4 * N] = pr[:, 0:2 * N].astype(BF16)
    heads = HL * NJ
    raw = jnp.concatenate([pf[:, 2 * N:], pr[:, 2 * N:]], axis=1).T
    bias = jnp.concatenate([prm_ref[0], prm_ref[0]], axis=0)
    v = raw + bias
    dts = jnp.maximum(v, 0.0) + jnp.log1p(jnp.exp(-jnp.abs(v)))
    for q in range(NJ):
        dtout[q, 0:HL, :] = dts[q * HL:(q + 1) * HL, :]
        dtout[q, HL:2 * HL, :] = dts[heads + (NJ - 1 - q) * HL:heads + (NJ - q) * HL, :]
    dtin[j] = dtout[j]

    def bcx(k, slot, dev):
        return rcopy(bc.at[slot], bc.at[slot], bc_s.at[k], bc_r.at[k], at(i, dev))

    def dtx(k, slot, dev):
        return rcopy(dtout.at[dev], dtin.at[slot], dt_s.at[k], dt_r.at[k], at(i, dev))

    for k in range(1, NJ):
        dtx(k, j, to(k)).start()
        bcx(k, j, to(k)).start()

    half = pl.ds(pl.multiple_of(core * (CW // 2), 16), CW // 2)

    def wx(k, slot, dev):
        cols = pl.ds(pl.multiple_of((dev // GROUP) * WC, 128), WC)
        return rcopy(
            w_ref.at[half, cols], wbuf.at[slot, half, :], w_s.at[k], w_r.at[k], at(i, dev)
        )

    for k in range(1, NJ):
        wx(k, j, to(k)).start()

    for h in halo:
        h.wait_recv()

    @pl.when(i == 0)
    def _():
        xpad[0:16, :] = jnp.zeros((16, CW), BF16)

    @pl.when(i == NC - 1)
    def _():
        xpad[16 + T:32 + T, :] = jnp.zeros((16, CW), BF16)

    own_conv(0, 0)
    own_conv(NJ - 1, 0)

    own = pl.ds(pl.multiple_of(j * HL, 8), HL)
    mirror = pl.ds(pl.multiple_of((NJ - 1 - j) * HL, 8), HL)

    def own_rows(which):
        return jnp.concatenate([prm_ref[which, own, :], prm_ref[which, mirror, :]], axis=0)

    rate = -jnp.exp(own_rows(1))
    up = jnp.where(iota((SR, SR), 0) <= iota((SR, SR), 1), 1.0, 0.0).astype(F32)
    down = jnp.where(iota((SR, SR), 0) >= iota((SR, SR), 1), 1.0, 0.0).astype(F32)
    is_fwd = iota((2 * HL, SR), 0) < HL

    def states(k, total):
        c = frm(k)

        @pl.when(k > 0)
        def _():
            dtx(k, c, c).wait_recv()
            bcx(k, c, c).wait_recv()

        rows = pl.ds(pl.multiple_of(c * SR, 16), SR)
        dt = dtin[c]
        a = dt * rate
        cum = jnp.where(
            is_fwd,
            mm(a, up, precision=lax.Precision.HIGHEST),
            mm(a, down, precision=lax.Precision.HIGHEST),
        )
        end = jnp.broadcast_to(jnp.sum(a, axis=1, keepdims=True), (2 * HL, SR))
        cumr[c] = cum
        ldr[c] = cum - jnp.log(dt)
        cumc[c] = jnp.concatenate([cum, jnp.zeros((SR - 2 * HL, SR), F32)], axis=0).T
        tail = expand(jnp.exp(end - cum) * dt)
        whole = expand(jnp.exp(end))
        dch[c] = whole[0:8, :]
        tf = (xf[rows, :].astype(F32) * tail[:, 0:CW]).astype(BF16)
        tr = (xr[rows, :].astype(F32) * tail[:, CW:2 * CW]).astype(BF16)
        fresh[c, :, 0:CW] = mm(bc[c, :, 0:N], tf, ((0,), (0,)))
        fresh[c, :, CW:2 * CW] = mm(bc[c, :, 2 * N:3 * N], tr, ((0,), (0,)))
        return total + end

    total = lax.fori_loop(0, NJ, states, jnp.zeros((2 * HL, SR), F32))
    decay_all = expand(jnp.exp(total))[0:8, :]

    stin[...] = jnp.zeros((N, 2 * CW), F32)

    def fold(c, carry):
        r = NJ - 1 - c
        stin[:, 0:CW] = dch[c, 0:1, 0:CW] * stin[:, 0:CW] + fresh[c, :, 0:CW]
        stin[:, CW:2 * CW] = (
            dch[r, 0:1, CW:2 * CW] * stin[:, CW:2 * CW] + fresh[r, :, CW:2 * CW]
        )
        return carry

    lax.fori_loop(0, NJ, fold, 0)

    low4 = iota((8, 128), 0) < 4
    for g in range(N // 8 * HALVES):
        rr, hh = (g // HALVES) * 8, (g % HALVES) * 128
        p, q = g // PP, g % PP
        sxs[p, q, 0:8, :] = stin[rr:rr + 8, hh:hh + 128]
        sxs[p, q, 8:16, :] = stin[rr:rr + 8, CW + hh:CW + hh + 128]
        sxs[p, q, 16:24, :] = jnp.where(
            low4, decay_all[:, hh:hh + 128], decay_all[:, CW + hh:CW + hh + 128]
        )
    sxr[i] = sxs[i]

    def sx(k, slot, dev):
        return rcopy(sxs.at[dev], sxr.at[slot], sx_s.at[k], sx_r.at[k], at(dev, j))

    def sy(k, slot, dev):
        return rcopy(sys_.at[dev], syr.at[slot], sy_s.at[k], sy_r.at[k], at(dev, j))

    def sx_send(k, c):
        sx(k, i, lax.rem(i + k, NC)).start()
        return c

    lax.fori_loop(1, NC, sx_send, 0)

    low = iota((SR, SR), 0) >= iota((SR, SR), 1)
    upp = iota((SR, SR), 0) <= iota((SR, SR), 1)
    lane_head = iota((8, CW), 1) // (CW // HL)
    skips = expand(own_rows(2))[0:8, :]

    def inner(c, carry):
        rows = pl.ds(pl.multiple_of(c * SR, 16), SR)
        cols = cumc[c]
        lds = ldr[c]
        y = jnp.zeros((SR, CW), F32)
        for d, (xs, mask) in enumerate(((xf, low), (xr, upp))):
            xv = xs[rows, :]
            score = mm(bc[c, :, (2 * d + 1) * N:(2 * d + 2) * N], bc[c, :, 2 * d * N:(2 * d + 1) * N], ((1,), (1,)))
            for q in range(HL):
                row = q if d == 0 else 2 * HL - 1 - q
                seg = jnp.where(mask, cols[:, row:row + 1] - lds[row:row + 1, :], -1e30)
                mcat[:, q * SR:(q + 1) * SR] = (score * jnp.exp(seg)).astype(BF16)
                keep = jnp.where(lane_head == q, 1.0, 0.0)[0:1, :].astype(BF16)
                xbd[q * SR:(q + 1) * SR, :] = xv * keep
            y = y + mm(mcat[...], xbd[...])
            y = y + skips[0:1, d * CW:(d + 1) * CW] * xv.astype(F32)
        yacc[rows, :] = y
        return carry

    lax.fori_loop(0, NJ // 2, inner, 0)

    def sx_wait(k, c):
        s = lax.rem(i + NC - k, NC)
        sx(k, s, s).wait_recv()
        return c

    lax.fori_loop(1, NC, sx_wait, 0)

    def link(s, carry):
        ef, eb = carry
        r = NC - 1 - s
        sys_[s, :, 0:8, :] = ef
        sys_[r, :, 8:16, :] = eb
        ef = sxr[s, :, 16:17, :] * ef + sxr[s, :, 0:8, :]
        eb = sxr[r, :, 20:21, :] * eb + sxr[r, :, 8:16, :]
        return ef, eb

    zero = jnp.zeros((PP, 8, 128), F32)
    lax.fori_loop(0, NC, link, (zero, zero))
    syr[i] = sys_[i]

    def sy_send(k, c):
        sy(k, i, lax.rem(i + k, NC)).start()
        return c

    lax.fori_loop(1, NC, sy_send, 0)
    lax.fori_loop(NJ // 2, NJ, inner, 0)

    def sy_wait(k, c):
        s = lax.rem(i + NC - k, NC)
        sy(k, s, s).wait_recv()
        return c

    lax.fori_loop(1, NC, sy_wait, 0)
    for g in range(N // 8 * HALVES):
        rr, hh = (g // HALVES) * 8, (g % HALVES) * 128
        p, q = g // PP, g % PP
        stin[rr:rr + 8, hh:hh + 128] = syr[p, q, 0:8, :]
        stin[rr:rr + 8, CW + hh:CW + hh + 128] = syr[p, q, 8:16, :]

    def finish(s, carry):
        for d in range(2):
            c = s if d == 0 else NJ - 1 - s
            rows = pl.ds(pl.multiple_of(c * SR, 16), SR)
            lanes = slice(d * CW, (d + 1) * CW)
            st = stin[:, lanes]
            z = mm(bc[c, :, (2 * d + 1) * N:(2 * d + 2) * N], st.astype(BF16))
            grown = expand(jnp.exp(cumr[c]))[:, lanes]
            yacc[rows, :] = yacc[rows, :] + grown * z
            stin[:, lanes] = dch[c, 0:1, lanes] * st + fresh[c, :, lanes]
        return carry

    lax.fori_loop(0, NJ, finish, 0)
    comb_s[...] = yacc[...].astype(BF16)

    def cbx(k, slot, dev):
        rows = pl.ds(pl.multiple_of(lax.rem(dev, GROUP) * RB, 16), RB)
        return rcopy(comb_s.at[rows, :], comb_r.at[slot], cb_s.at[k], cb_r.at[k], at(i, dev))

    for k in range(1, NJ):
        cbx(k, j, to(k)).start()
    comb_r[j] = comb_s[pl.ds(pl.multiple_of(yy * RB, 16), RB), :]

    def wfx(k, which):
        s = frm(k)
        part = pl.ds(pl.multiple_of(which * (CW // 2), 16), CW // 2)
        return rcopy(
            wbuf.at[s, part, :], wbuf.at[s, part, :], wf_s.at[k], wf_r.at[k], at(sib, j)
        )

    for k in range(1, NJ):
        wx(k, frm(k), frm(k)).wait_recv()
        wfx(k, core).start()
    for k in range(1, NJ):
        s = frm(k)
        rcopy(gall.at[s], gall.at[s], g_s.at[k], g_r.at[k], at(i, s)).wait_recv()

    acc[...] = jnp.zeros((RB, WC), F32)

    def project(k, squares):
        @pl.when(k > 0)
        def _():
            cbx(k, frm(k), frm(k)).wait_recv()
            wfx(k, 1 - core).wait_recv()

        b = frm(k)
        value = comb_r[b].astype(F32)
        scaled = (value * gall[b, 0:1, :]).astype(BF16)
        acc[...] += mm(scaled, wbuf[b])
        return squares + jnp.sum(value * value, axis=1, keepdims=True)

    squares = lax.fori_loop(0, NJ, project, jnp.zeros((RB, 1), F32))
    scale = lax.rsqrt(squares / D + EPS)
    for q in range(GROUP):
        obs[q] = (acc[:, q * CW:(q + 1) * CW] * scale).astype(BF16)

    def obx(k, slot, dest):
        return rcopy(
            obs.at[dest], obr.at[slot], ob_s.at[k], ob_r.at[k], at(i, xh * GROUP + dest)
        )

    for k in range(1, GROUP):
        obx(k, yy, lax.rem(yy + k, GROUP)).start()
    out_ref[pl.ds(pl.multiple_of(yy * RB, 16), RB), :] = obs[yy]
    for k in range(1, GROUP):
        s = lax.rem(yy + GROUP - k, GROUP)
        obx(k, s, s).wait_recv()
        out_ref[pl.ds(pl.multiple_of(s * RB, 16), RB), :] = obr[s]

    slab_pre.wait_send()
    slab_post.wait_send()
    for h in halo:
        h.wait_send()
    for g in gains:
        g.wait_send()
    for k in range(1, NJ):
        xa(k, to(k)).wait_send()
        dtx(k, j, to(k)).wait_send()
        bcx(k, j, to(k)).wait_send()
        wx(k, j, to(k)).wait_send()
        wfx(k, core).wait_send()
        cbx(k, j, to(k)).wait_send()

    def sent(k, c):
        dev = lax.rem(i + k, NC)
        sx(k, i, dev).wait_send()
        sy(k, i, dev).wait_send()
        return c

    lax.fori_loop(1, NC, sent, 0)
    for k in range(1, GROUP):
        obx(k, yy, lax.rem(yy + k, GROUP)).wait_send()


def shards(x_in, conv_weight, proj_weight, dt_bias, decay_log, skip_gain, norm_gain, out_weight):
    T, CW = x_in.shape
    D = conv_weight.shape[1]
    H = dt_bias.shape[0]
    N = (proj_weight.shape[1] - H) // 2
    NC, NJ = lax.axis_size("ctx"), lax.axis_size("chan")
    HL = H // NJ
    SR = T // NJ
    PP = (N // 8) * (CW // 128) // NC
    RB, WC = T // GROUP, GROUP * CW
    prm = jnp.broadcast_to(jnp.stack([dt_bias, decay_log, skip_gain])[:, :, None], (3, H, 128))
    gain = jnp.broadcast_to(norm_gain[None, :], (8, CW))
    dma = pltpu.SemaphoreType.DMA
    vm = pltpu.VMEM
    scratch = [
        vm((T + 32, CW), BF16), vm((NJ, SR + 64, CW), BF16), vm((SR + 32, CW), F32),
        vm((4, D), F32), vm((T, CW), BF16), vm((T, CW), BF16),
        vm((NJ, SR, 4 * N), BF16), vm((NJ, 2 * HL, SR), F32), vm((NJ, 2 * HL, SR), F32),
        vm((NJ, 2 * HL, SR), F32), vm((NJ, SR, 128), F32), vm((NJ, 2 * HL, SR), F32),
        vm((NJ, N, 2 * CW), F32), vm((NJ, 8, 2 * CW), F32), vm((T, CW), F32),
        vm((SR, HL * SR), BF16), vm((HL * SR, CW), BF16), vm((6 * HL, 2 * CW), BF16),
        vm((NC, PP, 24, 128), F32), vm((NC, PP, 24, 128), F32),
        vm((NC, PP, 16, 128), F32), vm((NC, PP, 16, 128), F32), vm((N, 2 * CW), F32),
        vm((T, CW), BF16), vm((NJ, RB, CW), BF16), vm((NJ, 8, CW), F32),
        vm((NJ, CW, WC), BF16), vm((RB, WC), F32),
        vm((GROUP, RB, CW), BF16), vm((GROUP, RB, CW), BF16),
        dma((NJ,)), dma((NJ,)), dma((4,)), dma((2 + NJ,)), dma((NJ,)), dma((NJ,)),
        dma((NJ,)), dma((NJ,)), dma((NJ,)), dma((NJ,)), dma((NJ,)), dma((NJ,)),
        dma((NJ,)), dma((NJ,)), dma((NC,)), dma((NC,)), dma((NC,)), dma((NC,)),
        dma((NJ,)), dma((NJ,)), dma((GROUP,)), dma((GROUP,)),
    ]
    return pl.pallas_call(
        functools.partial(kernel, (NC, NJ, T, CW, D, N, HL, PP)),
        out_shape=jax.ShapeDtypeStruct((T, CW), BF16),
        in_specs=[pl.BlockSpec(memory_space=pltpu.VMEM)] * 6,
        out_specs=pl.BlockSpec(memory_space=pltpu.VMEM),
        scratch_shapes=scratch,
        compiler_params=pltpu.CompilerParams(
            collective_id=0, has_side_effects=True, vmem_limit_bytes=50 * 1024 * 1024
        ),
        cost_estimate=pl.CostEstimate(
            flops=4 * T * D * CW, bytes_accessed=8 * T * CW, transcendentals=16 * T * SR
        ),
    )(x_in, conv_weight, proj_weight, prm, gain, out_weight)


def solution(mesh):
    in_specs = (P("ctx", "chan"), P(), P(), P(), P(), P(), P("chan"), P("chan", None))
    out_specs = P("ctx", "chan")
    return jax.shard_map(shards, mesh=mesh, in_specs=in_specs, out_specs=out_specs, check_vma=False)
```

```python
import functools

import jax
import jax.numpy as jnp
from jax import lax
from jax.experimental import pallas as pl
from jax.experimental.pallas import tpu as pltpu
from jax.sharding import PartitionSpec as P

F32 = jnp.float32
BF16 = jnp.bfloat16
MESH = pl.DeviceIdType.MESH
EPS = 1e-05
GROUP = 4


def mm(a, b, dims=((1,), (0,)), **kw):
    return lax.dot_general(a, b, (dims, ((), ())), preferred_element_type=F32, **kw)


def silu(v):
    return v / (1.0 + jnp.exp(-v))


def iota(shape, axis):
    return lax.broadcasted_iota(jnp.int32, shape, axis)


def kernel(
    dims,
    x_ref, cw_ref, pw_ref, bias_ref, decay_ref, skip_ref, gain_ref, w_ref, out_ref,
    xpad, xe, cbuf, cwr, xf, xr, bb, cc, dtout, dtin, cumr, cumc, ldr, fresh, dch, yacc,
    mcat, xbd, emat, sxs, sxr, sys_, syr, stin, comb_s, comb_r, gall, wbuf, acc, obs, obr, dec_tile, linked, sqs,
    xa_s, xa_r, ha_s, ha_r, g_s, g_r, w_s, w_r, wf_s, wf_r, bb_s, bb_r, cc_s, cc_r, dt_s, dt_r,
    sx_s, sx_r, sy_s, sy_r, cb_s, cb_r, ob_s, ob_r, pwv, pwt, prm, lc,
):
    NC, NJ, T, CW, D, N, HL, PP = dims
    SR = T // NJ
    HALVES = CW // 128
    RB = T // GROUP
    WC = GROUP * CW
    i = lax.axis_index("ctx")
    j = lax.axis_index("chan")
    prev_i = lax.rem(i + NC - 1, NC)
    next_i = lax.rem(i + 1, NC)
    core = lax.rem(i, 2)
    sib = i + 1 - 2 * core
    xh = j // GROUP
    yy = lax.rem(j, GROUP)

    def at(ci, cj):
        return {"ctx": ci, "chan": cj}

    def to(k):
        return lax.rem(j + k, NJ)

    def frm(k):
        return lax.rem(j + NJ - k, NJ)

    def rcopy(src, dst, ss, rs, dev):
        return pltpu.make_async_remote_copy(
            src_ref=src, dst_ref=dst, send_sem=ss, recv_sem=rs, device_id=dev, device_id_type=MESH
        )

    barrier = pltpu.get_barrier_semaphore()

    def hail(dev):
        pl.semaphore_signal(barrier, inc=1, device_id=dev, device_id_type=MESH)

    for k in range(1, NJ):
        hail(at(i, to(k)))

    def hail_ctx(k, c):
        hail(at(lax.rem(i + k, NC), j))
        return c

    lax.fori_loop(1, NC, hail_ctx, 0)

    @pl.when(j == 0)
    def _():
        for q in range(NJ):
            hail(at(prev_i, q))

    @pl.when(j == NJ - 1)
    def _():
        for q in range(NJ):
            hail(at(next_i, q))

    def win(jd):
        return pl.multiple_of(jnp.clip(SR * jd - 16, 0, T - SR - 32), 16)

    own_wide = pl.ds(pl.multiple_of(xh * WC, 128), WC)
    here = [
        pltpu.make_async_copy(x_ref, xpad.at[pl.ds(16, T), :], lc.at[0]),
        pltpu.make_async_copy(
            x_ref.at[pl.ds(win(j), SR + 32), :], xe.at[j, pl.ds(16, SR + 32), :], lc.at[1]
        ),
        pltpu.make_async_copy(pw_ref, pwt, lc.at[2]),
        pltpu.make_async_copy(w_ref.at[:, own_wide], wbuf.at[j], lc.at[3]),
    ]
    for h in here:
        h.start()
    gall[j] = jnp.broadcast_to(1.0 / (gain_ref[...] * gain_ref[...]), (8, CW))
    heads = HL * NJ
    eye = iota((heads, heads), 0) == iota((heads, heads), 1)
    for q, ref in enumerate((bias_ref, decay_ref, skip_ref)):
        row = jnp.broadcast_to(ref[...], (heads, heads))
        column = jnp.sum(jnp.where(eye, row, 0.0), axis=1, keepdims=True)
        prm[q] = jnp.broadcast_to(column, (heads, 128))
    anti = iota((CW, CW), 0) + iota((CW, CW), 1) == CW - 1
    anti_f = jnp.where(anti, 1.0, 0.0).astype(F32)
    anti_b = anti_f.astype(BF16)
    for b in range(NJ):
        cwr[:, b * CW:(b + 1) * CW] = mm(
            cw_ref[:, (NJ - 1 - b) * CW:(NJ - b) * CW], anti_f, precision=lax.Precision.HIGHEST
        )
    er = lax.rem(iota((6 * HL, 2 * CW), 0), 2 * HL)
    ec = iota((6 * HL, 2 * CW), 1)
    head_of = ec // (CW // HL)
    target = jnp.where(head_of < HL, head_of, 3 * HL - 1 - head_of)
    emat[...] = jnp.where(er == target, 1.0, 0.0).astype(BF16)

    def expand(rows):
        hi = rows.astype(BF16)
        rest = rows - hi.astype(F32)
        mid = rest.astype(BF16)
        low = (rest - mid.astype(F32)).astype(BF16)
        return mm(jnp.concatenate([hi, mid, low], axis=0), emat[...], ((0,), (0,)))

    here[2].wait()
    for b in range(NJ):
        pwv[b * CW:(b + 1) * CW, :] = pwt[:, b * CW:(b + 1) * CW].T

    pl.semaphore_wait(barrier, NJ - 1 + NC - 1 + 2)

    def xa(k, jd):
        return rcopy(
            x_ref.at[pl.ds(win(jd), SR + 32), :], xe.at[j, pl.ds(16, SR + 32), :],
            xa_s.at[k], xa_r.at[k], at(i, jd),
        )

    def xa_in(k):
        return rcopy(
            x_ref.at[pl.ds(0, SR + 32), :], xe.at[frm(k), pl.ds(16, SR + 32), :],
            xa_s.at[k], xa_r.at[k], at(i, frm(k)),
        )

    lastrows, firstrows = x_ref.at[pl.ds(T - 16, 16), :], x_ref.at[pl.ds(0, 16), :]
    halo = [
        rcopy(lastrows, xpad.at[pl.ds(0, 16), :], ha_s.at[0], ha_r.at[0], at(next_i, j)),
        rcopy(firstrows, xpad.at[pl.ds(16 + T, 16), :], ha_s.at[1], ha_r.at[1], at(prev_i, j)),
    ]
    slab_pre = rcopy(
        lastrows, xe.at[j, pl.ds(0, 16), :], ha_s.at[2], ha_r.at[2 + j], at(next_i, 0)
    )
    slab_post = rcopy(
        firstrows, xe.at[j, pl.ds(SR + 48, 16), :], ha_s.at[3], ha_r.at[2 + j], at(prev_i, NJ - 1)
    )
    slab_pre.start()
    slab_post.start()
    for k in range(1, NJ):
        xa(k, to(k)).start()
    for h in halo:
        h.start()
    gains = [
        rcopy(gall.at[j], gall.at[j], g_s.at[k], g_r.at[k], at(i, to(k))) for k in range(1, NJ)
    ]
    for g in gains:
        g.start()

    def conv_pair(taps, rtaps):
        vf = taps[0:1, :] * cbuf[13:13 + SR, :]
        vr = rtaps[0:1, :] * cbuf[19:19 + SR, :]
        for k in range(1, 4):
            vf = vf + taps[k:k + 1, :] * cbuf[13 + k:13 + k + SR, :]
            vr = vr + rtaps[k:k + 1, :] * cbuf[19 - k:19 - k + SR, :]
        return silu(vf).astype(BF16), silu(vr).astype(BF16)

    own_cols = pl.ds(pl.multiple_of(j * CW, 128), CW)

    def own_conv(c, carry):
        rows = pl.ds(pl.multiple_of(c * SR, 16), SR)
        cbuf[...] = xpad[pl.ds(pl.multiple_of(c * SR, 16), SR + 32), :].astype(F32)
        f, r = conv_pair(cw_ref[:, own_cols], cwr[:, own_cols])
        xf[rows, :] = f
        xr[rows, :] = r
        return carry

    here[0].wait()
    lax.fori_loop(1, NJ - 1, own_conv, 0)

    @pl.when(j == 0)
    def _():
        for q in range(NJ):
            rcopy(
                lastrows, xe.at[q, pl.ds(0, 16), :], ha_s.at[2], ha_r.at[2 + q], at(prev_i, q)
            ).wait_recv()

    @pl.when(j == NJ - 1)
    def _():
        for q in range(NJ):
            rcopy(
                firstrows, xe.at[q, pl.ds(SR + 48, 16), :], ha_s.at[3], ha_r.at[2 + q],
                at(next_i, q),
            ).wait_recv()

    @pl.when(jnp.logical_and(i == 0, j == 0))
    def _():
        for q in range(NJ):
            xe[q, 0:16, :] = jnp.zeros((16, CW), BF16)

    @pl.when(jnp.logical_and(i == NC - 1, j == NJ - 1))
    def _():
        for q in range(NJ):
            xe[q, SR + 48:SR + 64, :] = jnp.zeros((16, CW), BF16)

    start = pl.multiple_of(SR * j - win(j), 16)
    here[1].wait()

    def slab(k, carry):
        pf, pr = carry

        @pl.when(k > 0)
        def _():
            xa_in(k).wait_recv()

        b = frm(k)
        cols = pl.ds(pl.multiple_of(b * CW, 128), CW)
        cbuf[...] = xe[b, pl.ds(start, SR + 32), :].astype(F32)
        f, r = conv_pair(cw_ref[:, cols], cwr[:, cols])
        flipped = mm(r, anti_b).astype(BF16)
        pf = pf + mm(f, pwv[pl.ds(pl.multiple_of(b * CW, 128), CW), :])
        pr = pr + mm(flipped, pwv[pl.ds(pl.multiple_of((NJ - 1 - b) * CW, 128), CW), :])
        return pf, pr

    wide = pwv.shape[1]
    pf, pr = lax.fori_loop(
        0, NJ, slab, (jnp.zeros((SR, wide), F32), jnp.zeros((SR, wide), F32))
    )
    bb[j, :, 0:N] = pf[:, 0:N].astype(BF16)
    bb[j, :, N:2 * N] = pr[:, 0:N].astype(BF16)
    cc[j, :, 0:N] = pf[:, N:2 * N].astype(BF16)
    cc[j, :, N:2 * N] = pr[:, N:2 * N].astype(BF16)
    raw = jnp.concatenate([pf[:, 2 * N:], pr[:, 2 * N:]], axis=1).T
    bias = jnp.concatenate([prm[0], prm[0]], axis=0)
    v = raw + bias
    dts = jnp.maximum(v, 0.0) + jnp.log1p(jnp.exp(-jnp.abs(v)))
    for q in range(NJ):
        dtout[q, 0:HL, :] = dts[q * HL:(q + 1) * HL, :]
        dtout[q, HL:2 * HL, :] = dts[heads + (NJ - 1 - q) * HL:heads + (NJ - q) * HL, :]
    dtin[j] = dtout[j]

    def bbx(k, slot, dev):
        return rcopy(bb.at[slot], bb.at[slot], bb_s.at[k], bb_r.at[k], at(i, dev))

    def ccx(k, slot, dev):
        return rcopy(cc.at[slot], cc.at[slot], cc_s.at[k], cc_r.at[k], at(i, dev))

    def dtx(k, slot, dev):
        return rcopy(dtout.at[dev], dtin.at[slot], dt_s.at[k], dt_r.at[k], at(i, dev))

    for k in range(1, NJ):
        dtx(k, j, to(k)).start()
        bbx(k, j, to(k)).start()

    half = pl.ds(pl.multiple_of(core * (CW // 2), 16), CW // 2)

    def wx(k, slot, dev):
        cols = pl.ds(pl.multiple_of((dev // GROUP) * WC, 128), WC)
        return rcopy(
            w_ref.at[half, cols], wbuf.at[slot, half, :], w_s.at[k], w_r.at[k], at(i, dev)
        )

    for h in halo:
        h.wait_recv()

    @pl.when(i == 0)
    def _():
        xpad[0:16, :] = jnp.zeros((16, CW), BF16)

    @pl.when(i == NC - 1)
    def _():
        xpad[16 + T:32 + T, :] = jnp.zeros((16, CW), BF16)

    own_conv(0, 0)
    own_conv(NJ - 1, 0)

    own = pl.ds(pl.multiple_of(j * HL, 8), HL)
    mirror = pl.ds(pl.multiple_of((NJ - 1 - j) * HL, 8), HL)

    def own_rows(which):
        return jnp.concatenate([prm[which, own, :], prm[which, mirror, :]], axis=0)

    rate = -jnp.exp(own_rows(1))
    up = jnp.where(iota((SR, SR), 0) <= iota((SR, SR), 1), 1.0, 0.0).astype(F32)
    down = jnp.where(iota((SR, SR), 0) >= iota((SR, SR), 1), 1.0, 0.0).astype(F32)
    is_fwd = iota((2 * HL, SR), 0) < HL

    def states(k, total):
        c = frm(k)

        @pl.when(k > 0)
        def _():
            dtx(k, c, c).wait_recv()
            bbx(k, c, c).wait_recv()
            ccx(k, j, to(k)).start()

        rows = pl.ds(pl.multiple_of(c * SR, 16), SR)
        dt = dtin[c]
        a = dt * rate
        cum = jnp.where(
            is_fwd,
            mm(a, up, precision=lax.Precision.HIGHEST),
            mm(a, down, precision=lax.Precision.HIGHEST),
        )
        end = jnp.broadcast_to(jnp.sum(a, axis=1, keepdims=True), (2 * HL, SR))
        cumr[c] = cum
        ldr[c] = cum - jnp.log(dt)
        cumc[c] = jnp.concatenate([cum, jnp.zeros((SR - 2 * HL, SR), F32)], axis=0).T
        tail = expand(jnp.exp(end - cum) * dt)
        whole = expand(jnp.exp(end))
        dch[c] = whole[0:8, :]
        tf = (xf[rows, :].astype(F32) * tail[:, 0:CW]).astype(BF16)
        tr = (xr[rows, :].astype(F32) * tail[:, CW:2 * CW]).astype(BF16)
        fresh[c, :, 0:CW] = mm(bb[c, :, 0:N], tf, ((0,), (0,)))
        fresh[c, :, CW:2 * CW] = mm(bb[c, :, N:2 * N], tr, ((0,), (0,)))
        return total + end

    total = lax.fori_loop(0, NJ, states, jnp.zeros((2 * HL, SR), F32))
    decay_all = expand(jnp.exp(total))[0:16, :]

    stin[...] = jnp.zeros((N, 2 * CW), F32)

    def fold(c, carry):
        r = NJ - 1 - c
        stin[:, 0:CW] = dch[c, 0:1, 0:CW] * stin[:, 0:CW] + fresh[c, :, 0:CW]
        stin[:, CW:2 * CW] = (
            dch[r, 0:1, CW:2 * CW] * stin[:, CW:2 * CW] + fresh[r, :, CW:2 * CW]
        )
        return carry

    lax.fori_loop(0, NJ, fold, 0)

    place = iota((16, 128), 0)
    ahead = lax.rem(place, 4) < 2
    for g in range(N // 8 * HALVES):
        rr, hh = (g // HALVES) * 8, (g % HALVES) * 128
        p, q = g // PP, g % PP
        both = jnp.concatenate(
            [stin[rr:rr + 8, hh:hh + 128], stin[rr:rr + 8, CW + hh:CW + hh + 128]], axis=0
        )
        sxs[p, q, 0:16, :] = both.astype(BF16)
        if rr == 0:
            dec = jnp.where(
                ahead, decay_all[:, hh:hh + 128], decay_all[:, CW + hh:CW + hh + 128]
            )
            first = dec.astype(BF16).astype(F32)
            second = (dec - first).astype(BF16).astype(F32)
            third = dec - first - second
            dec_tile[hh // 128] = jnp.where(
                place < 4, first, jnp.where(place < 8, second, third)
            ).astype(BF16)
        sxs[p, q, 16:32, :] = dec_tile[hh // 128]
    sxr[i] = sxs[i]

    def sx(k, slot, dev):
        return rcopy(sxs.at[dev], sxr.at[slot], sx_s.at[k], sx_r.at[k], at(dev, j))

    def sy(k, slot, dev):
        return rcopy(sys_.at[dev], syr.at[slot], sy_s.at[k], sy_r.at[k], at(dev, j))

    def sx_send(k, c):
        sx(k, i, lax.rem(i + k, NC)).start()
        return c

    lax.fori_loop(1, NC, sx_send, 0)

    low = iota((SR, SR), 0) >= iota((SR, SR), 1)
    upp = iota((SR, SR), 0) <= iota((SR, SR), 1)
    lane_head = iota((8, CW), 1) // (CW // HL)
    skips = expand(own_rows(2))[0:8, :]

    def inner(k, carry):
        c = frm(k)

        @pl.when(k > 0)
        def _():
            ccx(k, c, c).wait_recv()

            @pl.when(k < NJ // 2)
            def _():
                wx(2 * k, j, to(2 * k)).start()

        @pl.when(k < NJ // 2)
        def _():
            wx(2 * k + 1, j, to(2 * k + 1)).start()

        rows = pl.ds(pl.multiple_of(c * SR, 16), SR)
        cols = cumc[c]
        lds = ldr[c]
        y = jnp.zeros((SR, CW), F32)
        for d, (xs, mask) in enumerate(((xf, low), (xr, upp))):
            xv = xs[rows, :]
            part = slice(d * N, (d + 1) * N)
            score = mm(cc[c, :, part], bb[c, :, part], ((1,), (1,)))
            for q in range(HL):
                row = q if d == 0 else 2 * HL - 1 - q
                seg = jnp.where(mask, cols[:, row:row + 1] - lds[row:row + 1, :], -1e30)
                mcat[:, q * SR:(q + 1) * SR] = (score * jnp.exp(seg)).astype(BF16)
                keep = jnp.where(lane_head == q, 1.0, 0.0)[0:1, :].astype(BF16)
                xbd[q * SR:(q + 1) * SR, :] = xv * keep
            y = y + mm(mcat[...], xbd[...])
            y = y + skips[0:1, d * CW:(d + 1) * CW] * xv.astype(F32)
        yacc[rows, :] = y
        return carry

    lax.fori_loop(0, NJ // 2, inner, 0)

    def sx_wait(k, c):
        s = lax.rem(i + NC - k, NC)
        sx(k, s, s).wait_recv()
        return c

    lax.fori_loop(1, NC, sx_wait, 0)

    def link(s, carry):
        ef, eb = carry
        r = NC - 1 - s
        linked[s, :, 0:8, :] = ef
        linked[r, :, 8:16, :] = eb
        vf, vb = sxr[s].astype(F32), sxr[r].astype(F32)
        df = vf[:, 16:17, :] + vf[:, 20:21, :] + vf[:, 24:25, :]
        db = vb[:, 18:19, :] + vb[:, 22:23, :] + vb[:, 26:27, :]
        ef = df * ef + vf[:, 0:8, :]
        eb = db * eb + vb[:, 8:16, :]
        return ef, eb

    zero = jnp.zeros((PP, 8, 128), F32)
    lax.fori_loop(0, NC, link, (zero, zero))
    sys_[...] = linked[...].astype(BF16)
    syr[i] = sys_[i]

    def sy_send(k, c):
        sy(k, i, lax.rem(i + k, NC)).start()
        return c

    lax.fori_loop(1, NC, sy_send, 0)
    lax.fori_loop(NJ // 2, NJ, inner, 0)

    def sy_wait(k, c):
        s = lax.rem(i + NC - k, NC)
        sy(k, s, s).wait_recv()
        return c

    lax.fori_loop(1, NC, sy_wait, 0)
    for g in range(N // 8 * HALVES):
        rr, hh = (g // HALVES) * 8, (g % HALVES) * 128
        p, q = g // PP, g % PP
        piece = syr[p, q].astype(F32)
        stin[rr:rr + 8, hh:hh + 128] = piece[0:8]
        stin[rr:rr + 8, CW + hh:CW + hh + 128] = piece[8:16]

    def finish(s, carry):
        for d in range(2):
            c = s if d == 0 else NJ - 1 - s
            rows = pl.ds(pl.multiple_of(c * SR, 16), SR)
            lanes = slice(d * CW, (d + 1) * CW)
            st = stin[:, lanes]
            z = mm(cc[c, :, d * N:(d + 1) * N], st.astype(BF16))
            grown = expand(jnp.exp(cumr[c]))[:, lanes]
            yacc[rows, :] = yacc[rows, :] + grown * z
            stin[:, lanes] = dch[c, 0:1, lanes] * st + fresh[c, :, lanes]
        return carry

    lax.fori_loop(0, NJ, finish, 0)
    comb_s[...] = (yacc[...] * gain_ref[...]).astype(BF16)

    def cbx(k, slot, dev):
        rows = pl.ds(pl.multiple_of(lax.rem(dev, GROUP) * RB, 16), RB)
        return rcopy(comb_s.at[rows, :], comb_r.at[slot], cb_s.at[k], cb_r.at[k], at(i, dev))

    for k in range(1, NJ):
        cbx(k, j, to(k)).start()
    comb_r[j] = comb_s[pl.ds(pl.multiple_of(yy * RB, 16), RB), :]

    def wfx(k, which):
        s = frm(k)
        part = pl.ds(pl.multiple_of(which * (CW // 2), 16), CW // 2)
        return rcopy(
            wbuf.at[s, part, :], wbuf.at[s, part, :], wf_s.at[k], wf_r.at[k], at(sib, j)
        )

    for k in range(1, NJ):
        wx(k, frm(k), frm(k)).wait_recv()
        wfx(k, core).start()
    for k in range(1, NJ):
        s = frm(k)
        rcopy(gall.at[s], gall.at[s], g_s.at[k], g_r.at[k], at(i, s)).wait_recv()

    acc[...] = jnp.zeros((RB, WC), F32)
    here[3].wait()

    def project(k, carry):
        @pl.when(k > 0)
        def _():
            cbx(k, frm(k), frm(k)).wait_recv()
            wfx(k, 1 - core).wait_recv()

        b = frm(k)
        acc[...] += mm(comb_r[b], wbuf[b])
        value = comb_r[b].astype(F32)
        sqs[...] += value * value * gall[b, 0:1, :]
        return carry

    sqs[...] = jnp.zeros((RB, CW), F32)
    lax.fori_loop(0, NJ, project, 0)
    scale = lax.rsqrt(jnp.sum(sqs[...], axis=1, keepdims=True) / D + EPS)
    for q in range(GROUP):
        obs[q] = (acc[:, q * CW:(q + 1) * CW] * scale).astype(BF16)

    def obx(k, slot, dest):
        return rcopy(
            obs.at[dest], obr.at[slot], ob_s.at[k], ob_r.at[k], at(i, xh * GROUP + dest)
        )

    for k in range(1, GROUP):
        obx(k, yy, lax.rem(yy + k, GROUP)).start()
    out_ref[pl.ds(pl.multiple_of(yy * RB, 16), RB), :] = obs[yy]
    for k in range(1, GROUP):
        s = lax.rem(yy + GROUP - k, GROUP)
        obx(k, s, s).wait_recv()
        out_ref[pl.ds(pl.multiple_of(s * RB, 16), RB), :] = obr[s]

    slab_pre.wait_send()
    slab_post.wait_send()
    for h in halo:
        h.wait_send()
    for g in gains:
        g.wait_send()
    for k in range(1, NJ):
        xa(k, to(k)).wait_send()
        dtx(k, j, to(k)).wait_send()
        bbx(k, j, to(k)).wait_send()
        ccx(k, j, to(k)).wait_send()
        wx(k, j, to(k)).wait_send()
        wfx(k, core).wait_send()
        cbx(k, j, to(k)).wait_send()

    def sent(k, c):
        dev = lax.rem(i + k, NC)
        sx(k, i, dev).wait_send()
        sy(k, i, dev).wait_send()
        return c

    lax.fori_loop(1, NC, sent, 0)
    for k in range(1, GROUP):
        obx(k, yy, lax.rem(yy + k, GROUP)).wait_send()


def shards(x_in, conv_weight, proj_weight, dt_bias, decay_log, skip_gain, norm_gain, out_weight):
    T, CW = x_in.shape
    D = conv_weight.shape[1]
    H = dt_bias.shape[0]
    N = (proj_weight.shape[1] - H) // 2
    NC, NJ = lax.axis_size("ctx"), lax.axis_size("chan")
    HL = H // NJ
    SR = T // NJ
    PP = (N // 8) * (CW // 128) // NC
    RB, WC = T // GROUP, GROUP * CW
    dma = pltpu.SemaphoreType.DMA
    vm = pltpu.VMEM
    scratch = [
        vm((T + 32, CW), BF16), vm((NJ, SR + 64, CW), BF16), vm((SR + 32, CW), F32),
        vm((4, D), F32), vm((T, CW), BF16), vm((T, CW), BF16),
        vm((NJ, SR, 2 * N), BF16), vm((NJ, SR, 2 * N), BF16),
        vm((NJ, 2 * HL, SR), F32), vm((NJ, 2 * HL, SR), F32),
        vm((NJ, 2 * HL, SR), F32), vm((NJ, SR, 128), F32), vm((NJ, 2 * HL, SR), F32),
        vm((NJ, N, 2 * CW), F32), vm((NJ, 8, 2 * CW), F32), vm((T, CW), F32),
        vm((SR, HL * SR), BF16), vm((HL * SR, CW), BF16), vm((6 * HL, 2 * CW), BF16),
        vm((NC, PP, 32, 128), BF16), vm((NC, PP, 32, 128), BF16),
        vm((NC, PP, 16, 128), BF16), vm((NC, PP, 16, 128), BF16), vm((N, 2 * CW), F32),
        vm((T, CW), BF16), vm((NJ, RB, CW), BF16), vm((NJ, 8, CW), F32),
        vm((NJ, CW, WC), BF16), vm((RB, WC), F32),
        vm((GROUP, RB, CW), BF16), vm((GROUP, RB, CW), BF16),
        vm((CW // 128, 16, 128), BF16), vm((NC, PP, 16, 128), F32), vm((RB, CW), F32),
        dma((NJ,)), dma((NJ,)), dma((4,)), dma((2 + NJ,)), dma((NJ,)), dma((NJ,)),
        dma((NJ,)), dma((NJ,)), dma((NJ,)), dma((NJ,)), dma((NJ,)), dma((NJ,)),
        dma((NJ,)), dma((NJ,)), dma((NJ,)), dma((NJ,)),
        dma((NC,)), dma((NC,)), dma((NC,)), dma((NC,)),
        dma((NJ,)), dma((NJ,)), dma((GROUP,)), dma((GROUP,)),
        vm(proj_weight.shape, BF16), vm(proj_weight.shape[::-1], BF16), vm((3, H, 128), F32), dma((4,)),
    ]
    return pl.pallas_call(
        functools.partial(kernel, (NC, NJ, T, CW, D, N, HL, PP)),
        out_shape=jax.ShapeDtypeStruct((T, CW), BF16),
        in_specs=[
            pl.BlockSpec(memory_space=pl.ANY if q in (0, 2, 7) else pltpu.VMEM) for q in range(8)
        ],
        out_specs=pl.BlockSpec(memory_space=pltpu.VMEM),
        scratch_shapes=scratch,
        compiler_params=pltpu.CompilerParams(
            collective_id=0, has_side_effects=True, vmem_limit_bytes=62 * 1024 * 1024
        ),
        cost_estimate=pl.CostEstimate(
            flops=4 * T * D * CW, bytes_accessed=8 * T * CW, transcendentals=16 * T * SR
        ),
    )(
        x_in, conv_weight, proj_weight.T, dt_bias[None], decay_log[None], skip_gain[None],
        norm_gain[None], out_weight,
    )


def solution(mesh):
    in_specs = (P("ctx", "chan"), P(), P(), P(), P(), P(), P("chan"), P("chan", None))
    out_specs = P("ctx", "chan")
    return jax.shard_map(shards, mesh=mesh, in_specs=in_specs, out_specs=out_specs, check_vma=False)
```

```python
import functools

import jax
import jax.numpy as jnp
from jax import lax
from jax.experimental import pallas as pl
from jax.experimental.pallas import tpu as pltpu
from jax.sharding import PartitionSpec as P

F32 = jnp.float32
BF16 = jnp.bfloat16
MESH = pl.DeviceIdType.MESH
EPS = 1e-05
GROUP = 4


def mm(a, b, dims=((1,), (0,)), **kw):
    return lax.dot_general(a, b, (dims, ((), ())), preferred_element_type=F32, **kw)


def silu(v):
    return v / (1.0 + jnp.exp(-v))


def iota(shape, axis):
    return lax.broadcasted_iota(jnp.int32, shape, axis)


def kernel(
    dims,
    x_ref, cw_ref, pw_ref, bias_ref, decay_ref, skip_ref, gain_ref, w_ref, out_ref,
    xpad, xe, cbuf, cwr, xf, xr, bb, cc, dtout, dtin, cumr, cumc, ldr, fresh, dch, yacc,
    mcat, xbd, emat, zs, zr, es, er, xs_, xr_, st_o, ech, dec_me, dec_o, stin, comb_s, comb_r, gall, wbuf, acc, obs, obr, sqs,
    xa_s, xa_r, ha_s, ha_r, g_s, g_r, w_s, w_r, up_s, up_r, dn_s, dn_r, bb_s, bb_r, cc_s, cc_r, dt_s, dt_r,
    zx_s, zx_r, zy_s, zy_r, sb_s, sb_r, cb_s, cb_r, ob_s, ob_r, pwv, pwt, prm, lc,
):
    NC, NJ, T, CW, D, N, HL, XL, ZC = dims
    SR = T // NJ
    PR = N // 2 // ZC
    LB = 2 * CW // 128
    WR = CW // 2 // ZC
    RB = T // GROUP
    WC = GROUP * CW
    i = lax.axis_index("ctx")
    j = lax.axis_index("chan")
    prev_i = lax.rem(i + NC - 1, NC)
    next_i = lax.rem(i + 1, NC)
    core = lax.rem(i, 2)
    sib = i + 1 - 2 * core
    xlo = i // (2 * ZC)
    zi = lax.rem(i // 2, ZC)
    xh = j // GROUP
    yy = lax.rem(j, GROUP)

    def at(ci, cj):
        return {"ctx": ci, "chan": cj}

    def to(k):
        return lax.rem(j + k, NJ)

    def frm(k):
        return lax.rem(j + NJ - k, NJ)

    def rcopy(src, dst, ss, rs, dev):
        return pltpu.make_async_remote_copy(
            src_ref=src, dst_ref=dst, send_sem=ss, recv_sem=rs, device_id=dev, device_id_type=MESH
        )

    barrier = pltpu.get_barrier_semaphore()

    def hail(dev):
        pl.semaphore_signal(barrier, inc=1, device_id=dev, device_id_type=MESH)

    for k in range(1, NJ):
        hail(at(i, to(k)))

    def zpos(z):
        return xlo * (2 * ZC) + z * 2 + core

    def zto(k):
        return lax.rem(zi + k, ZC)

    def zfrm(k):
        return lax.rem(zi + ZC - k, ZC)

    for k in range(1, ZC):
        hail(at(zpos(zto(k)), j))
    across = lax.rem(i + 2 * ZC, NC)
    if XL > 1:
        hail(at(across, j))
    for c in (sib, prev_i, next_i):
        hail(at(c, j))

    @pl.when(j == 0)
    def _():
        for q in range(NJ):
            hail(at(prev_i, q))

    @pl.when(j == NJ - 1)
    def _():
        for q in range(NJ):
            hail(at(next_i, q))

    def win(jd):
        return pl.multiple_of(jnp.clip(SR * jd - 16, 0, T - SR - 32), 16)

    def wrows(z):
        return pl.ds(pl.multiple_of(core * (CW // 2) + z * WR, 16), WR)

    own_wide = pl.ds(pl.multiple_of(xh * WC, 128), WC)
    here = [
        pltpu.make_async_copy(x_ref, xpad.at[pl.ds(16, T), :], lc.at[0]),
        pltpu.make_async_copy(
            x_ref.at[pl.ds(win(j), SR + 32), :], xe.at[j, pl.ds(16, SR + 32), :], lc.at[1]
        ),
        pltpu.make_async_copy(pw_ref, pwt, lc.at[2]),
        pltpu.make_async_copy(
            w_ref.at[wrows(zi), own_wide], wbuf.at[j, wrows(zi), :], lc.at[3]
        ),
    ]
    for h in here:
        h.start()
    gall[j] = jnp.broadcast_to(1.0 / (gain_ref[...] * gain_ref[...]), (8, CW))
    heads = HL * NJ
    eye = iota((heads, heads), 0) == iota((heads, heads), 1)
    for q, ref in enumerate((bias_ref, decay_ref, skip_ref)):
        row = jnp.broadcast_to(ref[...], (heads, heads))
        column = jnp.sum(jnp.where(eye, row, 0.0), axis=1, keepdims=True)
        prm[q] = jnp.broadcast_to(column, (heads, 128))
    anti = iota((CW, CW), 0) + iota((CW, CW), 1) == CW - 1
    anti_f = jnp.where(anti, 1.0, 0.0).astype(F32)
    anti_b = anti_f.astype(BF16)
    for b in range(NJ):
        cwr[:, b * CW:(b + 1) * CW] = mm(
            cw_ref[:, (NJ - 1 - b) * CW:(NJ - b) * CW], anti_f, precision=lax.Precision.HIGHEST
        )
    head_row = lax.rem(iota((6 * HL, 2 * CW), 0), 2 * HL)
    ec = iota((6 * HL, 2 * CW), 1)
    head_of = ec // (CW // HL)
    target = jnp.where(head_of < HL, head_of, 3 * HL - 1 - head_of)
    emat[...] = jnp.where(head_row == target, 1.0, 0.0).astype(BF16)

    def expand(rows):
        hi = rows.astype(BF16)
        rest = rows - hi.astype(F32)
        mid = rest.astype(BF16)
        low = (rest - mid.astype(F32)).astype(BF16)
        return mm(jnp.concatenate([hi, mid, low], axis=0), emat[...], ((0,), (0,)))

    here[2].wait()
    for b in range(NJ):
        pwv[b * CW:(b + 1) * CW, :] = pwt[:, b * CW:(b + 1) * CW].T

    pl.semaphore_wait(barrier, NJ - 1 + ZC - 1 + XL - 1 + 3 + 2)

    def xa(k, jd):
        return rcopy(
            x_ref.at[pl.ds(win(jd), SR + 32), :], xe.at[j, pl.ds(16, SR + 32), :],
            xa_s.at[k], xa_r.at[k], at(i, jd),
        )

    def xa_in(k):
        return rcopy(
            x_ref.at[pl.ds(0, SR + 32), :], xe.at[frm(k), pl.ds(16, SR + 32), :],
            xa_s.at[k], xa_r.at[k], at(i, frm(k)),
        )

    lastrows, firstrows = x_ref.at[pl.ds(T - 16, 16), :], x_ref.at[pl.ds(0, 16), :]
    halo = [
        rcopy(lastrows, xpad.at[pl.ds(0, 16), :], ha_s.at[0], ha_r.at[0], at(next_i, j)),
        rcopy(firstrows, xpad.at[pl.ds(16 + T, 16), :], ha_s.at[1], ha_r.at[1], at(prev_i, j)),
    ]
    slab_pre = rcopy(
        lastrows, xe.at[j, pl.ds(0, 16), :], ha_s.at[2], ha_r.at[2 + j], at(next_i, 0)
    )
    slab_post = rcopy(
        firstrows, xe.at[j, pl.ds(SR + 48, 16), :], ha_s.at[3], ha_r.at[2 + j], at(prev_i, NJ - 1)
    )
    slab_pre.start()
    slab_post.start()
    for k in range(1, NJ):
        xa(k, to(k)).start()
    for h in halo:
        h.start()
    gains = [
        rcopy(gall.at[j], gall.at[j], g_s.at[k], g_r.at[k], at(i, to(k))) for k in range(1, NJ)
    ]
    for g in gains:
        g.start()

    def conv_pair(taps, rtaps):
        vf = taps[0:1, :] * cbuf[13:13 + SR, :]
        vr = rtaps[0:1, :] * cbuf[19:19 + SR, :]
        for k in range(1, 4):
            vf = vf + taps[k:k + 1, :] * cbuf[13 + k:13 + k + SR, :]
            vr = vr + rtaps[k:k + 1, :] * cbuf[19 - k:19 - k + SR, :]
        return silu(vf).astype(BF16), silu(vr).astype(BF16)

    own_cols = pl.ds(pl.multiple_of(j * CW, 128), CW)

    def own_conv(c, carry):
        rows = pl.ds(pl.multiple_of(c * SR, 16), SR)
        cbuf[...] = xpad[pl.ds(pl.multiple_of(c * SR, 16), SR + 32), :].astype(F32)
        f, r = conv_pair(cw_ref[:, own_cols], cwr[:, own_cols])
        xf[rows, :] = f
        xr[rows, :] = r
        return carry

    here[0].wait()
    lax.fori_loop(1, NJ - 1, own_conv, 0)

    @pl.when(j == 0)
    def _():
        for q in range(NJ):
            rcopy(
                lastrows, xe.at[q, pl.ds(0, 16), :], ha_s.at[2], ha_r.at[2 + q], at(prev_i, q)
            ).wait_recv()

    @pl.when(j == NJ - 1)
    def _():
        for q in range(NJ):
            rcopy(
                firstrows, xe.at[q, pl.ds(SR + 48, 16), :], ha_s.at[3], ha_r.at[2 + q],
                at(next_i, q),
            ).wait_recv()

    @pl.when(jnp.logical_and(i == 0, j == 0))
    def _():
        for q in range(NJ):
            xe[q, 0:16, :] = jnp.zeros((16, CW), BF16)

    @pl.when(jnp.logical_and(i == NC - 1, j == NJ - 1))
    def _():
        for q in range(NJ):
            xe[q, SR + 48:SR + 64, :] = jnp.zeros((16, CW), BF16)

    start = pl.multiple_of(SR * j - win(j), 16)
    here[1].wait()

    def wx(k, slot, dev):
        cols = pl.ds(pl.multiple_of((dev // GROUP) * WC, 128), WC)
        return rcopy(
            w_ref.at[wrows(zi), cols], wbuf.at[slot, wrows(zi), :], w_s.at[k], w_r.at[k],
            at(i, dev),
        )

    def up_ring(d, z):
        part = wbuf.at[:, wrows(z), :]
        return rcopy(part, part, up_s.at[d], up_r.at[d], at(zpos(zto(1)), j))

    def down_ring(d, z):
        part = wbuf.at[:, wrows(z), :]
        return rcopy(part, part, dn_s.at[d], dn_r.at[d], at(zpos(zfrm(1)), j))

    def ring_start(d):
        if d < ZC // 2:
            up_ring(d, zfrm(d)).start()
        if d < (ZC - 1) // 2:
            down_ring(d, zto(d)).start()

    def ring_wait(d):
        if d < ZC // 2:
            up_ring(d, zfrm(d + 1)).wait_recv()
        if d < (ZC - 1) // 2:
            down_ring(d, zto(d + 1)).wait_recv()

    def slab(k, carry):
        pf, pr = carry

        @pl.when(k == NJ // 2)
        def _():
            for q in range(1, NJ):
                wx(q, j, to(q)).start()

        @pl.when(k > 0)
        def _():
            xa_in(k).wait_recv()

        b = frm(k)
        cols = pl.ds(pl.multiple_of(b * CW, 128), CW)
        cbuf[...] = xe[b, pl.ds(start, SR + 32), :].astype(F32)
        f, r = conv_pair(cw_ref[:, cols], cwr[:, cols])
        flipped = mm(r, anti_b).astype(BF16)
        pf = pf + mm(f, pwv[pl.ds(pl.multiple_of(b * CW, 128), CW), :])
        pr = pr + mm(flipped, pwv[pl.ds(pl.multiple_of((NJ - 1 - b) * CW, 128), CW), :])
        return pf, pr

    wide = pwv.shape[1]
    pf, pr = lax.fori_loop(
        0, NJ, slab, (jnp.zeros((SR, wide), F32), jnp.zeros((SR, wide), F32))
    )
    bb[j, :, 0:N] = pf[:, 0:N].astype(BF16)
    bb[j, :, N:2 * N] = pr[:, 0:N].astype(BF16)
    cc[j, :, 0:N] = pf[:, N:2 * N].astype(BF16)
    cc[j, :, N:2 * N] = pr[:, N:2 * N].astype(BF16)
    raw = jnp.concatenate([pf[:, 2 * N:], pr[:, 2 * N:]], axis=1).T
    bias = jnp.concatenate([prm[0], prm[0]], axis=0)
    v = raw + bias
    dts = jnp.maximum(v, 0.0) + jnp.log1p(jnp.exp(-jnp.abs(v)))
    for q in range(NJ):
        dtout[q, 0:HL, :] = dts[q * HL:(q + 1) * HL, :]
        dtout[q, HL:2 * HL, :] = dts[heads + (NJ - 1 - q) * HL:heads + (NJ - q) * HL, :]
    dtin[j] = dtout[j]

    def bbx(k, slot, dev):
        return rcopy(bb.at[slot], bb.at[slot], bb_s.at[k], bb_r.at[k], at(i, dev))

    def ccx(k, slot, dev):
        return rcopy(cc.at[slot], cc.at[slot], cc_s.at[k], cc_r.at[k], at(i, dev))

    def dtx(k, slot, dev):
        return rcopy(dtout.at[dev], dtin.at[slot], dt_s.at[k], dt_r.at[k], at(i, dev))

    for k in range(1, NJ):
        dtx(k, j, to(k)).start()
        bbx(k, j, to(k)).start()

    for k in range(1, NJ):
        wx(k, frm(k), frm(k)).wait_recv()
    here[3].wait()
    ring_start(0)

    for h in halo:
        h.wait_recv()

    @pl.when(i == 0)
    def _():
        xpad[0:16, :] = jnp.zeros((16, CW), BF16)

    @pl.when(i == NC - 1)
    def _():
        xpad[16 + T:32 + T, :] = jnp.zeros((16, CW), BF16)

    own_conv(0, 0)
    own_conv(NJ - 1, 0)

    own = pl.ds(pl.multiple_of(j * HL, 8), HL)
    mirror = pl.ds(pl.multiple_of((NJ - 1 - j) * HL, 8), HL)

    def own_rows(which):
        return jnp.concatenate([prm[which, own, :], prm[which, mirror, :]], axis=0)

    rate = -jnp.exp(own_rows(1))
    up = jnp.where(iota((SR, SR), 0) <= iota((SR, SR), 1), 1.0, 0.0).astype(F32)
    down = jnp.where(iota((SR, SR), 0) >= iota((SR, SR), 1), 1.0, 0.0).astype(F32)
    is_fwd = iota((2 * HL, SR), 0) < HL

    def states(k, total):
        c = frm(k)

        @pl.when(k > 0)
        def _():
            dtx(k, c, c).wait_recv()
            bbx(k, c, c).wait_recv()
            ccx(k, j, to(k)).start()

        rows = pl.ds(pl.multiple_of(c * SR, 16), SR)
        dt = dtin[c]
        a = dt * rate
        cum = jnp.where(
            is_fwd,
            mm(a, up, precision=lax.Precision.HIGHEST),
            mm(a, down, precision=lax.Precision.HIGHEST),
        )
        end = jnp.broadcast_to(jnp.sum(a, axis=1, keepdims=True), (2 * HL, SR))
        cumr[c] = cum
        ldr[c] = cum - jnp.log(dt)
        cumc[c] = jnp.concatenate([cum, jnp.zeros((SR - 2 * HL, SR), F32)], axis=0).T
        tail = expand(jnp.exp(end - cum) * dt)
        whole = expand(jnp.exp(end))
        dch[c] = whole[0:8, :]
        tf = (xf[rows, :].astype(F32) * tail[:, 0:CW]).astype(BF16)
        tr = (xr[rows, :].astype(F32) * tail[:, CW:2 * CW]).astype(BF16)
        fresh[c, :, 0:CW] = mm(bb[c, :, 0:N], tf, ((0,), (0,)))
        fresh[c, :, CW:2 * CW] = mm(bb[c, :, N:2 * N], tr, ((0,), (0,)))
        return total + end

    total = lax.fori_loop(0, NJ, states, jnp.zeros((2 * HL, SR), F32))
    dec_me[...] = expand(jnp.exp(total))[0:8, :]

    stin[...] = jnp.zeros((N, 2 * CW), F32)

    def fold(c, carry):
        r = NJ - 1 - c
        stin[:, 0:CW] = dch[c, 0:1, 0:CW] * stin[:, 0:CW] + fresh[c, :, 0:CW]
        stin[:, CW:2 * CW] = (
            dch[r, 0:1, CW:2 * CW] * stin[:, CW:2 * CW] + fresh[r, :, CW:2 * CW]
        )
        return carry

    lax.fori_loop(0, NJ, fold, 0)

    swap = [
        rcopy(stin, st_o, sb_s.at[0], sb_r.at[0], at(sib, j)),
        rcopy(dec_me, dec_o, sb_s.at[1], sb_r.at[1], at(sib, j)),
    ]
    for h in swap:
        h.start()
    ring_wait(0)
    ring_start(1)
    for h in swap:
        h.wait_recv()
    mine = pl.ds(pl.multiple_of(core * (N // 2), 8), N // 2)
    s_me, s_o = stin[mine, :], st_o[mine, :]
    d_me, d_o = dec_me[0:1, :], dec_o[0:1, :]
    fwd_lane = jnp.where(iota((8, 2 * CW), 1) < CW, 1, 0)[0:1, :]
    other_last = fwd_lane == 1 - core
    pair = jnp.where(other_last, d_o * s_me + s_o, d_me * s_o + s_me)
    d_pair = jnp.broadcast_to(d_me * d_o, (8, 2 * CW))
    place = iota((8, 128), 0)
    d_tile = jnp.zeros((8, 128), F32)
    for q in range(LB):
        d_tile = jnp.where(place == q, d_pair[:, q * 128:(q + 1) * 128], d_tile)
    for p in range(ZC):
        for q in range(LB):
            zs[p, q * PR:(q + 1) * PR, :] = pair[p * PR:(p + 1) * PR, q * 128:(q + 1) * 128]
        zs[p, LB * PR:LB * PR + 8, :] = d_tile
    zr[zi] = zs[zi]

    def zx(k, slot, z):
        return rcopy(zs.at[z], zr.at[slot], zx_s.at[k], zx_r.at[k], at(zpos(z), j))

    def zy(k, slot, z):
        return rcopy(es.at[z], er.at[slot], zy_s.at[k], zy_r.at[k], at(zpos(z), j))

    for k in range(1, ZC):
        zx(k, zi, zto(k)).start()

    low = iota((SR, SR), 0) >= iota((SR, SR), 1)
    upp = iota((SR, SR), 0) <= iota((SR, SR), 1)
    lane_head = iota((8, CW), 1) // (CW // HL)
    skips = expand(own_rows(2))[0:8, :]

    def inner(k, carry):
        c = frm(k)

        @pl.when(k > 0)
        def _():
            ccx(k, c, c).wait_recv()

        rows = pl.ds(pl.multiple_of(c * SR, 16), SR)
        cols = cumc[c]
        lds = ldr[c]
        y = jnp.zeros((SR, CW), F32)
        for d, (xs, mask) in enumerate(((xf, low), (xr, upp))):
            xv = xs[rows, :]
            part = slice(d * N, (d + 1) * N)
            score = mm(cc[c, :, part], bb[c, :, part], ((1,), (1,)))
            for q in range(HL):
                row = q if d == 0 else 2 * HL - 1 - q
                seg = jnp.where(mask, cols[:, row:row + 1] - lds[row:row + 1, :], -1e30)
                mcat[:, q * SR:(q + 1) * SR] = (score * jnp.exp(seg)).astype(BF16)
                keep = jnp.where(lane_head == q, 1.0, 0.0)[0:1, :].astype(BF16)
                xbd[q * SR:(q + 1) * SR, :] = xv * keep
            y = y + mm(mcat[...], xbd[...])
            y = y + skips[0:1, d * CW:(d + 1) * CW] * xv.astype(F32)
        yacc[rows, :] = y
        return carry

    lax.fori_loop(0, 3, inner, 0)

    ring_wait(1)
    ring_start(2)
    for k in range(1, ZC):
        zx(k, zfrm(k), zfrm(k)).wait_recv()

    def chain(q, e, keep):
        order = range(ZC) if q < LB // 2 else range(ZC - 1, -1, -1)
        rows = slice(q * PR, (q + 1) * PR)
        for z in order:
            if keep:
                es[z, rows, :] = e
            e = zr[z, LB * PR + q:LB * PR + q + 1, :] * e + zr[z, rows, :]
        return e

    zero = jnp.zeros((PR, 128), F32)
    if XL > 1:
        for q in range(LB):
            xs_[q * PR:(q + 1) * PR, :] = chain(q, zero, False)
        cross = rcopy(xs_, xr_, sb_s.at[2], sb_r.at[2], at(across, j))
        cross.start()
        lax.fori_loop(3, 4, inner, 0)
        cross.wait_recv()
    for q in range(LB):
        start_from = zero
        if XL > 1:
            takes = xlo == 1 if q < LB // 2 else xlo == 0
            start_from = jnp.where(takes, xr_[q * PR:(q + 1) * PR, :], 0.0)
        chain(q, start_from, True)
    er[zi] = es[zi]
    for k in range(1, ZC):
        zy(k, zi, zto(k)).start()
    lax.fori_loop(4 if XL > 1 else 3, NJ, inner, 0)
    ring_wait(2)
    ring_start(3)
    for k in range(1, ZC):
        zy(k, zfrm(k), zfrm(k)).wait_recv()
    for p in range(ZC):
        for q in range(LB):
            ech[pl.ds(pl.multiple_of(core * (N // 2) + p * PR, 8), PR), q * 128:(q + 1) * 128] = (
                er[p, q * PR:(q + 1) * PR, :]
            )
    halves = rcopy(ech.at[mine, :], ech.at[mine, :], sb_s.at[3], sb_r.at[3], at(sib, j))
    halves.start()
    for h in swap:
        h.wait_send()
    theirs = pl.ds(pl.multiple_of((1 - core) * (N // 2), 8), N // 2)
    rcopy(ech.at[theirs, :], ech.at[theirs, :], sb_s.at[3], sb_r.at[3], at(sib, j)).wait_recv()
    other_first = fwd_lane == core
    stin[...] = jnp.where(other_first, dec_o[0:1, :] * ech[...] + st_o[...], ech[...])

    def finish(s, carry):
        for d in range(2):
            c = s if d == 0 else NJ - 1 - s
            rows = pl.ds(pl.multiple_of(c * SR, 16), SR)
            lanes = slice(d * CW, (d + 1) * CW)
            st = stin[:, lanes]
            z = mm(cc[c, :, d * N:(d + 1) * N], st.astype(BF16))
            grown = expand(jnp.exp(cumr[c]))[:, lanes]
            yacc[rows, :] = yacc[rows, :] + grown * z
            stin[:, lanes] = dch[c, 0:1, lanes] * st + fresh[c, :, lanes]
        return carry

    lax.fori_loop(0, NJ, finish, 0)
    comb_s[...] = (yacc[...] * gain_ref[...]).astype(BF16)

    def cbx(k, slot, dev):
        rows = pl.ds(pl.multiple_of(lax.rem(dev, GROUP) * RB, 16), RB)
        return rcopy(comb_s.at[rows, :], comb_r.at[slot], cb_s.at[k], cb_r.at[k], at(i, dev))

    for k in range(1, NJ):
        cbx(k, j, to(k)).start()
    comb_r[j] = comb_s[pl.ds(pl.multiple_of(yy * RB, 16), RB), :]

    ring_wait(3)
    half = pl.ds(pl.multiple_of(core * (CW // 2), 16), CW // 2)
    rest = pl.ds(pl.multiple_of((1 - core) * (CW // 2), 16), CW // 2)
    share = rcopy(wbuf.at[:, half, :], wbuf.at[:, half, :], sb_s.at[4], sb_r.at[4], at(sib, j))
    share.start()
    for k in range(1, NJ):
        s = frm(k)
        rcopy(gall.at[s], gall.at[s], g_s.at[k], g_r.at[k], at(i, s)).wait_recv()

    acc[...] = jnp.zeros((RB, WC), F32)
    rcopy(
        wbuf.at[:, rest, :], wbuf.at[:, rest, :], sb_s.at[4], sb_r.at[4], at(sib, j)
    ).wait_recv()

    def project(k, carry):
        @pl.when(k > 0)
        def _():
            cbx(k, frm(k), frm(k)).wait_recv()

        b = frm(k)
        acc[...] += mm(comb_r[b], wbuf[b])
        value = comb_r[b].astype(F32)
        sqs[...] += value * value * gall[b, 0:1, :]
        return carry

    sqs[...] = jnp.zeros((RB, CW), F32)
    lax.fori_loop(0, NJ, project, 0)
    scale = lax.rsqrt(jnp.sum(sqs[...], axis=1, keepdims=True) / D + EPS)
    for q in range(GROUP):
        obs[q] = (acc[:, q * CW:(q + 1) * CW] * scale).astype(BF16)

    def obx(k, slot, dest):
        return rcopy(
            obs.at[dest], obr.at[slot], ob_s.at[k], ob_r.at[k], at(i, xh * GROUP + dest)
        )

    for k in range(1, GROUP):
        obx(k, yy, lax.rem(yy + k, GROUP)).start()
    out_ref[pl.ds(pl.multiple_of(yy * RB, 16), RB), :] = obs[yy]
    for k in range(1, GROUP):
        s = lax.rem(yy + GROUP - k, GROUP)
        obx(k, s, s).wait_recv()
        out_ref[pl.ds(pl.multiple_of(s * RB, 16), RB), :] = obr[s]

    slab_pre.wait_send()
    slab_post.wait_send()
    for h in halo:
        h.wait_send()
    for g in gains:
        g.wait_send()
    for k in range(1, NJ):
        xa(k, to(k)).wait_send()
        dtx(k, j, to(k)).wait_send()
        bbx(k, j, to(k)).wait_send()
        ccx(k, j, to(k)).wait_send()
        wx(k, j, to(k)).wait_send()
        cbx(k, j, to(k)).wait_send()

    for k in range(1, ZC):
        zx(k, zi, zto(k)).wait_send()
        zy(k, zi, zto(k)).wait_send()
    if XL > 1:
        cross.wait_send()
    halves.wait_send()
    share.wait_send()
    for d in range(ZC // 2):
        up_ring(d, zfrm(d)).wait_send()
    for d in range((ZC - 1) // 2):
        down_ring(d, zto(d)).wait_send()
    for k in range(1, GROUP):
        obx(k, yy, lax.rem(yy + k, GROUP)).wait_send()


def shards(x_in, conv_weight, proj_weight, dt_bias, decay_log, skip_gain, norm_gain, out_weight):
    T, CW = x_in.shape
    D = conv_weight.shape[1]
    H = dt_bias.shape[0]
    N = (proj_weight.shape[1] - H) // 2
    NC, NJ = lax.axis_size("ctx"), lax.axis_size("chan")
    HL = H // NJ
    SR = T // NJ
    XL = 2 if NC >= 4 else 1
    ZC = NC // (2 * XL)
    PR, LB = N // 2 // ZC, 2 * CW // 128
    RB, WC = T // GROUP, GROUP * CW
    dma = pltpu.SemaphoreType.DMA
    vm = pltpu.VMEM
    scratch = [
        vm((T + 32, CW), BF16), vm((NJ, SR + 64, CW), BF16), vm((SR + 32, CW), F32),
        vm((4, D), F32), vm((T, CW), BF16), vm((T, CW), BF16),
        vm((NJ, SR, 2 * N), BF16), vm((NJ, SR, 2 * N), BF16),
        vm((NJ, 2 * HL, SR), F32), vm((NJ, 2 * HL, SR), F32),
        vm((NJ, 2 * HL, SR), F32), vm((NJ, SR, 128), F32), vm((NJ, 2 * HL, SR), F32),
        vm((NJ, N, 2 * CW), F32), vm((NJ, 8, 2 * CW), F32), vm((T, CW), F32),
        vm((SR, HL * SR), BF16), vm((HL * SR, CW), BF16), vm((6 * HL, 2 * CW), BF16),
        vm((ZC, LB * PR + 8, 128), F32), vm((ZC, LB * PR + 8, 128), F32),
        vm((ZC, LB * PR, 128), F32), vm((ZC, LB * PR, 128), F32),
        vm((LB * PR, 128), F32), vm((LB * PR, 128), F32),
        vm((N, 2 * CW), F32), vm((N, 2 * CW), F32), vm((8, 2 * CW), F32), vm((8, 2 * CW), F32),
        vm((N, 2 * CW), F32),
        vm((T, CW), BF16), vm((NJ, RB, CW), BF16), vm((NJ, 8, CW), F32),
        vm((NJ, CW, WC), BF16), vm((RB, WC), F32),
        vm((GROUP, RB, CW), BF16), vm((GROUP, RB, CW), BF16),
        vm((RB, CW), F32),
        dma((NJ,)), dma((NJ,)), dma((4,)), dma((2 + NJ,)), dma((NJ,)), dma((NJ,)),
        dma((NJ,)), dma((NJ,)), dma((4,)), dma((4,)), dma((4,)), dma((4,)),
        dma((NJ,)), dma((NJ,)), dma((NJ,)), dma((NJ,)), dma((NJ,)), dma((NJ,)),
        dma((ZC,)), dma((ZC,)), dma((ZC,)), dma((ZC,)), dma((5,)), dma((5,)),
        dma((NJ,)), dma((NJ,)), dma((GROUP,)), dma((GROUP,)),
        vm(proj_weight.shape, BF16), vm(proj_weight.shape[::-1], BF16), vm((3, H, 128), F32), dma((4,)),
    ]
    return pl.pallas_call(
        functools.partial(kernel, (NC, NJ, T, CW, D, N, HL, XL, ZC)),
        out_shape=jax.ShapeDtypeStruct((T, CW), BF16),
        in_specs=[
            pl.BlockSpec(memory_space=pl.ANY if q in (0, 2, 7) else pltpu.VMEM) for q in range(8)
        ],
        out_specs=pl.BlockSpec(memory_space=pltpu.VMEM),
        scratch_shapes=scratch,
        compiler_params=pltpu.CompilerParams(
            collective_id=0, has_side_effects=True, vmem_limit_bytes=62 * 1024 * 1024
        ),
        cost_estimate=pl.CostEstimate(
            flops=4 * T * D * CW, bytes_accessed=8 * T * CW, transcendentals=16 * T * SR
        ),
    )(
        x_in, conv_weight, proj_weight.T, dt_bias[None], decay_log[None], skip_gain[None],
        norm_gain[None], out_weight,
    )


def solution(mesh):
    in_specs = (P("ctx", "chan"), P(), P(), P(), P(), P(), P("chan"), P("chan", None))
    out_specs = P("ctx", "chan")
    return jax.shard_map(shards, mesh=mesh, in_specs=in_specs, out_specs=out_specs, check_vma=False)
```

```python
import functools

import jax
import jax.numpy as jnp
from jax import lax
from jax.experimental import pallas as pl
from jax.experimental.pallas import tpu as pltpu
from jax.sharding import PartitionSpec as P

F32 = jnp.float32
BF16 = jnp.bfloat16
MESH = pl.DeviceIdType.MESH
EPS = 1e-05
GROUP = 4


def mm(a, b, dims=((1,), (0,)), **kw):
    return lax.dot_general(a, b, (dims, ((), ())), preferred_element_type=F32, **kw)


def silu(v):
    return v / (1.0 + jnp.exp(-v))


def iota(shape, axis):
    return lax.broadcasted_iota(jnp.int32, shape, axis)


def kernel(
    dims,
    x_ref, cw_ref, pw_ref, bias_ref, decay_ref, skip_ref, gain_ref, w_ref, out_ref,
    xpad, xe, cbuf, cwr, xf, xr, bb, cc, dtout, dtin, cumr, cumc, ldr, fresh, dch, yacc,
    mcat, xbd, emat, zs, zr, es, er, xs_, xr_, st_o, ech, dec_me, dec_o, stin, comb_s, comb_r, gall, wbuf, acc, obs, obr, sqs, grown, sbs,
    xa_s, xa_r, ha_s, ha_r, g_s, g_r, w_s, w_r, up_s, up_r, dn_s, dn_r, bb_s, bb_r, cc_s, cc_r, dt_s, dt_r,
    zx_s, zx_r, zy_s, zy_r, sb_s, sb_r, cb_s, cb_r, ob_s, ob_r, pwv, pwt, prm, lc,
):
    NC, NJ, T, CW, D, N, HL, XL, ZC = dims
    SR = T // NJ
    PR = N // 2 // ZC
    LB = 2 * CW // 128
    WR = CW // 2 // ZC
    RB = T // GROUP
    WC = GROUP * CW
    i = lax.axis_index("ctx")
    j = lax.axis_index("chan")
    prev_i = lax.rem(i + NC - 1, NC)
    next_i = lax.rem(i + 1, NC)
    core = lax.rem(i, 2)
    sib = i + 1 - 2 * core
    xlo = i // (2 * ZC)
    zi = lax.rem(i // 2, ZC)
    xh = j // GROUP
    yy = lax.rem(j, GROUP)

    def at(ci, cj):
        return {"ctx": ci, "chan": cj}

    def to(k):
        return lax.rem(j + k, NJ)

    def frm(k):
        return lax.rem(j + NJ - k, NJ)

    def rcopy(src, dst, ss, rs, dev):
        return pltpu.make_async_remote_copy(
            src_ref=src, dst_ref=dst, send_sem=ss, recv_sem=rs, device_id=dev, device_id_type=MESH
        )

    barrier = pltpu.get_barrier_semaphore()

    def hail(dev):
        pl.semaphore_signal(barrier, inc=1, device_id=dev, device_id_type=MESH)

    for k in range(1, NJ):
        hail(at(i, to(k)))

    def zpos(z):
        return xlo * (2 * ZC) + z * 2 + core

    def zto(k):
        return lax.rem(zi + k, ZC)

    def zfrm(k):
        return lax.rem(zi + ZC - k, ZC)

    for k in range(1, ZC):
        hail(at(zpos(zto(k)), j))
    across = lax.rem(i + 2 * ZC, NC)
    if XL > 1:
        hail(at(across, j))
    for c in (sib, prev_i, next_i):
        hail(at(c, j))

    @pl.when(j == 0)
    def _():
        for q in range(NJ):
            hail(at(prev_i, q))

    @pl.when(j == NJ - 1)
    def _():
        for q in range(NJ):
            hail(at(next_i, q))

    def win(jd):
        return pl.multiple_of(jnp.clip(SR * jd - 16, 0, T - SR - 32), 16)

    def wrows(z):
        return pl.ds(pl.multiple_of(core * (CW // 2) + z * WR, 16), WR)

    own_wide = pl.ds(pl.multiple_of(xh * WC, 128), WC)
    here = [
        pltpu.make_async_copy(x_ref, xpad.at[pl.ds(16, T), :], lc.at[0]),
        pltpu.make_async_copy(
            x_ref.at[pl.ds(win(j), SR + 32), :], xe.at[j, pl.ds(16, SR + 32), :], lc.at[1]
        ),
        pltpu.make_async_copy(pw_ref, pwt, lc.at[2]),
        pltpu.make_async_copy(
            w_ref.at[wrows(zi), own_wide], wbuf.at[j, wrows(zi), :], lc.at[3]
        ),
    ]
    for h in here:
        h.start()
    gall[j] = jnp.broadcast_to(1.0 / (gain_ref[...] * gain_ref[...]), (8, CW))
    heads = HL * NJ
    eye = iota((heads, heads), 0) == iota((heads, heads), 1)
    for q, ref in enumerate((bias_ref, decay_ref, skip_ref)):
        row = jnp.broadcast_to(ref[...], (heads, heads))
        column = jnp.sum(jnp.where(eye, row, 0.0), axis=1, keepdims=True)
        prm[q] = jnp.broadcast_to(column, (heads, 128))
    anti = iota((CW, CW), 0) + iota((CW, CW), 1) == CW - 1
    anti_f = jnp.where(anti, 1.0, 0.0).astype(F32)
    anti_b = anti_f.astype(BF16)
    for b in range(NJ):
        cwr[:, b * CW:(b + 1) * CW] = mm(
            cw_ref[:, (NJ - 1 - b) * CW:(NJ - b) * CW], anti_f, precision=lax.Precision.HIGHEST
        )
    head_row = lax.rem(iota((6 * HL, 2 * CW), 0), 2 * HL)
    ec = iota((6 * HL, 2 * CW), 1)
    head_of = ec // (CW // HL)
    target = jnp.where(head_of < HL, head_of, 3 * HL - 1 - head_of)
    emat[...] = jnp.where(head_row == target, 1.0, 0.0).astype(BF16)

    def expand(rows):
        hi = rows.astype(BF16)
        rest = rows - hi.astype(F32)
        mid = rest.astype(BF16)
        low = (rest - mid.astype(F32)).astype(BF16)
        return mm(jnp.concatenate([hi, mid, low], axis=0), emat[...], ((0,), (0,)))

    pl.semaphore_wait(barrier, NJ - 1 + ZC - 1 + XL - 1 + 3 + 2)

    def xa(k, jd):
        return rcopy(
            x_ref.at[pl.ds(win(jd), SR + 32), :], xe.at[j, pl.ds(16, SR + 32), :],
            xa_s.at[k], xa_r.at[k], at(i, jd),
        )

    def xa_in(k):
        return rcopy(
            x_ref.at[pl.ds(0, SR + 32), :], xe.at[frm(k), pl.ds(16, SR + 32), :],
            xa_s.at[k], xa_r.at[k], at(i, frm(k)),
        )

    lastrows, firstrows = x_ref.at[pl.ds(T - 16, 16), :], x_ref.at[pl.ds(0, 16), :]
    halo = [
        rcopy(lastrows, xpad.at[pl.ds(0, 16), :], ha_s.at[0], ha_r.at[0], at(next_i, j)),
        rcopy(firstrows, xpad.at[pl.ds(16 + T, 16), :], ha_s.at[1], ha_r.at[1], at(prev_i, j)),
    ]
    slab_pre = rcopy(
        lastrows, xe.at[j, pl.ds(0, 16), :], ha_s.at[2], ha_r.at[2 + j], at(next_i, 0)
    )
    slab_post = rcopy(
        firstrows, xe.at[j, pl.ds(SR + 48, 16), :], ha_s.at[3], ha_r.at[2 + j], at(prev_i, NJ - 1)
    )
    slab_pre.start()
    slab_post.start()
    for k in range(1, NJ):
        xa(k, to(k)).start()
    for h in halo:
        h.start()
    gains = [
        rcopy(gall.at[j], gall.at[j], g_s.at[k], g_r.at[k], at(i, to(k))) for k in range(1, NJ)
    ]
    for g in gains:
        g.start()

    def conv_pair(taps, rtaps):
        vf = taps[0:1, :] * cbuf[13:13 + SR, :]
        vr = rtaps[0:1, :] * cbuf[19:19 + SR, :]
        for k in range(1, 4):
            vf = vf + taps[k:k + 1, :] * cbuf[13 + k:13 + k + SR, :]
            vr = vr + rtaps[k:k + 1, :] * cbuf[19 - k:19 - k + SR, :]
        return silu(vf).astype(BF16), silu(vr).astype(BF16)

    here[2].wait()
    for b in range(NJ):
        pwv[b * CW:(b + 1) * CW, :] = pwt[:, b * CW:(b + 1) * CW].T

    own_cols = pl.ds(pl.multiple_of(j * CW, 128), CW)

    def own_conv(c, carry):
        rows = pl.ds(pl.multiple_of(c * SR, 16), SR)
        cbuf[...] = xpad[pl.ds(pl.multiple_of(c * SR, 16), SR + 32), :].astype(F32)
        f, r = conv_pair(cw_ref[:, own_cols], cwr[:, own_cols])
        xf[rows, :] = f
        xr[rows, :] = r
        return carry

    here[0].wait()
    lax.fori_loop(1, NJ - 1, own_conv, 0)

    @pl.when(j == 0)
    def _():
        for q in range(NJ):
            rcopy(
                lastrows, xe.at[q, pl.ds(0, 16), :], ha_s.at[2], ha_r.at[2 + q], at(prev_i, q)
            ).wait_recv()

    @pl.when(j == NJ - 1)
    def _():
        for q in range(NJ):
            rcopy(
                firstrows, xe.at[q, pl.ds(SR + 48, 16), :], ha_s.at[3], ha_r.at[2 + q],
                at(next_i, q),
            ).wait_recv()

    @pl.when(jnp.logical_and(i == 0, j == 0))
    def _():
        for q in range(NJ):
            xe[q, 0:16, :] = jnp.zeros((16, CW), BF16)

    @pl.when(jnp.logical_and(i == NC - 1, j == NJ - 1))
    def _():
        for q in range(NJ):
            xe[q, SR + 48:SR + 64, :] = jnp.zeros((16, CW), BF16)

    start = pl.multiple_of(SR * j - win(j), 16)
    here[1].wait()

    def wx(k, slot, dev):
        cols = pl.ds(pl.multiple_of((dev // GROUP) * WC, 128), WC)
        return rcopy(
            w_ref.at[wrows(zi), cols], wbuf.at[slot, wrows(zi), :], w_s.at[k], w_r.at[k],
            at(i, dev),
        )

    def halfway(d):
        return ZC % 2 == 0 and d == ZC // 2 - 1

    def up_ring(d, z):
        part = wbuf.at[pl.ds(0, NJ // 2 if halfway(d) else NJ), wrows(z), :]
        return rcopy(part, part, up_s.at[d], up_r.at[d], at(zpos(zto(1)), j))

    def down_ring(d, z):
        first = NJ // 2 if halfway(d) else 0
        part = wbuf.at[pl.ds(first, NJ - first), wrows(z), :]
        return rcopy(part, part, dn_s.at[d], dn_r.at[d], at(zpos(zfrm(1)), j))

    def ring_start(d):
        if d < ZC // 2:
            up_ring(d, zfrm(d)).start()
        if d < ZC // 2:
            down_ring(d, zto(d)).start()

    def ring_wait(d):
        if d < ZC // 2:
            up_ring(d, zfrm(d + 1)).wait_recv()
        if d < ZC // 2:
            down_ring(d, zto(d + 1)).wait_recv()

    def slab(k, carry):
        pf, pr = carry

        @pl.when(k == NJ // 2)
        def _():
            for q in range(1, NJ):
                wx(q, j, to(q)).start()

        @pl.when(k > 0)
        def _():
            xa_in(k).wait_recv()

        b = frm(k)
        cols = pl.ds(pl.multiple_of(b * CW, 128), CW)
        cbuf[...] = xe[b, pl.ds(start, SR + 32), :].astype(F32)
        f, r = conv_pair(cw_ref[:, cols], cwr[:, cols])
        flipped = mm(r, anti_b).astype(BF16)
        pf = pf + mm(f, pwv[pl.ds(pl.multiple_of(b * CW, 128), CW), :])
        pr = pr + mm(flipped, pwv[pl.ds(pl.multiple_of((NJ - 1 - b) * CW, 128), CW), :])
        return pf, pr

    wide = pwv.shape[1]
    pf, pr = lax.fori_loop(
        0, NJ, slab, (jnp.zeros((SR, wide), F32), jnp.zeros((SR, wide), F32))
    )
    def bbx(k, slot, dev):
        return rcopy(bb.at[slot], bb.at[slot], bb_s.at[k], bb_r.at[k], at(i, dev))

    def ccx(k, slot, dev):
        return rcopy(cc.at[slot], cc.at[slot], cc_s.at[k], cc_r.at[k], at(i, dev))

    def dtx(k, slot, dev):
        return rcopy(dtout.at[dev], dtin.at[slot], dt_s.at[k], dt_r.at[k], at(i, dev))

    bb[j, :, 0:N] = pf[:, 0:N].astype(BF16)
    bb[j, :, N:2 * N] = pr[:, 0:N].astype(BF16)
    for k in range(1, NJ):
        bbx(k, j, to(k)).start()
    raw = jnp.concatenate([pf[:, 2 * N:], pr[:, 2 * N:]], axis=1).T
    bias = jnp.concatenate([prm[0], prm[0]], axis=0)
    v = raw + bias
    dts = jnp.maximum(v, 0.0) + jnp.log1p(jnp.exp(-jnp.abs(v)))
    for q in range(NJ):
        dtout[q, 0:HL, :] = dts[q * HL:(q + 1) * HL, :]
        dtout[q, HL:2 * HL, :] = dts[heads + (NJ - 1 - q) * HL:heads + (NJ - q) * HL, :]
    for k in range(1, NJ):
        dtx(k, j, to(k)).start()
    dtin[j] = dtout[j]
    cc[j, :, 0:N] = pf[:, N:2 * N].astype(BF16)
    cc[j, :, N:2 * N] = pr[:, N:2 * N].astype(BF16)

    for h in halo:
        h.wait_recv()

    @pl.when(i == 0)
    def _():
        xpad[0:16, :] = jnp.zeros((16, CW), BF16)

    @pl.when(i == NC - 1)
    def _():
        xpad[16 + T:32 + T, :] = jnp.zeros((16, CW), BF16)

    own_conv(0, 0)
    own_conv(NJ - 1, 0)

    for k in range(1, NJ):
        wx(k, frm(k), frm(k)).wait_recv()
    here[3].wait()
    ring_start(0)

    own = pl.ds(pl.multiple_of(j * HL, 8), HL)
    mirror = pl.ds(pl.multiple_of((NJ - 1 - j) * HL, 8), HL)

    def own_rows(which):
        return jnp.concatenate([prm[which, own, :], prm[which, mirror, :]], axis=0)

    rate = -jnp.exp(own_rows(1))
    up = jnp.where(iota((SR, SR), 0) <= iota((SR, SR), 1), 1.0, 0.0).astype(F32)
    down = jnp.where(iota((SR, SR), 0) >= iota((SR, SR), 1), 1.0, 0.0).astype(F32)
    is_fwd = iota((2 * HL, SR), 0) < HL

    def states(k, total):
        c = frm(k)

        @pl.when(k > 0)
        def _():
            dtx(k, c, c).wait_recv()
            bbx(k, c, c).wait_recv()
            ccx(k, j, to(k)).start()

        @pl.when(k == NJ // 2)
        def _():
            ring_wait(0)
            ring_start(1)

        rows = pl.ds(pl.multiple_of(c * SR, 16), SR)
        dt = dtin[c]
        a = dt * rate
        cum = jnp.where(
            is_fwd,
            mm(a, up, precision=lax.Precision.HIGHEST),
            mm(a, down, precision=lax.Precision.HIGHEST),
        )
        end = jnp.broadcast_to(jnp.sum(a, axis=1, keepdims=True), (2 * HL, SR))
        cumr[c] = cum
        ldr[c] = cum - jnp.log(dt)
        cumc[c] = jnp.concatenate([cum, jnp.zeros((SR - 2 * HL, SR), F32)], axis=0).T
        tail = expand(jnp.exp(end - cum) * dt)
        whole = expand(jnp.exp(end))
        dch[c] = whole[0:8, :]
        tf = (xf[rows, :].astype(F32) * tail[:, 0:CW]).astype(BF16)
        tr = (xr[rows, :].astype(F32) * tail[:, CW:2 * CW]).astype(BF16)
        fresh[c, :, 0:CW] = mm(bb[c, :, 0:N], tf, ((0,), (0,)))
        fresh[c, :, CW:2 * CW] = mm(bb[c, :, N:2 * N], tr, ((0,), (0,)))
        return total + end

    total = lax.fori_loop(0, NJ, states, jnp.zeros((2 * HL, SR), F32))
    dec_me[...] = expand(jnp.exp(total))[0:8, :]

    stin[...] = jnp.zeros((N, 2 * CW), F32)

    def fold(c, carry):
        r = NJ - 1 - c
        stin[:, 0:CW] = dch[c, 0:1, 0:CW] * stin[:, 0:CW] + fresh[c, :, 0:CW]
        stin[:, CW:2 * CW] = (
            dch[r, 0:1, CW:2 * CW] * stin[:, CW:2 * CW] + fresh[r, :, CW:2 * CW]
        )
        return carry

    lax.fori_loop(0, NJ, fold, 0)

    swap = [
        rcopy(stin, st_o, sb_s.at[0], sb_r.at[0], at(sib, j)),
        rcopy(dec_me, dec_o, sb_s.at[1], sb_r.at[1], at(sib, j)),
    ]
    for h in swap:
        h.start()
    for h in swap:
        h.wait_recv()
    mine = pl.ds(pl.multiple_of(core * (N // 2), 8), N // 2)
    s_me, s_o = stin[mine, :], st_o[mine, :]
    d_me, d_o = dec_me[0:1, :], dec_o[0:1, :]
    fwd_lane = jnp.where(iota((8, 2 * CW), 1) < CW, 1, 0)[0:1, :]
    other_last = fwd_lane == 1 - core
    pair = jnp.where(other_last, d_o * s_me + s_o, d_me * s_o + s_me)
    d_pair = jnp.broadcast_to(d_me * d_o, (8, 2 * CW))
    place = iota((8, 128), 0)
    d_tile = jnp.zeros((8, 128), F32)
    for q in range(LB):
        d_tile = jnp.where(place == q, d_pair[:, q * 128:(q + 1) * 128], d_tile)
    for p in range(ZC):
        for q in range(LB):
            zs[p, q * PR:(q + 1) * PR, :] = pair[p * PR:(p + 1) * PR, q * 128:(q + 1) * 128]
        zs[p, LB * PR:LB * PR + 8, :] = d_tile
    zr[zi] = zs[zi]

    def zx(k, slot, z):
        return rcopy(zs.at[z], zr.at[slot], zx_s.at[k], zx_r.at[k], at(zpos(z), j))

    def zy(k, slot, z):
        return rcopy(es.at[z], er.at[slot], zy_s.at[k], zy_r.at[k], at(zpos(z), j))

    for k in range(1, ZC):
        zx(k, zi, zto(k)).start()

    low = iota((SR, SR), 0) >= iota((SR, SR), 1)
    upp = iota((SR, SR), 0) <= iota((SR, SR), 1)
    lane_head = iota((8, CW), 1) // (CW // HL)
    skips = expand(own_rows(2))[0:8, :]

    def inner(k, carry):
        c = frm(k)

        @pl.when(k > 0)
        def _():
            ccx(k, c, c).wait_recv()

        rows = pl.ds(pl.multiple_of(c * SR, 16), SR)
        cols = cumc[c]
        lds = ldr[c]
        y = jnp.zeros((SR, CW), F32)
        for d, (xs, mask) in enumerate(((xf, low), (xr, upp))):
            xv = xs[rows, :]
            part = slice(d * N, (d + 1) * N)
            score = mm(cc[c, :, part], bb[c, :, part], ((1,), (1,)))
            for q in range(HL):
                row = q if d == 0 else 2 * HL - 1 - q
                seg = jnp.where(mask, cols[:, row:row + 1] - lds[row:row + 1, :], -1e30)
                mcat[:, q * SR:(q + 1) * SR] = (score * jnp.exp(seg)).astype(BF16)
                keep = jnp.where(lane_head == q, 1.0, 0.0)[0:1, :].astype(BF16)
                xbd[q * SR:(q + 1) * SR, :] = xv * keep
            y = y + mm(mcat[...], xbd[...])
            y = y + skips[0:1, d * CW:(d + 1) * CW] * xv.astype(F32)
        yacc[rows, :] = y
        grown[c] = expand(jnp.exp(cumr[c]))
        return carry

    lax.fori_loop(0, 3, inner, 0)

    for k in range(1, ZC):
        zx(k, zfrm(k), zfrm(k)).wait_recv()

    def chain(q, e, keep):
        order = range(ZC) if q < LB // 2 else range(ZC - 1, -1, -1)
        rows = slice(q * PR, (q + 1) * PR)
        for z in order:
            if keep:
                es[z, rows, :] = e
            e = zr[z, LB * PR + q:LB * PR + q + 1, :] * e + zr[z, rows, :]
        return e

    zero = jnp.zeros((PR, 128), F32)
    if XL > 1:
        for q in range(LB):
            xs_[q * PR:(q + 1) * PR, :] = chain(q, zero, False)
        cross = rcopy(xs_, xr_, sb_s.at[2], sb_r.at[2], at(across, j))
        cross.start()
        lax.fori_loop(3, 4, inner, 0)
        cross.wait_recv()
    for q in range(LB):
        start_from = zero
        if XL > 1:
            takes = xlo == 1 if q < LB // 2 else xlo == 0
            start_from = jnp.where(takes, xr_[q * PR:(q + 1) * PR, :], 0.0)
        chain(q, start_from, True)
    er[zi] = es[zi]
    for k in range(1, ZC):
        zy(k, zi, zto(k)).start()
    lax.fori_loop(4 if XL > 1 else 3, NJ, inner, 0)
    for k in range(1, ZC):
        zy(k, zfrm(k), zfrm(k)).wait_recv()
    ring_wait(1)
    ring_start(2)
    for p in range(ZC):
        for q in range(LB):
            ech[pl.ds(pl.multiple_of(core * (N // 2) + p * PR, 8), PR), q * 128:(q + 1) * 128] = (
                er[p, q * PR:(q + 1) * PR, :]
            )
    halves = rcopy(ech.at[mine, :], ech.at[mine, :], sb_s.at[3], sb_r.at[3], at(sib, j))
    halves.start()
    for h in swap:
        h.wait_send()
    theirs = pl.ds(pl.multiple_of((1 - core) * (N // 2), 8), N // 2)
    rcopy(ech.at[theirs, :], ech.at[theirs, :], sb_s.at[3], sb_r.at[3], at(sib, j)).wait_recv()
    other_first = fwd_lane == core
    stin[...] = jnp.where(other_first, dec_o[0:1, :] * ech[...] + st_o[...], ech[...])

    def enter(s, carry):
        for d in range(2):
            c = s if d == 0 else NJ - 1 - s
            lanes = slice(d * CW, (d + 1) * CW)
            st = stin[:, lanes]
            sbs[c, :, lanes] = st.astype(BF16)
            stin[:, lanes] = dch[c, 0:1, lanes] * st + fresh[c, :, lanes]
        return carry

    lax.fori_loop(0, NJ, enter, 0)

    HB = RB // 2

    def cbx(h, k, slot, dev):
        rows = pl.ds(pl.multiple_of(lax.rem(dev, GROUP) * RB + h * HB, 16), HB)
        return rcopy(
            comb_s.at[rows, :], comb_r.at[slot, pl.ds(h * HB, HB), :],
            cb_s.at[h, k], cb_r.at[h, k], at(i, dev),
        )

    chunks = HB // SR
    for h in range(2):

        def finish(n, carry):
            c = (n // chunks) * (2 * chunks) + h * chunks + lax.rem(n, chunks)
            rows = pl.ds(pl.multiple_of(c * SR, 16), SR)
            y = yacc[rows, :]
            for d in range(2):
                lanes = slice(d * CW, (d + 1) * CW)
                z = mm(cc[c, :, d * N:(d + 1) * N], sbs[c, :, lanes])
                y = y + grown[c, :, lanes] * z
            comb_s[rows, :] = (y * gain_ref[...]).astype(BF16)
            return carry

        lax.fori_loop(0, NJ // 2, finish, 0)
        for k in range(1, NJ):
            cbx(h, k, j, to(k)).start()
    comb_r[j] = comb_s[pl.ds(pl.multiple_of(yy * RB, 16), RB), :]
    ring_wait(2)
    ring_start(3)
    ring_wait(3)
    half = pl.ds(pl.multiple_of(core * (CW // 2), 16), CW // 2)
    rest = pl.ds(pl.multiple_of((1 - core) * (CW // 2), 16), CW // 2)
    share = rcopy(wbuf.at[:, half, :], wbuf.at[:, half, :], sb_s.at[4], sb_r.at[4], at(sib, j))
    share.start()
    for k in range(1, NJ):
        s = frm(k)
        rcopy(gall.at[s], gall.at[s], g_s.at[k], g_r.at[k], at(i, s)).wait_recv()
    rcopy(
        wbuf.at[:, rest, :], wbuf.at[:, rest, :], sb_s.at[4], sb_r.at[4], at(sib, j)
    ).wait_recv()

    def obx(h, k, slot, dest):
        rows = pl.ds(h * HB, HB)
        return rcopy(
            obs.at[dest, rows, :], obr.at[slot, rows, :], ob_s.at[h, k], ob_r.at[h, k],
            at(i, xh * GROUP + dest),
        )

    for h in range(2):
        rows = slice(h * HB, (h + 1) * HB)
        acc[...] = jnp.zeros((HB, WC), F32)
        sqs[...] = jnp.zeros((HB, CW), F32)

        def project(k, carry):
            @pl.when(k > 0)
            def _():
                cbx(h, k, frm(k), frm(k)).wait_recv()

            b = frm(k)
            piece = comb_r[b, rows, :]
            acc[...] += mm(piece, wbuf[b])
            value = piece.astype(F32)
            sqs[...] += value * value * gall[b, 0:1, :]
            return carry

        lax.fori_loop(0, NJ, project, 0)
        scale = lax.rsqrt(jnp.sum(sqs[...], axis=1, keepdims=True) / D + EPS)
        for q in range(GROUP):
            obs[q, rows, :] = (acc[:, q * CW:(q + 1) * CW] * scale).astype(BF16)
        for k in range(1, GROUP):
            obx(h, k, yy, lax.rem(yy + k, GROUP)).start()
    out_ref[pl.ds(pl.multiple_of(yy * RB, 16), RB), :] = obs[yy]
    for h in range(2):
        for k in range(1, GROUP):
            s = lax.rem(yy + GROUP - k, GROUP)
            obx(h, k, s, s).wait_recv()
            out_ref[pl.ds(pl.multiple_of(s * RB + h * HB, 16), HB), :] = (
                obr[s, h * HB:(h + 1) * HB, :]
            )

    slab_pre.wait_send()
    slab_post.wait_send()
    for h in halo:
        h.wait_send()
    for g in gains:
        g.wait_send()
    for k in range(1, NJ):
        xa(k, to(k)).wait_send()
        dtx(k, j, to(k)).wait_send()
        bbx(k, j, to(k)).wait_send()
        ccx(k, j, to(k)).wait_send()
        wx(k, j, to(k)).wait_send()
        for h in range(2):
            cbx(h, k, j, to(k)).wait_send()

    for k in range(1, ZC):
        zx(k, zi, zto(k)).wait_send()
        zy(k, zi, zto(k)).wait_send()
    if XL > 1:
        cross.wait_send()
    halves.wait_send()
    share.wait_send()
    for d in range(ZC // 2):
        up_ring(d, zfrm(d)).wait_send()
    for d in range(ZC // 2):
        down_ring(d, zto(d)).wait_send()
    for h in range(2):
        for k in range(1, GROUP):
            obx(h, k, yy, lax.rem(yy + k, GROUP)).wait_send()


def shards(x_in, conv_weight, proj_weight, dt_bias, decay_log, skip_gain, norm_gain, out_weight):
    T, CW = x_in.shape
    D = conv_weight.shape[1]
    H = dt_bias.shape[0]
    N = (proj_weight.shape[1] - H) // 2
    NC, NJ = lax.axis_size("ctx"), lax.axis_size("chan")
    HL = H // NJ
    SR = T // NJ
    XL = 2 if NC >= 4 else 1
    ZC = NC // (2 * XL)
    PR, LB = N // 2 // ZC, 2 * CW // 128
    RB, WC = T // GROUP, GROUP * CW
    dma = pltpu.SemaphoreType.DMA
    vm = pltpu.VMEM
    scratch = [
        vm((T + 32, CW), BF16), vm((NJ, SR + 64, CW), BF16), vm((SR + 32, CW), F32),
        vm((4, D), F32), vm((T, CW), BF16), vm((T, CW), BF16),
        vm((NJ, SR, 2 * N), BF16), vm((NJ, SR, 2 * N), BF16),
        vm((NJ, 2 * HL, SR), F32), vm((NJ, 2 * HL, SR), F32),
        vm((NJ, 2 * HL, SR), F32), vm((NJ, SR, 128), F32), vm((NJ, 2 * HL, SR), F32),
        vm((NJ, N, 2 * CW), F32), vm((NJ, 8, 2 * CW), F32), vm((T, CW), F32),
        vm((SR, HL * SR), BF16), vm((HL * SR, CW), BF16), vm((6 * HL, 2 * CW), BF16),
        vm((ZC, LB * PR + 8, 128), F32), vm((ZC, LB * PR + 8, 128), F32),
        vm((ZC, LB * PR, 128), F32), vm((ZC, LB * PR, 128), F32),
        vm((LB * PR, 128), F32), vm((LB * PR, 128), F32),
        vm((N, 2 * CW), F32), vm((N, 2 * CW), F32), vm((8, 2 * CW), F32), vm((8, 2 * CW), F32),
        vm((N, 2 * CW), F32),
        vm((T, CW), BF16), vm((NJ, RB, CW), BF16), vm((NJ, 8, CW), F32),
        vm((NJ, CW, WC), BF16), vm((RB // 2, WC), F32),
        vm((GROUP, RB, CW), BF16), vm((GROUP, RB, CW), BF16),
        vm((RB // 2, CW), F32), vm((NJ, SR, 2 * CW), F32), vm((NJ, N, 2 * CW), BF16),
        dma((NJ,)), dma((NJ,)), dma((4,)), dma((2 + NJ,)), dma((NJ,)), dma((NJ,)),
        dma((NJ,)), dma((NJ,)), dma((4,)), dma((4,)), dma((4,)), dma((4,)),
        dma((NJ,)), dma((NJ,)), dma((NJ,)), dma((NJ,)), dma((NJ,)), dma((NJ,)),
        dma((ZC,)), dma((ZC,)), dma((ZC,)), dma((ZC,)), dma((5,)), dma((5,)),
        dma((2, NJ)), dma((2, NJ)), dma((2, GROUP)), dma((2, GROUP)),
        vm(proj_weight.shape, BF16), vm(proj_weight.shape[::-1], BF16), vm((3, H, 128), F32), dma((4,)),
    ]
    return pl.pallas_call(
        functools.partial(kernel, (NC, NJ, T, CW, D, N, HL, XL, ZC)),
        out_shape=jax.ShapeDtypeStruct((T, CW), BF16),
        in_specs=[
            pl.BlockSpec(memory_space=pl.ANY if q in (0, 2, 7) else pltpu.VMEM) for q in range(8)
        ],
        out_specs=pl.BlockSpec(memory_space=pltpu.VMEM),
        scratch_shapes=scratch,
        compiler_params=pltpu.CompilerParams(
            collective_id=0, has_side_effects=True, vmem_limit_bytes=53 * 1024 * 1024
        ),
        cost_estimate=pl.CostEstimate(
            flops=4 * T * D * CW, bytes_accessed=8 * T * CW, transcendentals=16 * T * SR
        ),
    )(
        x_in, conv_weight, proj_weight.T, dt_bias[None], decay_log[None], skip_gain[None],
        norm_gain[None], out_weight,
    )


def solution(mesh):
    in_specs = (P("ctx", "chan"), P(), P(), P(), P(), P(), P("chan"), P("chan", None))
    out_specs = P("ctx", "chan")
    return jax.shard_map(shards, mesh=mesh, in_specs=in_specs, out_specs=out_specs, check_vma=False)
```

```python
import functools

import jax
import jax.numpy as jnp
from jax import lax
from jax.experimental import pallas as pl
from jax.experimental.pallas import tpu as pltpu
from jax.sharding import PartitionSpec as P

F32 = jnp.float32
BF16 = jnp.bfloat16
MESH = pl.DeviceIdType.MESH
EPS = 1e-05
GROUP = 4


def mm(a, b, dims=((1,), (0,)), **kw):
    return lax.dot_general(a, b, (dims, ((), ())), preferred_element_type=F32, **kw)


def silu(v):
    return v / (1.0 + jnp.exp(-v))


def iota(shape, axis):
    return lax.broadcasted_iota(jnp.int32, shape, axis)


def kernel(
    dims,
    x_ref, cw_hbm, pw_ref, bias_hbm, decay_hbm, skip_hbm, gain_hbm, w_ref, out_ref,
    xpad, xe, cbuf, cwr, xf, xr, bb, cc, dtout, dtin, cumr, fresh, dch, yacc,
    mcat, xbd, emat, zs, zr, es, er, xs_, xr_, st_o, ech, dec_me, dec_o, stin, comb_s, comb_r, gall, wbuf, acc, obs, obr, sqs, grown, sbs,
    xa_s, xa_r, ha_s, ha_r, g_s, g_r, w_s, w_r, up_s, up_r, dn_s, dn_r, bb_s, bb_r, cc_s, cc_r, dt_s, dt_r,
    zx_s, zx_r, zy_s, zy_r, sb_s, sb_r, cb_s, cb_r, ob_s, ob_r, pwv, pwr, pwt, prm, lc,
    cw_ref, bias_ref, decay_ref, skip_ref, gain_ref, oc,
):
    NC, NJ, T, CW, D, N, HL, XL, ZC = dims
    SR = T // NJ
    PR = N // 2 // ZC
    LB = 2 * CW // 128
    WR = CW // 2 // ZC
    RB = T // GROUP
    WC = GROUP * CW
    i = lax.axis_index("ctx")
    j = lax.axis_index("chan")
    prev_i = lax.rem(i + NC - 1, NC)
    next_i = lax.rem(i + 1, NC)
    core = lax.rem(i, 2)
    sib = i + 1 - 2 * core
    xlo = i // (2 * ZC)
    zi = lax.rem(i // 2, ZC)
    xh = j // GROUP
    yy = lax.rem(j, GROUP)

    def at(ci, cj):
        return {"ctx": ci, "chan": cj}

    def to(k):
        return lax.rem(xh + k // GROUP, 2) * GROUP + lax.rem(yy + lax.rem(k, GROUP), GROUP)

    def frm(k):
        return (
            lax.rem(xh + k // GROUP, 2) * GROUP
            + lax.rem(yy + GROUP - lax.rem(k, GROUP), GROUP)
        )

    far_first = (6, 5, 7, 4, 2, 1, 3)

    def rcopy(src, dst, ss, rs, dev):
        return pltpu.make_async_remote_copy(
            src_ref=src, dst_ref=dst, send_sem=ss, recv_sem=rs, device_id=dev, device_id_type=MESH
        )

    def win(jd):
        return pl.multiple_of(jnp.clip(SR * jd - 16, 0, T - SR - 32), 16)

    def wrows(z):
        return pl.ds(pl.multiple_of(core * (CW // 2) + z * WR, 16), WR)

    own_wide = pl.ds(pl.multiple_of(xh * WC, 128), WC)
    here = [
        pltpu.make_async_copy(x_ref, xpad.at[pl.ds(16, T), :], lc.at[0]),
        pltpu.make_async_copy(
            x_ref.at[pl.ds(win(j), SR + 32), :], xe.at[j, pl.ds(16, SR + 32), :], lc.at[1]
        ),
        pltpu.make_async_copy(pw_ref, pwt, lc.at[2]),
        pltpu.make_async_copy(
            w_ref.at[wrows(zi), own_wide], wbuf.at[j, wrows(zi), :], lc.at[3]
        ),
    ]
    small = [
        pltpu.make_async_copy(src, dst, lc.at[4 + q])
        for q, (src, dst) in enumerate((
            (cw_hbm, cw_ref), (bias_hbm, bias_ref), (decay_hbm, decay_ref),
            (skip_hbm, skip_ref), (gain_hbm, gain_ref),
        ))
    ]
    for h in small + here:
        h.start()

    barrier = pltpu.get_barrier_semaphore()

    def hail(dev):
        pl.semaphore_signal(barrier, inc=1, device_id=dev, device_id_type=MESH)

    for k in range(1, NJ):
        hail(at(i, to(k)))

    def zpos(z):
        return xlo * (2 * ZC) + z * 2 + core

    def zto(k):
        return lax.rem(zi + k, ZC)

    def zfrm(k):
        return lax.rem(zi + ZC - k, ZC)

    for k in range(1, ZC):
        hail(at(zpos(zto(k)), j))
    across = lax.rem(i + 2 * ZC, NC)
    if XL > 1:
        hail(at(across, j))
    for c in (sib, prev_i, next_i):
        hail(at(c, j))

    @pl.when(j == 0)
    def _():
        for q in range(NJ):
            hail(at(prev_i, q))

    @pl.when(j == NJ - 1)
    def _():
        for q in range(NJ):
            hail(at(next_i, q))

    for h in small:
        h.wait()
    gall[j] = jnp.broadcast_to(1.0 / (gain_ref[...] * gain_ref[...]), (8, CW))
    heads = HL * NJ
    eye = iota((heads, heads), 0) == iota((heads, heads), 1)
    for q, ref in enumerate((bias_ref, decay_ref, skip_ref)):
        row = jnp.broadcast_to(ref[...], (heads, heads))
        column = jnp.sum(jnp.where(eye, row, 0.0), axis=1, keepdims=True)
        prm[q] = jnp.broadcast_to(column, (heads, 128))
    anti = iota((CW, CW), 0) + iota((CW, CW), 1) == CW - 1
    anti_f = jnp.where(anti, 1.0, 0.0).astype(F32)
    anti_b = anti_f.astype(BF16)
    for b in range(NJ):
        cwr[:, b * CW:(b + 1) * CW] = mm(
            cw_ref[:, (NJ - 1 - b) * CW:(NJ - b) * CW], anti_f, precision=lax.Precision.HIGHEST
        )
    head_row = lax.rem(iota((6 * HL, 2 * CW), 0), 2 * HL)
    ec = iota((6 * HL, 2 * CW), 1)
    head_of = ec // (CW // HL)
    target = jnp.where(head_of < HL, head_of, 3 * HL - 1 - head_of)
    emat[...] = jnp.where(head_row == target, 1.0, 0.0).astype(BF16)

    def terms(rows):
        hi = rows.astype(BF16)
        rest = rows - hi.astype(F32)
        mid = rest.astype(BF16)
        low = (rest - mid.astype(F32)).astype(BF16)
        return jnp.concatenate([hi, mid, low], axis=0)

    def expand(rows):
        return mm(terms(rows), emat[...], ((0,), (0,)))

    pl.semaphore_wait(barrier, NJ - 1 + ZC - 1 + XL - 1 + 3 + 2)

    def xa(k, jd):
        return rcopy(
            x_ref.at[pl.ds(win(jd), SR + 32), :], xe.at[j, pl.ds(16, SR + 32), :],
            xa_s.at[k], xa_r.at[k], at(i, jd),
        )

    def xa_in(k):
        return rcopy(
            x_ref.at[pl.ds(0, SR + 32), :], xe.at[frm(k), pl.ds(16, SR + 32), :],
            xa_s.at[k], xa_r.at[k], at(i, frm(k)),
        )

    lastrows, firstrows = x_ref.at[pl.ds(T - 16, 16), :], x_ref.at[pl.ds(0, 16), :]
    halo = [
        rcopy(lastrows, xpad.at[pl.ds(0, 16), :], ha_s.at[0], ha_r.at[0], at(next_i, j)),
        rcopy(firstrows, xpad.at[pl.ds(16 + T, 16), :], ha_s.at[1], ha_r.at[1], at(prev_i, j)),
    ]
    slab_pre = rcopy(
        lastrows, xe.at[j, pl.ds(0, 16), :], ha_s.at[2], ha_r.at[2 + j], at(next_i, 0)
    )
    slab_post = rcopy(
        firstrows, xe.at[j, pl.ds(SR + 48, 16), :], ha_s.at[3], ha_r.at[2 + j], at(prev_i, NJ - 1)
    )
    slab_pre.start()
    slab_post.start()
    for k in far_first:
        xa(k, to(k)).start()
    for h in halo:
        h.start()
    gains = [
        rcopy(gall.at[j], gall.at[j], g_s.at[k], g_r.at[k], at(i, to(k))) for k in range(1, NJ)
    ]
    for g in gains:
        g.start()

    def conv_pair(taps, rtaps):
        vf = taps[0:1, :] * cbuf[13:13 + SR, :]
        vr = rtaps[0:1, :] * cbuf[19:19 + SR, :]
        for k in range(1, 4):
            vf = vf + taps[k:k + 1, :] * cbuf[13 + k:13 + k + SR, :]
            vr = vr + rtaps[k:k + 1, :] * cbuf[19 - k:19 - k + SR, :]
        return silu(vf).astype(BF16), silu(vr).astype(BF16)

    here[2].wait()
    for b in range(NJ):
        block = pwt[:, b * CW:(b + 1) * CW].T
        pwv[b * CW:(b + 1) * CW, :] = block
        pwr[(NJ - 1 - b) * CW:(NJ - b) * CW, :] = mm(anti_b, block).astype(BF16)

    own_cols = pl.ds(pl.multiple_of(j * CW, 128), CW)

    def own_conv(c, carry):
        rows = pl.ds(pl.multiple_of(c * SR, 16), SR)
        cbuf[...] = xpad[pl.ds(pl.multiple_of(c * SR, 16), SR + 32), :].astype(F32)
        f, r = conv_pair(cw_ref[:, own_cols], cwr[:, own_cols])
        xf[rows, :] = f
        xr[rows, :] = r
        return carry

    here[0].wait()
    lax.fori_loop(1, NJ - 1, own_conv, 0)

    @pl.when(j == 0)
    def _():
        for q in range(NJ):
            rcopy(
                lastrows, xe.at[q, pl.ds(0, 16), :], ha_s.at[2], ha_r.at[2 + q], at(prev_i, q)
            ).wait_recv()

    @pl.when(j == NJ - 1)
    def _():
        for q in range(NJ):
            rcopy(
                firstrows, xe.at[q, pl.ds(SR + 48, 16), :], ha_s.at[3], ha_r.at[2 + q],
                at(next_i, q),
            ).wait_recv()

    @pl.when(jnp.logical_and(i == 0, j == 0))
    def _():
        for q in range(NJ):
            xe[q, 0:16, :] = jnp.zeros((16, CW), BF16)

    @pl.when(jnp.logical_and(i == NC - 1, j == NJ - 1))
    def _():
        for q in range(NJ):
            xe[q, SR + 48:SR + 64, :] = jnp.zeros((16, CW), BF16)

    start = pl.multiple_of(SR * j - win(j), 16)
    here[1].wait()

    def wx(k, slot, dev):
        cols = pl.ds(pl.multiple_of((dev // GROUP) * WC, 128), WC)
        return rcopy(
            w_ref.at[wrows(zi), cols], wbuf.at[slot, wrows(zi), :], w_s.at[k], w_r.at[k],
            at(i, dev),
        )

    def halfway(d):
        return ZC % 2 == 0 and d == ZC // 2 - 1

    def up_ring(d, z):
        part = wbuf.at[pl.ds(0, NJ // 2 if halfway(d) else NJ), wrows(z), :]
        return rcopy(part, part, up_s.at[d], up_r.at[d], at(zpos(zto(1)), j))

    def down_ring(d, z):
        first = NJ // 2 if halfway(d) else 0
        part = wbuf.at[pl.ds(first, NJ - first), wrows(z), :]
        return rcopy(part, part, dn_s.at[d], dn_r.at[d], at(zpos(zfrm(1)), j))

    def ring_start(d):
        if d < ZC // 2:
            up_ring(d, zfrm(d)).start()
        if d < ZC // 2:
            down_ring(d, zto(d)).start()

    def ring_wait(d):
        if d < ZC // 2:
            up_ring(d, zfrm(d + 1)).wait_recv()
        if d < ZC // 2:
            down_ring(d, zto(d + 1)).wait_recv()

    def slab(k, carry):
        pf, pr = carry

        @pl.when(k == NJ // 2)
        def _():
            for q in far_first:
                wx(q, j, to(q)).start()

        @pl.when(k > 0)
        def _():
            xa_in(k).wait_recv()

        b = frm(k)
        cols = pl.ds(pl.multiple_of(b * CW, 128), CW)
        cbuf[...] = xe[b, pl.ds(start, SR + 32), :].astype(F32)
        f, r = conv_pair(cw_ref[:, cols], cwr[:, cols])
        pf = pf + mm(f, pwv[cols, :])
        pr = pr + mm(r, pwr[cols, :])
        return pf, pr

    wide = pwv.shape[1]
    pf, pr = lax.fori_loop(
        0, NJ, slab, (jnp.zeros((SR, wide), F32), jnp.zeros((SR, wide), F32))
    )
    def bbx(k, slot, dev):
        return rcopy(bb.at[slot], bb.at[slot], bb_s.at[k], bb_r.at[k], at(i, dev))

    def ccx(k, slot, dev):
        return rcopy(cc.at[slot], cc.at[slot], cc_s.at[k], cc_r.at[k], at(i, dev))

    def dtx(k, slot, dev):
        return rcopy(dtout.at[dev], dtin.at[slot], dt_s.at[k], dt_r.at[k], at(i, dev))

    bb[j, :, 0:N] = pf[:, 0:N].astype(BF16)
    bb[j, :, N:2 * N] = pr[:, 0:N].astype(BF16)
    for k in far_first:
        bbx(k, j, to(k)).start()
    raw = jnp.concatenate([pf[:, 2 * N:], pr[:, 2 * N:]], axis=1).T
    bias = jnp.concatenate([prm[0], prm[0]], axis=0)
    v = raw + bias
    dts = jnp.maximum(v, 0.0) + jnp.log1p(jnp.exp(-jnp.abs(v)))
    for q in range(NJ):
        dtout[q, 0:HL, :] = dts[q * HL:(q + 1) * HL, :]
        dtout[q, HL:2 * HL, :] = dts[heads + (NJ - 1 - q) * HL:heads + (NJ - q) * HL, :]
    for k in far_first:
        dtx(k, j, to(k)).start()
    dtin[j] = dtout[j]
    cc[j, :, 0:N] = pf[:, N:2 * N].astype(BF16)
    cc[j, :, N:2 * N] = pr[:, N:2 * N].astype(BF16)

    for h in halo:
        h.wait_recv()

    @pl.when(i == 0)
    def _():
        xpad[0:16, :] = jnp.zeros((16, CW), BF16)

    @pl.when(i == NC - 1)
    def _():
        xpad[16 + T:32 + T, :] = jnp.zeros((16, CW), BF16)

    own_conv(0, 0)
    own_conv(NJ - 1, 0)

    for k in range(1, NJ):
        wx(k, frm(k), frm(k)).wait_recv()
    here[3].wait()
    ring_start(0)

    own = pl.ds(pl.multiple_of(j * HL, 8), HL)
    mirror = pl.ds(pl.multiple_of((NJ - 1 - j) * HL, 8), HL)

    def own_rows(which):
        return jnp.concatenate([prm[which, own, :], prm[which, mirror, :]], axis=0)

    rate = -jnp.exp(own_rows(1))
    src, dst = iota((SR, 2 * SR), 0), iota((SR, 2 * SR), 1)
    sums = jnp.where(dst < SR, dst - src, src - dst + SR) >= 0
    sums = jnp.where(sums, 1.0, 0.0).astype(BF16)
    is_fwd = iota((2 * HL, SR), 0) < HL
    chunk_lane = iota((2 * HL, SR), 1)

    def states(k, ends):
        c = frm(k)

        @pl.when(k > 0)
        def _():
            dtx(k, c, c).wait_recv()
            bbx(k, c, c).wait_recv()

        @pl.when(k == NJ // 2)
        def _():
            ring_wait(0)
            ring_start(1)

        @pl.when(k == NJ - 1)
        def _():
            for q in far_first:
                ccx(q, j, to(q)).start()

        rows = pl.ds(pl.multiple_of(c * SR, 16), SR)
        dt = dtin[c]
        a = dt * rate
        run = mm(terms(a), sums)
        run = run[0:2 * HL] + run[2 * HL:4 * HL] + run[4 * HL:6 * HL]
        cum = jnp.where(is_fwd, run[:, 0:SR], run[:, SR:2 * SR])
        end = jnp.sum(a, axis=1, keepdims=True)
        cumr[c] = cum
        tail = expand(jnp.exp(end - cum) * dt)
        tf = (xf[rows, :].astype(F32) * tail[:, 0:CW]).astype(BF16)
        tr = (xr[rows, :].astype(F32) * tail[:, CW:2 * CW]).astype(BF16)
        fresh[c, :, 0:CW] = mm(bb[c, :, 0:N], tf, ((0,), (0,)))
        fresh[c, :, CW:2 * CW] = mm(bb[c, :, N:2 * N], tr, ((0,), (0,)))
        return jnp.where(chunk_lane == c, end, ends)

    ends = lax.fori_loop(0, NJ, states, jnp.zeros((2 * HL, SR), F32))
    ends = jnp.where(chunk_lane == NJ, jnp.sum(ends, axis=1, keepdims=True), ends)
    whole = expand(jnp.exp(ends))
    for c in range(NJ):
        dch[c] = jnp.broadcast_to(whole[c:c + 1, :], (8, 2 * CW))
    dec_me[...] = jnp.broadcast_to(whole[NJ:NJ + 1, :], (8, 2 * CW))

    stin[...] = jnp.zeros((N, 2 * CW), F32)

    def fold(c, carry):
        r = NJ - 1 - c
        stin[:, 0:CW] = dch[c, 0:1, 0:CW] * stin[:, 0:CW] + fresh[c, :, 0:CW]
        stin[:, CW:2 * CW] = (
            dch[r, 0:1, CW:2 * CW] * stin[:, CW:2 * CW] + fresh[r, :, CW:2 * CW]
        )
        return carry

    lax.fori_loop(0, NJ, fold, 0)

    swap = [
        rcopy(stin, st_o, sb_s.at[0], sb_r.at[0], at(sib, j)),
        rcopy(dec_me, dec_o, sb_s.at[1], sb_r.at[1], at(sib, j)),
    ]
    for h in swap:
        h.start()
    for h in swap:
        h.wait_recv()
    mine = pl.ds(pl.multiple_of(core * (N // 2), 8), N // 2)
    s_me, s_o = stin[mine, :], st_o[mine, :]
    d_me, d_o = dec_me[0:1, :], dec_o[0:1, :]
    fwd_lane = jnp.where(iota((8, 2 * CW), 1) < CW, 1, 0)[0:1, :]
    other_last = fwd_lane == 1 - core
    pair = jnp.where(other_last, d_o * s_me + s_o, d_me * s_o + s_me)
    d_pair = jnp.broadcast_to(d_me * d_o, (8, 2 * CW))
    place = iota((8, 128), 0)
    d_tile = jnp.zeros((8, 128), F32)
    for q in range(LB):
        d_tile = jnp.where(place == q, d_pair[:, q * 128:(q + 1) * 128], d_tile)
    for p in range(ZC):
        for q in range(LB):
            zs[p, q * PR:(q + 1) * PR, :] = pair[p * PR:(p + 1) * PR, q * 128:(q + 1) * 128]
        zs[p, LB * PR:LB * PR + 8, :] = d_tile
    zr[zi] = zs[zi]

    def zx(k, slot, z):
        return rcopy(zs.at[z], zr.at[slot], zx_s.at[k], zx_r.at[k], at(zpos(z), j))

    def zy(k, slot, z):
        return rcopy(es.at[z], er.at[slot], zy_s.at[k], zy_r.at[k], at(zpos(z), j))

    for k in range(1, ZC):
        zx(k, zi, zto(k)).start()

    low = iota((SR, SR), 0) >= iota((SR, SR), 1)
    upp = iota((SR, SR), 0) <= iota((SR, SR), 1)
    lane_head = iota((8, CW), 1) // (CW // HL)
    skips = expand(own_rows(2))[0:8, :]

    def inner(k, carry):
        c = frm(k)

        @pl.when(k > 0)
        def _():
            ccx(k, c, c).wait_recv()

        rows = pl.ds(pl.multiple_of(c * SR, 16), SR)
        cum = cumr[c]
        cols = jnp.concatenate([cum, jnp.zeros((SR - 2 * HL, SR), F32)], axis=0).T
        lds = cum - jnp.log(dtin[c])
        y = jnp.zeros((SR, CW), F32)
        for d, (xs, mask) in enumerate(((xf, low), (xr, upp))):
            xv = xs[rows, :]
            part = slice(d * N, (d + 1) * N)
            score = mm(cc[c, :, part], bb[c, :, part], ((1,), (1,)))
            for q in range(HL):
                row = q if d == 0 else 2 * HL - 1 - q
                seg = jnp.where(mask, cols[:, row:row + 1] - lds[row:row + 1, :], -1e30)
                mcat[:, q * SR:(q + 1) * SR] = (score * jnp.exp(seg)).astype(BF16)
                keep = jnp.where(lane_head == q, 1.0, 0.0)[0:1, :].astype(BF16)
                xbd[q * SR:(q + 1) * SR, :] = xv * keep
            y = y + mm(mcat[...], xbd[...])
            y = y + skips[0:1, d * CW:(d + 1) * CW] * xv.astype(F32)
        yacc[rows, :] = y
        grown[c] = expand(jnp.exp(cum))
        return carry

    lax.fori_loop(0, 3, inner, 0)

    for k in range(1, ZC):
        zx(k, zfrm(k), zfrm(k)).wait_recv()

    def chain(q, e, keep):
        order = range(ZC) if q < LB // 2 else range(ZC - 1, -1, -1)
        rows = slice(q * PR, (q + 1) * PR)
        for z in order:
            if keep:
                es[z, rows, :] = e
            e = zr[z, LB * PR + q:LB * PR + q + 1, :] * e + zr[z, rows, :]
        return e

    zero = jnp.zeros((PR, 128), F32)
    if XL > 1:
        for q in range(LB):
            xs_[q * PR:(q + 1) * PR, :] = chain(q, zero, False)
        cross = rcopy(xs_, xr_, sb_s.at[2], sb_r.at[2], at(across, j))
        cross.start()
        lax.fori_loop(3, 4, inner, 0)
        cross.wait_recv()
    for q in range(LB):
        start_from = zero
        if XL > 1:
            takes = xlo == 1 if q < LB // 2 else xlo == 0
            start_from = jnp.where(takes, xr_[q * PR:(q + 1) * PR, :], 0.0)
        chain(q, start_from, True)
    er[zi] = es[zi]
    for k in range(1, ZC):
        zy(k, zi, zto(k)).start()
    lax.fori_loop(4 if XL > 1 else 3, NJ, inner, 0)
    for k in range(1, ZC):
        zy(k, zfrm(k), zfrm(k)).wait_recv()
    ring_wait(1)
    ring_start(2)
    for p in range(ZC):
        for q in range(LB):
            ech[pl.ds(pl.multiple_of(core * (N // 2) + p * PR, 8), PR), q * 128:(q + 1) * 128] = (
                er[p, q * PR:(q + 1) * PR, :]
            )
    halves = rcopy(ech.at[mine, :], ech.at[mine, :], sb_s.at[3], sb_r.at[3], at(sib, j))
    halves.start()
    for h in swap:
        h.wait_send()
    theirs = pl.ds(pl.multiple_of((1 - core) * (N // 2), 8), N // 2)
    rcopy(ech.at[theirs, :], ech.at[theirs, :], sb_s.at[3], sb_r.at[3], at(sib, j)).wait_recv()
    other_first = fwd_lane == core
    stin[...] = jnp.where(other_first, dec_o[0:1, :] * ech[...] + st_o[...], ech[...])

    def enter(s, carry):
        for d in range(2):
            c = s if d == 0 else NJ - 1 - s
            lanes = slice(d * CW, (d + 1) * CW)
            st = stin[:, lanes]
            sbs[c, :, lanes] = st.astype(BF16)
            stin[:, lanes] = dch[c, 0:1, lanes] * st + fresh[c, :, lanes]
        return carry

    lax.fori_loop(0, NJ, enter, 0)

    HB = RB // 2

    def cbx(h, k, slot, dev):
        rows = pl.ds(pl.multiple_of(lax.rem(dev, GROUP) * RB + h * HB, 16), HB)
        return rcopy(
            comb_s.at[rows, :], comb_r.at[slot, pl.ds(h * HB, HB), :],
            cb_s.at[h, k], cb_r.at[h, k], at(i, dev),
        )

    chunks = HB // SR
    for h in range(2):

        def finish(n, carry):
            c = (n // chunks) * (2 * chunks) + h * chunks + lax.rem(n, chunks)
            rows = pl.ds(pl.multiple_of(c * SR, 16), SR)
            y = yacc[rows, :]
            for d in range(2):
                lanes = slice(d * CW, (d + 1) * CW)
                z = mm(cc[c, :, d * N:(d + 1) * N], sbs[c, :, lanes])
                y = y + grown[c, :, lanes] * z
            comb_s[rows, :] = (y * gain_ref[...]).astype(BF16)
            return carry

        lax.fori_loop(0, NJ // 2, finish, 0)
        for k in far_first:
            cbx(h, k, j, to(k)).start()
    comb_r[j] = comb_s[pl.ds(pl.multiple_of(yy * RB, 16), RB), :]
    ring_wait(2)
    ring_start(3)
    ring_wait(3)
    half = pl.ds(pl.multiple_of(core * (CW // 2), 16), CW // 2)
    rest = pl.ds(pl.multiple_of((1 - core) * (CW // 2), 16), CW // 2)
    share = rcopy(wbuf.at[:, half, :], wbuf.at[:, half, :], sb_s.at[4], sb_r.at[4], at(sib, j))
    share.start()
    for k in range(1, NJ):
        s = frm(k)
        rcopy(gall.at[s], gall.at[s], g_s.at[k], g_r.at[k], at(i, s)).wait_recv()
    rcopy(
        wbuf.at[:, rest, :], wbuf.at[:, rest, :], sb_s.at[4], sb_r.at[4], at(sib, j)
    ).wait_recv()

    def obx(h, k, slot, dest):
        rows = pl.ds(h * HB, HB)
        return rcopy(
            obs.at[dest, rows, :], obr.at[slot, rows, :], ob_s.at[h, k], ob_r.at[h, k],
            at(i, xh * GROUP + dest),
        )

    for h in range(2):
        rows = slice(h * HB, (h + 1) * HB)
        acc[...] = jnp.zeros((HB, WC), F32)
        sqs[...] = jnp.zeros((HB, CW), F32)

        def project(k, carry):
            @pl.when(k > 0)
            def _():
                cbx(h, k, frm(k), frm(k)).wait_recv()

            b = frm(k)
            piece = comb_r[b, rows, :]
            acc[...] += mm(piece, wbuf[b])
            value = piece.astype(F32)
            sqs[...] += value * value * gall[b, 0:1, :]
            return carry

        lax.fori_loop(0, NJ, project, 0)
        scale = lax.rsqrt(jnp.sum(sqs[...], axis=1, keepdims=True) / D + EPS)
        for q in range(GROUP):
            obs[q, rows, :] = (acc[:, q * CW:(q + 1) * CW] * scale).astype(BF16)
        for k in range(1, GROUP):
            obx(h, k, yy, lax.rem(yy + k, GROUP)).start()
    def place_out(n, src, s, h, size):
        rows = pl.ds(pl.multiple_of(s * RB + h * HB, 16), size)
        return pltpu.make_async_copy(src, out_ref.at[rows, :], oc.at[n])

    outs = [place_out(0, obs.at[yy], yy, 0, RB)]
    outs[0].start()
    for h in range(2):
        for k in range(1, GROUP):
            s = lax.rem(yy + GROUP - k, GROUP)
            obx(h, k, s, s).wait_recv()
            outs.append(
                place_out(h * GROUP + k, obr.at[s, pl.ds(h * HB, HB), :], s, h, HB)
            )
            outs[-1].start()
    for h in outs:
        h.wait()

    slab_pre.wait_send()
    slab_post.wait_send()
    for h in halo:
        h.wait_send()
    for g in gains:
        g.wait_send()
    for k in range(1, NJ):
        xa(k, to(k)).wait_send()
        dtx(k, j, to(k)).wait_send()
        bbx(k, j, to(k)).wait_send()
        ccx(k, j, to(k)).wait_send()
        wx(k, j, to(k)).wait_send()
        for h in range(2):
            cbx(h, k, j, to(k)).wait_send()

    for k in range(1, ZC):
        zx(k, zi, zto(k)).wait_send()
        zy(k, zi, zto(k)).wait_send()
    if XL > 1:
        cross.wait_send()
    halves.wait_send()
    share.wait_send()
    for d in range(ZC // 2):
        up_ring(d, zfrm(d)).wait_send()
    for d in range(ZC // 2):
        down_ring(d, zto(d)).wait_send()
    for h in range(2):
        for k in range(1, GROUP):
            obx(h, k, yy, lax.rem(yy + k, GROUP)).wait_send()


def shards(x_in, conv_weight, proj_weight, dt_bias, decay_log, skip_gain, norm_gain, out_weight):
    T, CW = x_in.shape
    D = conv_weight.shape[1]
    H = dt_bias.shape[0]
    N = (proj_weight.shape[1] - H) // 2
    NC, NJ = lax.axis_size("ctx"), lax.axis_size("chan")
    HL = H // NJ
    SR = T // NJ
    XL = 2 if NC >= 4 else 1
    ZC = NC // (2 * XL)
    PR, LB = N // 2 // ZC, 2 * CW // 128
    RB, WC = T // GROUP, GROUP * CW
    dma = pltpu.SemaphoreType.DMA
    vm = pltpu.VMEM
    scratch = [
        vm((T + 32, CW), BF16), vm((NJ, SR + 64, CW), BF16), vm((SR + 32, CW), F32),
        vm((4, D), F32), vm((T, CW), BF16), vm((T, CW), BF16),
        vm((NJ, SR, 2 * N), BF16), vm((NJ, SR, 2 * N), BF16),
        vm((NJ, 2 * HL, SR), F32), vm((NJ, 2 * HL, SR), F32),
        vm((NJ, 2 * HL, SR), F32),
        vm((NJ, N, 2 * CW), F32), vm((NJ, 8, 2 * CW), F32), vm((T, CW), F32),
        vm((SR, HL * SR), BF16), vm((HL * SR, CW), BF16), vm((6 * HL, 2 * CW), BF16),
        vm((ZC, LB * PR + 8, 128), F32), vm((ZC, LB * PR + 8, 128), F32),
        vm((ZC, LB * PR, 128), F32), vm((ZC, LB * PR, 128), F32),
        vm((LB * PR, 128), F32), vm((LB * PR, 128), F32),
        vm((N, 2 * CW), F32), vm((N, 2 * CW), F32), vm((8, 2 * CW), F32), vm((8, 2 * CW), F32),
        vm((N, 2 * CW), F32),
        vm((T, CW), BF16), vm((NJ, RB, CW), BF16), vm((NJ, 8, CW), F32),
        vm((NJ, CW, WC), BF16), vm((RB // 2, WC), F32),
        vm((GROUP, RB, CW), BF16), vm((GROUP, RB, CW), BF16),
        vm((RB // 2, CW), F32), vm((NJ, SR, 2 * CW), F32), vm((NJ, N, 2 * CW), BF16),
        dma((NJ,)), dma((NJ,)), dma((4,)), dma((2 + NJ,)), dma((NJ,)), dma((NJ,)),
        dma((NJ,)), dma((NJ,)), dma((4,)), dma((4,)), dma((4,)), dma((4,)),
        dma((NJ,)), dma((NJ,)), dma((NJ,)), dma((NJ,)), dma((NJ,)), dma((NJ,)),
        dma((ZC,)), dma((ZC,)), dma((ZC,)), dma((ZC,)), dma((5,)), dma((5,)),
        dma((2, NJ)), dma((2, NJ)), dma((2, GROUP)), dma((2, GROUP)),
        vm(proj_weight.shape, BF16), vm(proj_weight.shape, BF16),
        vm(proj_weight.shape[::-1], BF16), vm((3, H, 128), F32), dma((9,)),
        vm((4, D), F32), vm((1, H), F32), vm((1, H), F32), vm((1, H), F32), vm((1, CW), F32), dma((2 * GROUP,)),
    ]
    return pl.pallas_call(
        functools.partial(kernel, (NC, NJ, T, CW, D, N, HL, XL, ZC)),
        out_shape=jax.ShapeDtypeStruct((T, CW), BF16),
        in_specs=[pl.BlockSpec(memory_space=pl.ANY)] * 8,
        out_specs=pl.BlockSpec(memory_space=pl.ANY),
        scratch_shapes=scratch,
        compiler_params=pltpu.CompilerParams(
            collective_id=0, has_side_effects=True, vmem_limit_bytes=62 * 1024 * 1024
        ),
        cost_estimate=pl.CostEstimate(
            flops=4 * T * D * CW, bytes_accessed=8 * T * CW, transcendentals=16 * T * SR
        ),
    )(
        x_in, conv_weight, proj_weight.T, dt_bias[None], decay_log[None], skip_gain[None],
        norm_gain[None], out_weight,
    )


def solution(mesh):
    in_specs = (P("ctx", "chan"), P(), P(), P(), P(), P(), P("chan"), P("chan", None))
    out_specs = P("ctx", "chan")
    return jax.shard_map(shards, mesh=mesh, in_specs=in_specs, out_specs=out_specs, check_vma=False)
```

```python
import functools

import jax
import jax.numpy as jnp
from jax import lax
from jax.experimental import pallas as pl
from jax.experimental.pallas import tpu as pltpu
from jax.sharding import PartitionSpec as P

F32 = jnp.float32
BF16 = jnp.bfloat16
MESH = pl.DeviceIdType.MESH
EPS = 1e-05
GROUP = 4


def mm(a, b, dims=((1,), (0,)), **kw):
    return lax.dot_general(a, b, (dims, ((), ())), preferred_element_type=F32, **kw)


def silu(v):
    return v / (1.0 + jnp.exp(-v))


def iota(shape, axis):
    return lax.broadcasted_iota(jnp.int32, shape, axis)


def kernel(
    dims,
    x_ref, cw_hbm, pw_ref, bias_hbm, decay_hbm, skip_hbm, gain_hbm, w_ref, out_ref,
    xpad, xe, cbuf, cwr, xf, xr, bb, cc, dtout, dtin, cumr, fresh, dch, yacc,
    mcat, xbd, emat, zs, zr, es, er, xs_, xr_, st_o, ech, dec_me, dec_o, stin, comb_s, comb_r, gall, wbuf, acc, obs, obr, sqs, grown, sbs,
    xa_s, xa_r, ha_s, ha_r, g_s, g_r, w_s, w_r, up_s, up_r, dn_s, dn_r, bb_s, bb_r, cc_s, cc_r, dt_s, dt_r,
    zx_s, zx_r, zy_s, zy_r, sb_s, sb_r, cb_s, cb_r, ob_s, ob_r, pwv, pwr, pwt, prm, lc,
    cw_ref, bias_ref, decay_ref, skip_ref, gain_ref, oc,
):
    NC, NJ, T, CW, D, N, HL, XL, ZC = dims
    SR = T // NJ
    PR = N // 2 // ZC
    LB = 2 * CW // 128
    WR = CW // 2 // ZC
    RB = T // GROUP
    WC = GROUP * CW
    i = lax.axis_index("ctx")
    j = lax.axis_index("chan")
    prev_i = lax.rem(i + NC - 1, NC)
    next_i = lax.rem(i + 1, NC)
    core = lax.rem(i, 2)
    sib = i + 1 - 2 * core
    xlo = i // (2 * ZC)
    zi = lax.rem(i // 2, ZC)
    xh = j // GROUP
    yy = lax.rem(j, GROUP)

    def at(ci, cj):
        return {"ctx": ci, "chan": cj}

    def to(k):
        return lax.rem(xh + k // GROUP, 2) * GROUP + lax.rem(yy + lax.rem(k, GROUP), GROUP)

    def frm(k):
        return (
            lax.rem(xh + k // GROUP, 2) * GROUP
            + lax.rem(yy + GROUP - lax.rem(k, GROUP), GROUP)
        )

    far_first = (6, 5, 7, 4, 2, 1, 3)

    def rcopy(src, dst, ss, rs, dev):
        return pltpu.make_async_remote_copy(
            src_ref=src, dst_ref=dst, send_sem=ss, recv_sem=rs, device_id=dev, device_id_type=MESH
        )

    def win(jd):
        return pl.multiple_of(jnp.clip(SR * jd - 16, 0, T - SR - 32), 16)

    def wrows(z):
        return pl.ds(pl.multiple_of(core * (CW // 2) + z * WR, 16), WR)

    own_wide = pl.ds(pl.multiple_of(xh * WC, 128), WC)
    here = [
        pltpu.make_async_copy(x_ref, xpad.at[pl.ds(16, T), :], lc.at[0]),
        pltpu.make_async_copy(
            x_ref.at[pl.ds(win(j), SR + 32), :], xe.at[j, pl.ds(16, SR + 32), :], lc.at[1]
        ),
        pltpu.make_async_copy(pw_ref, pwt, lc.at[2]),
        pltpu.make_async_copy(
            w_ref.at[wrows(zi), own_wide], wbuf.at[j, wrows(zi), :], lc.at[3]
        ),
    ]
    small = [
        pltpu.make_async_copy(src, dst, lc.at[4 + q])
        for q, (src, dst) in enumerate((
            (cw_hbm, cw_ref), (bias_hbm, bias_ref), (decay_hbm, decay_ref),
            (skip_hbm, skip_ref), (gain_hbm, gain_ref),
        ))
    ]
    for h in small + here:
        h.start()

    barrier = pltpu.get_barrier_semaphore()

    def hail(dev):
        pl.semaphore_signal(barrier, inc=1, device_id=dev, device_id_type=MESH)

    for k in range(1, NJ):
        hail(at(i, to(k)))

    def zpos(z):
        return xlo * (2 * ZC) + z * 2 + core

    def zto(k):
        return lax.rem(zi + k, ZC)

    def zfrm(k):
        return lax.rem(zi + ZC - k, ZC)

    for k in range(1, ZC):
        hail(at(zpos(zto(k)), j))
    across = lax.rem(i + 2 * ZC, NC)
    if XL > 1:
        hail(at(across, j))
    for c in (sib, prev_i, next_i):
        hail(at(c, j))

    @pl.when(j == 0)
    def _():
        for q in range(NJ):
            hail(at(prev_i, q))

    @pl.when(j == NJ - 1)
    def _():
        for q in range(NJ):
            hail(at(next_i, q))

    for h in small:
        h.wait()
    gall[j] = jnp.broadcast_to(1.0 / (gain_ref[...] * gain_ref[...]), (8, CW))
    heads = HL * NJ
    eye = iota((heads, heads), 0) == iota((heads, heads), 1)
    for q, ref in enumerate((bias_ref, decay_ref, skip_ref)):
        row = jnp.broadcast_to(ref[...], (heads, heads))
        column = jnp.sum(jnp.where(eye, row, 0.0), axis=1, keepdims=True)
        prm[q] = jnp.broadcast_to(column, (heads, 128))
    anti = iota((CW, CW), 0) + iota((CW, CW), 1) == CW - 1
    anti_f = jnp.where(anti, 1.0, 0.0).astype(F32)
    anti_b = anti_f.astype(BF16)
    for b in range(NJ):
        cwr[:, b * CW:(b + 1) * CW] = mm(
            cw_ref[:, (NJ - 1 - b) * CW:(NJ - b) * CW], anti_f, precision=lax.Precision.HIGHEST
        )
    head_row = lax.rem(iota((6 * HL, 2 * CW), 0), 2 * HL)
    ec = iota((6 * HL, 2 * CW), 1)
    head_of = ec // (CW // HL)
    target = jnp.where(head_of < HL, head_of, 3 * HL - 1 - head_of)
    emat[...] = jnp.where(head_row == target, 1.0, 0.0).astype(BF16)

    def terms(rows):
        hi = rows.astype(BF16)
        rest = rows - hi.astype(F32)
        mid = rest.astype(BF16)
        low = (rest - mid.astype(F32)).astype(BF16)
        return jnp.concatenate([hi, mid, low], axis=0)

    def expand(rows):
        return mm(terms(rows), emat[...], ((0,), (0,)))

    pl.semaphore_wait(barrier, NJ - 1 + ZC - 1 + XL - 1 + 3 + 2)

    def xa(k, jd):
        return rcopy(
            x_ref.at[pl.ds(win(jd), SR + 32), :], xe.at[j, pl.ds(16, SR + 32), :],
            xa_s.at[k], xa_r.at[k], at(i, jd),
        )

    def xa_in(k):
        return rcopy(
            x_ref.at[pl.ds(0, SR + 32), :], xe.at[frm(k), pl.ds(16, SR + 32), :],
            xa_s.at[k], xa_r.at[k], at(i, frm(k)),
        )

    lastrows, firstrows = x_ref.at[pl.ds(T - 16, 16), :], x_ref.at[pl.ds(0, 16), :]
    halo = [
        rcopy(lastrows, xpad.at[pl.ds(0, 16), :], ha_s.at[0], ha_r.at[0], at(next_i, j)),
        rcopy(firstrows, xpad.at[pl.ds(16 + T, 16), :], ha_s.at[1], ha_r.at[1], at(prev_i, j)),
    ]
    slab_pre = rcopy(
        lastrows, xe.at[j, pl.ds(0, 16), :], ha_s.at[2], ha_r.at[2 + j], at(next_i, 0)
    )
    slab_post = rcopy(
        firstrows, xe.at[j, pl.ds(SR + 48, 16), :], ha_s.at[3], ha_r.at[2 + j], at(prev_i, NJ - 1)
    )
    slab_pre.start()
    slab_post.start()
    for k in far_first:
        xa(k, to(k)).start()
    for h in halo:
        h.start()
    gains = [
        rcopy(gall.at[j], gall.at[j], g_s.at[k], g_r.at[k], at(i, to(k))) for k in range(1, NJ)
    ]
    for g in gains:
        g.start()

    def conv_pair(taps, rtaps):
        vf = taps[0:1, :] * cbuf[13:13 + SR, :]
        vr = rtaps[0:1, :] * cbuf[19:19 + SR, :]
        for k in range(1, 4):
            vf = vf + taps[k:k + 1, :] * cbuf[13 + k:13 + k + SR, :]
            vr = vr + rtaps[k:k + 1, :] * cbuf[19 - k:19 - k + SR, :]
        return silu(vf).astype(BF16), silu(vr).astype(BF16)

    here[2].wait()
    for b in range(NJ):
        block = pwt[:, b * CW:(b + 1) * CW].T
        pwv[b * CW:(b + 1) * CW, :] = block
        pwr[(NJ - 1 - b) * CW:(NJ - b) * CW, :] = mm(anti_b, block).astype(BF16)

    own_cols = pl.ds(pl.multiple_of(j * CW, 128), CW)

    def own_conv(c, carry):
        rows = pl.ds(pl.multiple_of(c * SR, 16), SR)
        cbuf[...] = xpad[pl.ds(pl.multiple_of(c * SR, 16), SR + 32), :].astype(F32)
        f, r = conv_pair(cw_ref[:, own_cols], cwr[:, own_cols])
        xf[rows, :] = f
        xr[rows, :] = r
        return carry

    here[0].wait()
    lax.fori_loop(1, NJ - 1, own_conv, 0)

    @pl.when(j == 0)
    def _():
        for q in range(NJ):
            rcopy(
                lastrows, xe.at[q, pl.ds(0, 16), :], ha_s.at[2], ha_r.at[2 + q], at(prev_i, q)
            ).wait_recv()

    @pl.when(j == NJ - 1)
    def _():
        for q in range(NJ):
            rcopy(
                firstrows, xe.at[q, pl.ds(SR + 48, 16), :], ha_s.at[3], ha_r.at[2 + q],
                at(next_i, q),
            ).wait_recv()

    @pl.when(jnp.logical_and(i == 0, j == 0))
    def _():
        for q in range(NJ):
            xe[q, 0:16, :] = jnp.zeros((16, CW), BF16)

    @pl.when(jnp.logical_and(i == NC - 1, j == NJ - 1))
    def _():
        for q in range(NJ):
            xe[q, SR + 48:SR + 64, :] = jnp.zeros((16, CW), BF16)

    start = pl.multiple_of(SR * j - win(j), 16)
    here[1].wait()

    def wx(k, slot, dev):
        cols = pl.ds(pl.multiple_of((dev // GROUP) * WC, 128), WC)
        return rcopy(
            w_ref.at[wrows(zi), cols], wbuf.at[slot, wrows(zi), :], w_s.at[k], w_r.at[k],
            at(i, dev),
        )

    def halfway(d):
        return ZC % 2 == 0 and d == ZC // 2 - 1

    def up_ring(d, z):
        part = wbuf.at[pl.ds(0, NJ // 2 if halfway(d) else NJ), wrows(z), :]
        return rcopy(part, part, up_s.at[d], up_r.at[d], at(zpos(zto(1)), j))

    def down_ring(d, z):
        first = NJ // 2 if halfway(d) else 0
        part = wbuf.at[pl.ds(first, NJ - first), wrows(z), :]
        return rcopy(part, part, dn_s.at[d], dn_r.at[d], at(zpos(zfrm(1)), j))

    def ring_start(d):
        if d < ZC // 2:
            up_ring(d, zfrm(d)).start()
        if d < ZC // 2:
            down_ring(d, zto(d)).start()

    def ring_wait(d):
        if d < ZC // 2:
            up_ring(d, zfrm(d + 1)).wait_recv()
        if d < ZC // 2:
            down_ring(d, zto(d + 1)).wait_recv()

    def slab(k, carry):
        pf, pr = carry

        @pl.when(k == NJ // 2)
        def _():
            for q in far_first:
                wx(q, j, to(q)).start()

        @pl.when(k > 0)
        def _():
            xa_in(k).wait_recv()

        b = frm(k)
        cols = pl.ds(pl.multiple_of(b * CW, 128), CW)
        cbuf[...] = xe[b, pl.ds(start, SR + 32), :].astype(F32)
        f, r = conv_pair(cw_ref[:, cols], cwr[:, cols])
        pf = pf + mm(f, pwv[cols, :])
        pr = pr + mm(r, pwr[cols, :])
        return pf, pr

    wide = pwv.shape[1]
    pf, pr = lax.fori_loop(
        0, NJ, slab, (jnp.zeros((SR, wide), F32), jnp.zeros((SR, wide), F32))
    )
    def bbx(k, slot, dev):
        return rcopy(bb.at[slot], bb.at[slot], bb_s.at[k], bb_r.at[k], at(i, dev))

    def ccx(k, slot, dev):
        return rcopy(cc.at[slot], cc.at[slot], cc_s.at[k], cc_r.at[k], at(i, dev))

    def dtx(k, slot, dev):
        return rcopy(dtout.at[dev], dtin.at[slot], dt_s.at[k], dt_r.at[k], at(i, dev))

    bb[j, :, 0:N] = pf[:, 0:N].astype(BF16)
    bb[j, :, N:2 * N] = pr[:, 0:N].astype(BF16)
    for k in far_first:
        bbx(k, j, to(k)).start()
    raw = jnp.concatenate([pf[:, 2 * N:], pr[:, 2 * N:]], axis=1).T
    bias = jnp.concatenate([prm[0], prm[0]], axis=0)
    v = raw + bias
    dts = jnp.maximum(v, 0.0) + jnp.log1p(jnp.exp(-jnp.abs(v)))
    for q in range(NJ):
        dtout[q, 0:HL, :] = dts[q * HL:(q + 1) * HL, :]
        dtout[q, HL:2 * HL, :] = dts[heads + (NJ - 1 - q) * HL:heads + (NJ - q) * HL, :]
    for k in far_first:
        dtx(k, j, to(k)).start()
    dtin[j] = dtout[j]
    cc[j, :, 0:N] = pf[:, N:2 * N].astype(BF16)
    cc[j, :, N:2 * N] = pr[:, N:2 * N].astype(BF16)

    for h in halo:
        h.wait_recv()

    @pl.when(i == 0)
    def _():
        xpad[0:16, :] = jnp.zeros((16, CW), BF16)

    @pl.when(i == NC - 1)
    def _():
        xpad[16 + T:32 + T, :] = jnp.zeros((16, CW), BF16)

    own_conv(0, 0)
    own_conv(NJ - 1, 0)

    for k in range(1, NJ):
        wx(k, frm(k), frm(k)).wait_recv()
    here[3].wait()
    ring_start(0)

    own = pl.ds(pl.multiple_of(j * HL, 8), HL)
    mirror = pl.ds(pl.multiple_of((NJ - 1 - j) * HL, 8), HL)

    def own_rows(which):
        return jnp.concatenate([prm[which, own, :], prm[which, mirror, :]], axis=0)

    rate = -jnp.exp(own_rows(1))
    src, dst = iota((SR, 2 * SR), 0), iota((SR, 2 * SR), 1)
    sums = jnp.where(dst < SR, dst - src, src - dst + SR) >= 0
    sums = jnp.where(sums, 1.0, 0.0).astype(BF16)
    is_fwd = iota((2 * HL, SR), 0) < HL
    chunk_lane = iota((2 * HL, SR), 1)

    def states(k, ends):
        c = frm(k)

        @pl.when(k > 0)
        def _():
            dtx(k, c, c).wait_recv()
            bbx(k, c, c).wait_recv()

        @pl.when(k == NJ // 2)
        def _():
            ring_wait(0)
            ring_start(1)

        @pl.when(k == 1)
        def _():
            for q in range(1, GROUP):
                ccx(q, j, to(q)).start()

        @pl.when(k == NJ - 1)
        def _():
            for q in range(GROUP, NJ):
                ccx(q, j, to(q)).start()

        rows = pl.ds(pl.multiple_of(c * SR, 16), SR)
        dt = dtin[c]
        a = dt * rate
        run = mm(terms(a), sums)
        run = run[0:2 * HL] + run[2 * HL:4 * HL] + run[4 * HL:6 * HL]
        cum = jnp.where(is_fwd, run[:, 0:SR], run[:, SR:2 * SR])
        end = jnp.sum(a, axis=1, keepdims=True)
        cumr[c] = cum
        tail = expand(jnp.exp(end - cum) * dt)
        tf = (xf[rows, :].astype(F32) * tail[:, 0:CW]).astype(BF16)
        tr = (xr[rows, :].astype(F32) * tail[:, CW:2 * CW]).astype(BF16)
        fresh[c, :, 0:CW] = mm(bb[c, :, 0:N], tf, ((0,), (0,)))
        fresh[c, :, CW:2 * CW] = mm(bb[c, :, N:2 * N], tr, ((0,), (0,)))
        return jnp.where(chunk_lane == c, end, ends)

    ends = lax.fori_loop(0, NJ, states, jnp.zeros((2 * HL, SR), F32))
    ends = jnp.where(chunk_lane == NJ, jnp.sum(ends, axis=1, keepdims=True), ends)
    whole = expand(jnp.exp(ends))
    for c in range(NJ):
        dch[c] = jnp.broadcast_to(whole[c:c + 1, :], (8, 2 * CW))
    dec_me[...] = jnp.broadcast_to(whole[NJ:NJ + 1, :], (8, 2 * CW))

    stin[...] = jnp.zeros((N, 2 * CW), F32)

    def fold(c, carry):
        r = NJ - 1 - c
        stin[:, 0:CW] = dch[c, 0:1, 0:CW] * stin[:, 0:CW] + fresh[c, :, 0:CW]
        stin[:, CW:2 * CW] = (
            dch[r, 0:1, CW:2 * CW] * stin[:, CW:2 * CW] + fresh[r, :, CW:2 * CW]
        )
        return carry

    lax.fori_loop(0, NJ, fold, 0)

    swap = [
        rcopy(stin, st_o, sb_s.at[0], sb_r.at[0], at(sib, j)),
        rcopy(dec_me, dec_o, sb_s.at[1], sb_r.at[1], at(sib, j)),
    ]
    for h in swap:
        h.start()
    for h in swap:
        h.wait_recv()
    mine = pl.ds(pl.multiple_of(core * (N // 2), 8), N // 2)
    s_me, s_o = stin[mine, :], st_o[mine, :]
    d_me, d_o = dec_me[0:1, :], dec_o[0:1, :]
    fwd_lane = jnp.where(iota((8, 2 * CW), 1) < CW, 1, 0)[0:1, :]
    other_last = fwd_lane == 1 - core
    pair = jnp.where(other_last, d_o * s_me + s_o, d_me * s_o + s_me)
    d_pair = jnp.broadcast_to(d_me * d_o, (8, 2 * CW))
    place = iota((16, 128), 0)
    d_tile = jnp.zeros((16, 128), F32)
    for q in range(LB):
        d = d_pair[:, q * 128:(q + 1) * 128][0:1, :]
        hi = d.astype(BF16).astype(F32)
        mid = (d - hi).astype(BF16).astype(F32)
        for t, term in enumerate((hi, mid, d - hi - mid)):
            d_tile = jnp.where(place == t * LB + q, term, d_tile)
    d_tile = d_tile.astype(BF16)
    for p in range(ZC):
        blocks = [pair[p * PR:(p + 1) * PR, q * 128:(q + 1) * 128] for q in range(LB)]
        zs[p, 0:LB * PR, :] = jnp.concatenate(blocks, axis=0).astype(BF16)
        zs[p, LB * PR:LB * PR + 16, :] = d_tile
    zr[zi] = zs[zi]

    def zx(k, slot, z):
        return rcopy(zs.at[z], zr.at[slot], zx_s.at[k], zx_r.at[k], at(zpos(z), j))

    def zy(k, slot, z):
        return rcopy(es.at[z], er.at[slot], zy_s.at[k], zy_r.at[k], at(zpos(z), j))

    for k in range(1, ZC):
        zx(k, zi, zto(k)).start()

    low = iota((SR, SR), 0) >= iota((SR, SR), 1)
    upp = iota((SR, SR), 0) <= iota((SR, SR), 1)
    lane_head = iota((8, CW), 1) // (CW // HL)
    skips = expand(own_rows(2))[0:8, :]

    def inner(k, carry):
        c = frm(k)

        @pl.when(k > 0)
        def _():
            ccx(k, c, c).wait_recv()

        rows = pl.ds(pl.multiple_of(c * SR, 16), SR)
        cum = cumr[c]
        cols = jnp.concatenate([cum, jnp.zeros((SR - 2 * HL, SR), F32)], axis=0).T
        lds = cum - jnp.log(dtin[c])
        y = jnp.zeros((SR, CW), F32)
        for d, (xs, mask) in enumerate(((xf, low), (xr, upp))):
            xv = xs[rows, :]
            part = slice(d * N, (d + 1) * N)
            score = mm(cc[c, :, part], bb[c, :, part], ((1,), (1,)))
            for q in range(HL):
                row = q if d == 0 else 2 * HL - 1 - q
                seg = jnp.where(mask, cols[:, row:row + 1] - lds[row:row + 1, :], -1e30)
                mcat[:, q * SR:(q + 1) * SR] = (score * jnp.exp(seg)).astype(BF16)
                keep = jnp.where(lane_head == q, 1.0, 0.0)[0:1, :].astype(BF16)
                xbd[q * SR:(q + 1) * SR, :] = xv * keep
            y = y + mm(mcat[...], xbd[...])
            y = y + skips[0:1, d * CW:(d + 1) * CW] * xv.astype(F32)
        yacc[rows, :] = y
        grown[c] = expand(jnp.exp(cum))
        return carry

    lax.fori_loop(0, 3, inner, 0)

    for k in range(1, ZC):
        zx(k, zfrm(k), zfrm(k)).wait_recv()

    pieces, decays = [], []
    for z in range(ZC):
        whole = zr[z].astype(F32)
        pieces.append(whole[0:LB * PR])
        tile = whole[LB * PR:LB * PR + 16]
        decays.append([
            tile[q:q + 1] + tile[LB + q:LB + q + 1] + tile[2 * LB + q:2 * LB + q + 1]
            for q in range(LB)
        ])

    def chain(q, e):
        order = range(ZC) if q < LB // 2 else range(ZC - 1, -1, -1)
        before = [None] * ZC
        for z in order:
            before[z] = e
            e = decays[z][q] * e + pieces[z][q * PR:(q + 1) * PR]
        return before, e

    zero = jnp.zeros((PR, 128), F32)
    if XL > 1:
        for q in range(LB):
            xs_[q * PR:(q + 1) * PR, :] = chain(q, zero)[1]
        cross = rcopy(xs_, xr_, sb_s.at[2], sb_r.at[2], at(across, j))
        cross.start()
        lax.fori_loop(3, 4, inner, 0)
        cross.wait_recv()
    before = []
    for q in range(LB):
        start_from = zero
        if XL > 1:
            takes = xlo == 1 if q < LB // 2 else xlo == 0
            start_from = jnp.where(takes, xr_[q * PR:(q + 1) * PR, :], 0.0)
        before.append(chain(q, start_from)[0])
    for z in range(ZC):
        es[z] = jnp.concatenate([before[q][z] for q in range(LB)], axis=0).astype(BF16)
    er[zi] = es[zi]
    for k in range(1, ZC):
        zy(k, zi, zto(k)).start()
    lax.fori_loop(4 if XL > 1 else 3, NJ, inner, 0)
    for k in range(1, ZC):
        zy(k, zfrm(k), zfrm(k)).wait_recv()
    ring_wait(1)
    ring_start(2)
    for p in range(ZC):
        piece = er[p].astype(F32)
        for q in range(LB):
            ech[pl.ds(pl.multiple_of(core * (N // 2) + p * PR, 8), PR), q * 128:(q + 1) * 128] = (
                piece[q * PR:(q + 1) * PR, :]
            )
    halves = rcopy(ech.at[mine, :], ech.at[mine, :], sb_s.at[3], sb_r.at[3], at(sib, j))
    halves.start()
    for h in swap:
        h.wait_send()
    theirs = pl.ds(pl.multiple_of((1 - core) * (N // 2), 8), N // 2)
    rcopy(ech.at[theirs, :], ech.at[theirs, :], sb_s.at[3], sb_r.at[3], at(sib, j)).wait_recv()
    other_first = fwd_lane == core
    stin[...] = jnp.where(other_first, dec_o[0:1, :] * ech[...] + st_o[...], ech[...])

    def enter(s, carry):
        for d in range(2):
            c = s if d == 0 else NJ - 1 - s
            lanes = slice(d * CW, (d + 1) * CW)
            st = stin[:, lanes]
            sbs[c, :, lanes] = st.astype(BF16)
            stin[:, lanes] = dch[c, 0:1, lanes] * st + fresh[c, :, lanes]
        return carry

    lax.fori_loop(0, NJ, enter, 0)

    HB = RB // 2

    def cbx(h, k, slot, dev):
        rows = pl.ds(pl.multiple_of(lax.rem(dev, GROUP) * RB + h * HB, 16), HB)
        return rcopy(
            comb_s.at[rows, :], comb_r.at[slot, pl.ds(h * HB, HB), :],
            cb_s.at[h, k], cb_r.at[h, k], at(i, dev),
        )

    chunks = HB // SR
    for h in range(2):

        def finish(n, carry):
            c = (n // chunks) * (2 * chunks) + h * chunks + lax.rem(n, chunks)
            rows = pl.ds(pl.multiple_of(c * SR, 16), SR)
            y = yacc[rows, :]
            for d in range(2):
                lanes = slice(d * CW, (d + 1) * CW)
                z = mm(cc[c, :, d * N:(d + 1) * N], sbs[c, :, lanes])
                y = y + grown[c, :, lanes] * z
            comb_s[rows, :] = (y * gain_ref[...]).astype(BF16)
            return carry

        lax.fori_loop(0, NJ // 2, finish, 0)
        for k in far_first:
            cbx(h, k, j, to(k)).start()
    comb_r[j] = comb_s[pl.ds(pl.multiple_of(yy * RB, 16), RB), :]
    ring_wait(2)
    ring_start(3)
    ring_wait(3)
    half = pl.ds(pl.multiple_of(core * (CW // 2), 16), CW // 2)
    rest = pl.ds(pl.multiple_of((1 - core) * (CW // 2), 16), CW // 2)
    share = rcopy(wbuf.at[:, half, :], wbuf.at[:, half, :], sb_s.at[4], sb_r.at[4], at(sib, j))
    share.start()
    for k in range(1, NJ):
        s = frm(k)
        rcopy(gall.at[s], gall.at[s], g_s.at[k], g_r.at[k], at(i, s)).wait_recv()
    rcopy(
        wbuf.at[:, rest, :], wbuf.at[:, rest, :], sb_s.at[4], sb_r.at[4], at(sib, j)
    ).wait_recv()

    def obx(h, k, slot, dest):
        rows = pl.ds(h * HB, HB)
        return rcopy(
            obs.at[dest, rows, :], obr.at[slot, rows, :], ob_s.at[h, k], ob_r.at[h, k],
            at(i, xh * GROUP + dest),
        )

    for h in range(2):
        rows = slice(h * HB, (h + 1) * HB)
        acc[...] = jnp.zeros((HB, WC), F32)
        sqs[...] = jnp.zeros((HB, CW), F32)

        def project(k, carry):
            @pl.when(k > 0)
            def _():
                cbx(h, k, frm(k), frm(k)).wait_recv()

            b = frm(k)
            piece = comb_r[b, rows, :]
            acc[...] += mm(piece, wbuf[b])
            value = piece.astype(F32)
            sqs[...] += value * value * gall[b, 0:1, :]
            return carry

        lax.fori_loop(0, NJ, project, 0)
        scale = lax.rsqrt(jnp.sum(sqs[...], axis=1, keepdims=True) / D + EPS)
        for q in range(GROUP):
            obs[q, rows, :] = (acc[:, q * CW:(q + 1) * CW] * scale).astype(BF16)
        for k in range(1, GROUP):
            obx(h, k, yy, lax.rem(yy + k, GROUP)).start()
    def place_out(n, src, s, h, size):
        rows = pl.ds(pl.multiple_of(s * RB + h * HB, 16), size)
        return pltpu.make_async_copy(src, out_ref.at[rows, :], oc.at[n])

    outs = [place_out(0, obs.at[yy], yy, 0, RB)]
    outs[0].start()
    for h in range(2):
        for k in range(1, GROUP):
            s = lax.rem(yy + GROUP - k, GROUP)
            obx(h, k, s, s).wait_recv()
            outs.append(
                place_out(h * GROUP + k, obr.at[s, pl.ds(h * HB, HB), :], s, h, HB)
            )
            outs[-1].start()
    for h in outs:
        h.wait()

    slab_pre.wait_send()
    slab_post.wait_send()
    for h in halo:
        h.wait_send()
    for g in gains:
        g.wait_send()
    for k in range(1, NJ):
        xa(k, to(k)).wait_send()
        dtx(k, j, to(k)).wait_send()
        bbx(k, j, to(k)).wait_send()
        ccx(k, j, to(k)).wait_send()
        wx(k, j, to(k)).wait_send()
        for h in range(2):
            cbx(h, k, j, to(k)).wait_send()

    for k in range(1, ZC):
        zx(k, zi, zto(k)).wait_send()
        zy(k, zi, zto(k)).wait_send()
    if XL > 1:
        cross.wait_send()
    halves.wait_send()
    share.wait_send()
    for d in range(ZC // 2):
        up_ring(d, zfrm(d)).wait_send()
    for d in range(ZC // 2):
        down_ring(d, zto(d)).wait_send()
    for h in range(2):
        for k in range(1, GROUP):
            obx(h, k, yy, lax.rem(yy + k, GROUP)).wait_send()


def shards(x_in, conv_weight, proj_weight, dt_bias, decay_log, skip_gain, norm_gain, out_weight):
    T, CW = x_in.shape
    D = conv_weight.shape[1]
    H = dt_bias.shape[0]
    N = (proj_weight.shape[1] - H) // 2
    NC, NJ = lax.axis_size("ctx"), lax.axis_size("chan")
    HL = H // NJ
    SR = T // NJ
    XL = 2 if NC >= 4 else 1
    ZC = NC // (2 * XL)
    PR, LB = N // 2 // ZC, 2 * CW // 128
    RB, WC = T // GROUP, GROUP * CW
    dma = pltpu.SemaphoreType.DMA
    vm = pltpu.VMEM
    scratch = [
        vm((T + 32, CW), BF16), vm((NJ, SR + 64, CW), BF16), vm((SR + 32, CW), F32),
        vm((4, D), F32), vm((T, CW), BF16), vm((T, CW), BF16),
        vm((NJ, SR, 2 * N), BF16), vm((NJ, SR, 2 * N), BF16),
        vm((NJ, 2 * HL, SR), F32), vm((NJ, 2 * HL, SR), F32),
        vm((NJ, 2 * HL, SR), F32),
        vm((NJ, N, 2 * CW), F32), vm((NJ, 8, 2 * CW), F32), vm((T, CW), F32),
        vm((SR, HL * SR), BF16), vm((HL * SR, CW), BF16), vm((6 * HL, 2 * CW), BF16),
        vm((ZC, LB * PR + 16, 128), BF16), vm((ZC, LB * PR + 16, 128), BF16),
        vm((ZC, LB * PR, 128), BF16), vm((ZC, LB * PR, 128), BF16),
        vm((LB * PR, 128), F32), vm((LB * PR, 128), F32),
        vm((N, 2 * CW), F32), vm((N, 2 * CW), F32), vm((8, 2 * CW), F32), vm((8, 2 * CW), F32),
        vm((N, 2 * CW), F32),
        vm((T, CW), BF16), vm((NJ, RB, CW), BF16), vm((NJ, 8, CW), F32),
        vm((NJ, CW, WC), BF16), vm((RB // 2, WC), F32),
        vm((GROUP, RB, CW), BF16), vm((GROUP, RB, CW), BF16),
        vm((RB // 2, CW), F32), vm((NJ, SR, 2 * CW), F32), vm((NJ, N, 2 * CW), BF16),
        dma((NJ,)), dma((NJ,)), dma((4,)), dma((2 + NJ,)), dma((NJ,)), dma((NJ,)),
        dma((NJ,)), dma((NJ,)), dma((4,)), dma((4,)), dma((4,)), dma((4,)),
        dma((NJ,)), dma((NJ,)), dma((NJ,)), dma((NJ,)), dma((NJ,)), dma((NJ,)),
        dma((ZC,)), dma((ZC,)), dma((ZC,)), dma((ZC,)), dma((5,)), dma((5,)),
        dma((2, NJ)), dma((2, NJ)), dma((2, GROUP)), dma((2, GROUP)),
        vm(proj_weight.shape, BF16), vm(proj_weight.shape, BF16),
        vm(proj_weight.shape[::-1], BF16), vm((3, H, 128), F32), dma((9,)),
        vm((4, D), F32), vm((1, H), F32), vm((1, H), F32), vm((1, H), F32), vm((1, CW), F32), dma((2 * GROUP,)),
    ]
    return pl.pallas_call(
        functools.partial(kernel, (NC, NJ, T, CW, D, N, HL, XL, ZC)),
        out_shape=jax.ShapeDtypeStruct((T, CW), BF16),
        in_specs=[pl.BlockSpec(memory_space=pl.ANY)] * 8,
        out_specs=pl.BlockSpec(memory_space=pl.ANY),
        scratch_shapes=scratch,
        compiler_params=pltpu.CompilerParams(
            collective_id=0, has_side_effects=True, vmem_limit_bytes=62 * 1024 * 1024
        ),
        cost_estimate=pl.CostEstimate(
            flops=4 * T * D * CW, bytes_accessed=8 * T * CW, transcendentals=16 * T * SR
        ),
    )(
        x_in, conv_weight, proj_weight.T, dt_bias[None], decay_log[None], skip_gain[None],
        norm_gain[None], out_weight,
    )


def solution(mesh):
    in_specs = (P("ctx", "chan"), P(), P(), P(), P(), P(), P("chan"), P("chan", None))
    out_specs = P("ctx", "chan")
    return jax.shard_map(shards, mesh=mesh, in_specs=in_specs, out_specs=out_specs, check_vma=False)
```

```python
import functools

import jax
import jax.numpy as jnp
from jax import lax
from jax.experimental import pallas as pl
from jax.experimental.pallas import tpu as pltpu
from jax.sharding import PartitionSpec as P

F32 = jnp.float32
BF16 = jnp.bfloat16
MESH = pl.DeviceIdType.MESH
EPS = 1e-05
GROUP = 4


def mm(a, b, dims=((1,), (0,)), **kw):
    return lax.dot_general(a, b, (dims, ((), ())), preferred_element_type=F32, **kw)


def silu(v):
    return v / (1.0 + jnp.exp(-v))


def iota(shape, axis):
    return lax.broadcasted_iota(jnp.int32, shape, axis)


def kernel(
    dims,
    x_ref, cw_hbm, pw_ref, bias_hbm, decay_hbm, skip_hbm, gain_hbm, w_ref, out_ref,
    xpad, xe, cbuf, cwr, xf, xr, bb, cc, dtout, dtin, cumr, fresh, dch, yacc,
    mcat, xbd, emat, zs, zr, es, er, xs_, xr_, st_o, ech, dec_me, dec_o, stin, comb_s, comb_r, gall, wbuf, acc, obs, obr, sqs, grown, sbs,
    xa_s, xa_r, ha_s, ha_r, g_s, g_r, w_s, w_r, up_s, up_r, dn_s, dn_r, bb_s, bb_r, cc_s, cc_r, dt_s, dt_r,
    zx_s, zx_r, zy_s, zy_r, sb_s, sb_r, cb_s, cb_r, ob_s, ob_r, pwv, pwr, pwt, prm, lc,
    cw_ref, bias_ref, decay_ref, skip_ref, gain_ref, oc,
):
    NC, NJ, T, CW, D, N, HL, XL, ZC = dims
    SR = T // NJ
    PR = N // 2 // ZC
    LB = 2 * CW // 128
    WR = CW // 2 // ZC
    RB = T // GROUP
    WC = GROUP * CW
    i = lax.axis_index("ctx")
    j = lax.axis_index("chan")
    prev_i = lax.rem(i + NC - 1, NC)
    next_i = lax.rem(i + 1, NC)
    core = lax.rem(i, 2)
    sib = i + 1 - 2 * core
    xlo = i // (2 * ZC)
    zi = lax.rem(i // 2, ZC)
    xh = j // GROUP
    yy = lax.rem(j, GROUP)

    def at(ci, cj):
        return {"ctx": ci, "chan": cj}

    def to(k):
        return lax.rem(xh + k // GROUP, 2) * GROUP + lax.rem(yy + lax.rem(k, GROUP), GROUP)

    def frm(k):
        return (
            lax.rem(xh + k // GROUP, 2) * GROUP
            + lax.rem(yy + GROUP - lax.rem(k, GROUP), GROUP)
        )

    far_first = (6, 5, 7, 4, 2, 1, 3)

    def rcopy(src, dst, ss, rs, dev):
        return pltpu.make_async_remote_copy(
            src_ref=src, dst_ref=dst, send_sem=ss, recv_sem=rs, device_id=dev, device_id_type=MESH
        )

    def win(jd):
        return pl.multiple_of(jnp.clip(SR * jd - 16, 0, T - SR - 32), 16)

    def wrows(z):
        return pl.ds(pl.multiple_of(core * (CW // 2) + z * WR, 16), WR)

    own_wide = pl.ds(pl.multiple_of(xh * WC, 128), WC)
    here = [
        pltpu.make_async_copy(x_ref, xpad.at[pl.ds(16, T), :], lc.at[0]),
        pltpu.make_async_copy(
            x_ref.at[pl.ds(win(j), SR + 32), :], xe.at[j, pl.ds(16, SR + 32), :], lc.at[1]
        ),
        pltpu.make_async_copy(pw_ref, pwt, lc.at[2]),
        pltpu.make_async_copy(
            w_ref.at[wrows(zi), own_wide], wbuf.at[j, wrows(zi), :], lc.at[3]
        ),
    ]
    small = [
        pltpu.make_async_copy(src, dst, lc.at[4 + q])
        for q, (src, dst) in enumerate((
            (cw_hbm, cw_ref), (bias_hbm, bias_ref), (decay_hbm, decay_ref),
            (skip_hbm, skip_ref), (gain_hbm, gain_ref),
        ))
    ]
    for h in small + here:
        h.start()

    barrier = pltpu.get_barrier_semaphore()

    def hail(dev):
        pl.semaphore_signal(barrier, inc=1, device_id=dev, device_id_type=MESH)

    for k in range(1, NJ):
        hail(at(i, to(k)))

    def zpos(z):
        return xlo * (2 * ZC) + z * 2 + core

    def zto(k):
        return lax.rem(zi + k, ZC)

    def zfrm(k):
        return lax.rem(zi + ZC - k, ZC)

    for k in range(1, ZC):
        hail(at(zpos(zto(k)), j))
    across = lax.rem(i + 2 * ZC, NC)
    if XL > 1:
        hail(at(across, j))
    for c in (sib, prev_i, next_i):
        hail(at(c, j))

    @pl.when(j == 0)
    def _():
        for q in range(NJ):
            hail(at(prev_i, q))

    @pl.when(j == NJ - 1)
    def _():
        for q in range(NJ):
            hail(at(next_i, q))

    for h in small:
        h.wait()
    gall[j] = jnp.broadcast_to(1.0 / (gain_ref[...] * gain_ref[...]), (8, CW))
    heads = HL * NJ
    eye = iota((heads, heads), 0) == iota((heads, heads), 1)
    for q, ref in enumerate((bias_ref, decay_ref, skip_ref)):
        row = jnp.broadcast_to(ref[...], (heads, heads))
        column = jnp.sum(jnp.where(eye, row, 0.0), axis=1, keepdims=True)
        prm[q] = jnp.broadcast_to(column, (heads, 128))
    anti = iota((CW, CW), 0) + iota((CW, CW), 1) == CW - 1
    anti_f = jnp.where(anti, 1.0, 0.0).astype(F32)
    anti_b = anti_f.astype(BF16)
    for b in range(NJ):
        cwr[:, b * CW:(b + 1) * CW] = mm(
            cw_ref[:, (NJ - 1 - b) * CW:(NJ - b) * CW], anti_f, precision=lax.Precision.HIGHEST
        )
    head_row = lax.rem(iota((6 * HL, 2 * CW), 0), 2 * HL)
    ec = iota((6 * HL, 2 * CW), 1)
    head_of = ec // (CW // HL)
    target = jnp.where(head_of < HL, head_of, 3 * HL - 1 - head_of)
    emat[...] = jnp.where(head_row == target, 1.0, 0.0).astype(BF16)

    def terms(rows):
        hi = rows.astype(BF16)
        rest = rows - hi.astype(F32)
        mid = rest.astype(BF16)
        low = (rest - mid.astype(F32)).astype(BF16)
        return jnp.concatenate([hi, mid, low], axis=0)

    def expand(rows):
        return mm(terms(rows), emat[...], ((0,), (0,)))

    pl.semaphore_wait(barrier, NJ - 1 + ZC - 1 + XL - 1 + 3 + 2)

    def xa(k, jd):
        return rcopy(
            x_ref.at[pl.ds(win(jd), SR + 32), :], xe.at[j, pl.ds(16, SR + 32), :],
            xa_s.at[k], xa_r.at[k], at(i, jd),
        )

    def xa_in(k):
        return rcopy(
            x_ref.at[pl.ds(0, SR + 32), :], xe.at[frm(k), pl.ds(16, SR + 32), :],
            xa_s.at[k], xa_r.at[k], at(i, frm(k)),
        )

    lastrows, firstrows = x_ref.at[pl.ds(T - 16, 16), :], x_ref.at[pl.ds(0, 16), :]
    halo = [
        rcopy(lastrows, xpad.at[pl.ds(0, 16), :], ha_s.at[0], ha_r.at[0], at(next_i, j)),
        rcopy(firstrows, xpad.at[pl.ds(16 + T, 16), :], ha_s.at[1], ha_r.at[1], at(prev_i, j)),
    ]
    slab_pre = rcopy(
        lastrows, xe.at[j, pl.ds(0, 16), :], ha_s.at[2], ha_r.at[2 + j], at(next_i, 0)
    )
    slab_post = rcopy(
        firstrows, xe.at[j, pl.ds(SR + 48, 16), :], ha_s.at[3], ha_r.at[2 + j], at(prev_i, NJ - 1)
    )
    slab_pre.start()
    slab_post.start()
    for k in far_first:
        xa(k, to(k)).start()
    for h in halo:
        h.start()
    gains = [
        rcopy(gall.at[j], gall.at[j], g_s.at[k], g_r.at[k], at(i, to(k))) for k in range(1, NJ)
    ]
    for g in gains:
        g.start()

    def conv_pair(taps, rtaps):
        vf = taps[0:1, :] * cbuf[13:13 + SR, :]
        vr = rtaps[0:1, :] * cbuf[19:19 + SR, :]
        for k in range(1, 4):
            vf = vf + taps[k:k + 1, :] * cbuf[13 + k:13 + k + SR, :]
            vr = vr + rtaps[k:k + 1, :] * cbuf[19 - k:19 - k + SR, :]
        return silu(vf).astype(BF16), silu(vr).astype(BF16)

    here[2].wait()
    for b in range(NJ):
        block = pwt[:, b * CW:(b + 1) * CW].T
        pwv[b * CW:(b + 1) * CW, :] = block
        pwr[(NJ - 1 - b) * CW:(NJ - b) * CW, :] = mm(anti_b, block).astype(BF16)

    own_cols = pl.ds(pl.multiple_of(j * CW, 128), CW)

    def own_conv(c, carry):
        rows = pl.ds(pl.multiple_of(c * SR, 16), SR)
        cbuf[...] = xpad[pl.ds(pl.multiple_of(c * SR, 16), SR + 32), :].astype(F32)
        f, r = conv_pair(cw_ref[:, own_cols], cwr[:, own_cols])
        xf[rows, :] = f
        xr[rows, :] = r
        return carry

    here[0].wait()
    lax.fori_loop(1, NJ - 1, own_conv, 0)

    @pl.when(j == 0)
    def _():
        for q in range(NJ):
            rcopy(
                lastrows, xe.at[q, pl.ds(0, 16), :], ha_s.at[2], ha_r.at[2 + q], at(prev_i, q)
            ).wait_recv()

    @pl.when(j == NJ - 1)
    def _():
        for q in range(NJ):
            rcopy(
                firstrows, xe.at[q, pl.ds(SR + 48, 16), :], ha_s.at[3], ha_r.at[2 + q],
                at(next_i, q),
            ).wait_recv()

    @pl.when(jnp.logical_and(i == 0, j == 0))
    def _():
        for q in range(NJ):
            xe[q, 0:16, :] = jnp.zeros((16, CW), BF16)

    @pl.when(jnp.logical_and(i == NC - 1, j == NJ - 1))
    def _():
        for q in range(NJ):
            xe[q, SR + 48:SR + 64, :] = jnp.zeros((16, CW), BF16)

    start = pl.multiple_of(SR * j - win(j), 16)
    here[1].wait()

    def wx(k, slot, dev):
        cols = pl.ds(pl.multiple_of((dev // GROUP) * WC, 128), WC)
        return rcopy(
            w_ref.at[wrows(zi), cols], wbuf.at[slot, wrows(zi), :], w_s.at[k], w_r.at[k],
            at(i, dev),
        )

    def halfway(d):
        return ZC % 2 == 0 and d == ZC // 2 - 1

    def up_ring(d, z):
        part = wbuf.at[pl.ds(0, NJ // 2 if halfway(d) else NJ), wrows(z), :]
        return rcopy(part, part, up_s.at[d], up_r.at[d], at(zpos(zto(1)), j))

    def down_ring(d, z):
        first = NJ // 2 if halfway(d) else 0
        part = wbuf.at[pl.ds(first, NJ - first), wrows(z), :]
        return rcopy(part, part, dn_s.at[d], dn_r.at[d], at(zpos(zfrm(1)), j))

    def ring_start(d):
        if d < ZC // 2:
            up_ring(d, zfrm(d)).start()
        if d < ZC // 2:
            down_ring(d, zto(d)).start()

    def ring_wait(d):
        if d < ZC // 2:
            up_ring(d, zfrm(d + 1)).wait_recv()
        if d < ZC // 2:
            down_ring(d, zto(d + 1)).wait_recv()

    def slab(k, carry):
        pf, pr = carry

        @pl.when(k == NJ // 2)
        def _():
            for q in far_first:
                wx(q, j, to(q)).start()

        @pl.when(k > 0)
        def _():
            xa_in(k).wait_recv()

        b = frm(k)
        cols = pl.ds(pl.multiple_of(b * CW, 128), CW)
        cbuf[...] = xe[b, pl.ds(start, SR + 32), :].astype(F32)
        f, r = conv_pair(cw_ref[:, cols], cwr[:, cols])
        pf = pf + mm(f, pwv[cols, :])
        pr = pr + mm(r, pwr[cols, :])
        return pf, pr

    wide = pwv.shape[1]
    pf, pr = lax.fori_loop(
        0, NJ, slab, (jnp.zeros((SR, wide), F32), jnp.zeros((SR, wide), F32))
    )
    def bbx(k, slot, dev):
        return rcopy(bb.at[slot], bb.at[slot], bb_s.at[k], bb_r.at[k], at(i, dev))

    def relay(k, slot, dev):
        return rcopy(bb.at[slot], bb.at[slot], bb_s.at[GROUP + k], bb_r.at[GROUP + k], at(i, dev))

    def ccx(k, slot, dev):
        return rcopy(cc.at[slot], cc.at[slot], cc_s.at[k], cc_r.at[k], at(i, dev))

    def dtx(k, slot, dev):
        return rcopy(dtout.at[dev], dtin.at[slot], dt_s.at[k], dt_r.at[k], at(i, dev))

    bb[j, :, 0:N] = pf[:, 0:N].astype(BF16)
    bb[j, :, N:2 * N] = pr[:, 0:N].astype(BF16)
    for k in (GROUP, 2, 1, 3):
        bbx(k, j, to(k)).start()
    raw = jnp.concatenate([pf[:, 2 * N:], pr[:, 2 * N:]], axis=1).T
    bias = jnp.concatenate([prm[0], prm[0]], axis=0)
    v = raw + bias
    dts = jnp.maximum(v, 0.0) + jnp.log1p(jnp.exp(-jnp.abs(v)))
    for q in range(NJ):
        dtout[q, 0:HL, :] = dts[q * HL:(q + 1) * HL, :]
        dtout[q, HL:2 * HL, :] = dts[heads + (NJ - 1 - q) * HL:heads + (NJ - q) * HL, :]
    for k in far_first:
        dtx(k, j, to(k)).start()
    dtin[j] = dtout[j]
    cc[j, :, 0:N] = pf[:, N:2 * N].astype(BF16)
    cc[j, :, N:2 * N] = pr[:, N:2 * N].astype(BF16)

    for h in halo:
        h.wait_recv()

    @pl.when(i == 0)
    def _():
        xpad[0:16, :] = jnp.zeros((16, CW), BF16)

    @pl.when(i == NC - 1)
    def _():
        xpad[16 + T:32 + T, :] = jnp.zeros((16, CW), BF16)

    own_conv(0, 0)
    own_conv(NJ - 1, 0)

    bbx(GROUP, frm(GROUP), frm(GROUP)).wait_recv()
    for k in (2, 1, 3):
        relay(k, to(GROUP), to(k)).start()

    for k in range(1, NJ):
        wx(k, frm(k), frm(k)).wait_recv()
    here[3].wait()
    ring_start(0)

    own = pl.ds(pl.multiple_of(j * HL, 8), HL)
    mirror = pl.ds(pl.multiple_of((NJ - 1 - j) * HL, 8), HL)

    def own_rows(which):
        return jnp.concatenate([prm[which, own, :], prm[which, mirror, :]], axis=0)

    rate = -jnp.exp(own_rows(1))
    src, dst = iota((SR, 2 * SR), 0), iota((SR, 2 * SR), 1)
    sums = jnp.where(dst < SR, dst - src, src - dst + SR) >= 0
    sums = jnp.where(sums, 1.0, 0.0).astype(BF16)
    is_fwd = iota((2 * HL, SR), 0) < HL
    chunk_lane = iota((2 * HL, SR), 1)

    def states(k, ends):
        c = frm(k)

        @pl.when(k > 0)
        def _():
            dtx(k, c, c).wait_recv()

        @pl.when(jnp.logical_and(k > 0, k < GROUP))
        def _():
            bbx(k, c, c).wait_recv()

        @pl.when(k > GROUP)
        def _():
            relay(k - GROUP, c, c).wait_recv()

        @pl.when(k == NJ // 2)
        def _():
            ring_wait(0)
            ring_start(1)

        @pl.when(k == 1)
        def _():
            for q in range(1, GROUP):
                ccx(q, j, to(q)).start()

        @pl.when(k == NJ - 1)
        def _():
            for q in range(GROUP, NJ):
                ccx(q, j, to(q)).start()

        rows = pl.ds(pl.multiple_of(c * SR, 16), SR)
        dt = dtin[c]
        a = dt * rate
        run = mm(terms(a), sums)
        run = run[0:2 * HL] + run[2 * HL:4 * HL] + run[4 * HL:6 * HL]
        cum = jnp.where(is_fwd, run[:, 0:SR], run[:, SR:2 * SR])
        end = jnp.sum(a, axis=1, keepdims=True)
        cumr[c] = cum
        tail = expand(jnp.exp(end - cum) * dt)
        tf = (xf[rows, :].astype(F32) * tail[:, 0:CW]).astype(BF16)
        tr = (xr[rows, :].astype(F32) * tail[:, CW:2 * CW]).astype(BF16)
        fresh[c, :, 0:CW] = mm(bb[c, :, 0:N], tf, ((0,), (0,)))
        fresh[c, :, CW:2 * CW] = mm(bb[c, :, N:2 * N], tr, ((0,), (0,)))
        return jnp.where(chunk_lane == c, end, ends)

    ends = lax.fori_loop(0, NJ, states, jnp.zeros((2 * HL, SR), F32))
    ends = jnp.where(chunk_lane == NJ, jnp.sum(ends, axis=1, keepdims=True), ends)
    whole = expand(jnp.exp(ends))
    for c in range(NJ):
        dch[c] = jnp.broadcast_to(whole[c:c + 1, :], (8, 2 * CW))
    dec_me[...] = jnp.broadcast_to(whole[NJ:NJ + 1, :], (8, 2 * CW))

    stin[...] = jnp.zeros((N, 2 * CW), F32)

    def fold(c, carry):
        r = NJ - 1 - c
        stin[:, 0:CW] = dch[c, 0:1, 0:CW] * stin[:, 0:CW] + fresh[c, :, 0:CW]
        stin[:, CW:2 * CW] = (
            dch[r, 0:1, CW:2 * CW] * stin[:, CW:2 * CW] + fresh[r, :, CW:2 * CW]
        )
        return carry

    lax.fori_loop(0, NJ, fold, 0)

    swap = [
        rcopy(stin, st_o, sb_s.at[0], sb_r.at[0], at(sib, j)),
        rcopy(dec_me, dec_o, sb_s.at[1], sb_r.at[1], at(sib, j)),
    ]
    for h in swap:
        h.start()
    for h in swap:
        h.wait_recv()
    mine = pl.ds(pl.multiple_of(core * (N // 2), 8), N // 2)
    s_me, s_o = stin[mine, :], st_o[mine, :]
    d_me, d_o = dec_me[0:1, :], dec_o[0:1, :]
    fwd_lane = jnp.where(iota((8, 2 * CW), 1) < CW, 1, 0)[0:1, :]
    other_last = fwd_lane == 1 - core
    pair = jnp.where(other_last, d_o * s_me + s_o, d_me * s_o + s_me)
    d_pair = jnp.broadcast_to(d_me * d_o, (8, 2 * CW))
    place = iota((16, 128), 0)
    d_tile = jnp.zeros((16, 128), F32)
    for q in range(LB):
        d = d_pair[:, q * 128:(q + 1) * 128][0:1, :]
        hi = d.astype(BF16).astype(F32)
        mid = (d - hi).astype(BF16).astype(F32)
        for t, term in enumerate((hi, mid, d - hi - mid)):
            d_tile = jnp.where(place == t * LB + q, term, d_tile)
    d_tile = d_tile.astype(BF16)
    for p in range(ZC):
        blocks = [pair[p * PR:(p + 1) * PR, q * 128:(q + 1) * 128] for q in range(LB)]
        zs[p, 0:LB * PR, :] = jnp.concatenate(blocks, axis=0).astype(BF16)
        zs[p, LB * PR:LB * PR + 16, :] = d_tile
    zr[zi] = zs[zi]

    def zx(k, slot, z):
        return rcopy(zs.at[z], zr.at[slot], zx_s.at[k], zx_r.at[k], at(zpos(z), j))

    def zy(k, slot, z):
        return rcopy(es.at[z], er.at[slot], zy_s.at[k], zy_r.at[k], at(zpos(z), j))

    for k in range(1, ZC):
        zx(k, zi, zto(k)).start()

    low = iota((SR, SR), 0) >= iota((SR, SR), 1)
    upp = iota((SR, SR), 0) <= iota((SR, SR), 1)
    lane_head = iota((8, CW), 1) // (CW // HL)
    skips = expand(own_rows(2))[0:8, :]

    def inner(k, carry):
        c = frm(k)

        @pl.when(k > 0)
        def _():
            ccx(k, c, c).wait_recv()

        rows = pl.ds(pl.multiple_of(c * SR, 16), SR)
        cum = cumr[c]
        cols = jnp.concatenate([cum, jnp.zeros((SR - 2 * HL, SR), F32)], axis=0).T
        lds = cum - jnp.log(dtin[c])
        y = jnp.zeros((SR, CW), F32)
        for d, (xs, mask) in enumerate(((xf, low), (xr, upp))):
            xv = xs[rows, :]
            part = slice(d * N, (d + 1) * N)
            score = mm(cc[c, :, part], bb[c, :, part], ((1,), (1,)))
            for q in range(HL):
                row = q if d == 0 else 2 * HL - 1 - q
                seg = jnp.where(mask, cols[:, row:row + 1] - lds[row:row + 1, :], -1e30)
                mcat[:, q * SR:(q + 1) * SR] = (score * jnp.exp(seg)).astype(BF16)
                keep = jnp.where(lane_head == q, 1.0, 0.0)[0:1, :].astype(BF16)
                xbd[q * SR:(q + 1) * SR, :] = xv * keep
            y = y + mm(mcat[...], xbd[...])
            y = y + skips[0:1, d * CW:(d + 1) * CW] * xv.astype(F32)
        yacc[rows, :] = y
        grown[c] = expand(jnp.exp(cum))
        return carry

    lax.fori_loop(0, 3, inner, 0)

    for k in range(1, ZC):
        zx(k, zfrm(k), zfrm(k)).wait_recv()
    ring_wait(1)
    ring_start(2)

    pieces, decays = [], []
    for z in range(ZC):
        whole = zr[z].astype(F32)
        pieces.append(whole[0:LB * PR])
        tile = whole[LB * PR:LB * PR + 16]
        decays.append([
            tile[q:q + 1] + tile[LB + q:LB + q + 1] + tile[2 * LB + q:2 * LB + q + 1]
            for q in range(LB)
        ])

    def chain(q, e):
        order = range(ZC) if q < LB // 2 else range(ZC - 1, -1, -1)
        before = [None] * ZC
        for z in order:
            before[z] = e
            e = decays[z][q] * e + pieces[z][q * PR:(q + 1) * PR]
        return before, e

    zero = jnp.zeros((PR, 128), F32)
    if XL > 1:
        for q in range(LB):
            xs_[q * PR:(q + 1) * PR, :] = chain(q, zero)[1]
        cross = rcopy(xs_, xr_, sb_s.at[2], sb_r.at[2], at(across, j))
        cross.start()
        lax.fori_loop(3, 4, inner, 0)
        cross.wait_recv()
    before = []
    for q in range(LB):
        start_from = zero
        if XL > 1:
            takes = xlo == 1 if q < LB // 2 else xlo == 0
            start_from = jnp.where(takes, xr_[q * PR:(q + 1) * PR, :], 0.0)
        before.append(chain(q, start_from)[0])
    for z in range(ZC):
        es[z] = jnp.concatenate([before[q][z] for q in range(LB)], axis=0).astype(BF16)
    er[zi] = es[zi]
    for k in range(1, ZC):
        zy(k, zi, zto(k)).start()
    lax.fori_loop(4 if XL > 1 else 3, NJ, inner, 0)
    for k in range(1, ZC):
        zy(k, zfrm(k), zfrm(k)).wait_recv()
    ring_wait(2)
    ring_start(3)
    for p in range(ZC):
        piece = er[p].astype(F32)
        for q in range(LB):
            ech[pl.ds(pl.multiple_of(core * (N // 2) + p * PR, 8), PR), q * 128:(q + 1) * 128] = (
                piece[q * PR:(q + 1) * PR, :]
            )
    halves = rcopy(ech.at[mine, :], ech.at[mine, :], sb_s.at[3], sb_r.at[3], at(sib, j))
    halves.start()
    for h in swap:
        h.wait_send()
    theirs = pl.ds(pl.multiple_of((1 - core) * (N // 2), 8), N // 2)
    rcopy(ech.at[theirs, :], ech.at[theirs, :], sb_s.at[3], sb_r.at[3], at(sib, j)).wait_recv()
    other_first = fwd_lane == core
    stin[...] = jnp.where(other_first, dec_o[0:1, :] * ech[...] + st_o[...], ech[...])

    def enter(s, carry):
        for d in range(2):
            c = s if d == 0 else NJ - 1 - s
            lanes = slice(d * CW, (d + 1) * CW)
            st = stin[:, lanes]
            sbs[c, :, lanes] = st.astype(BF16)
            stin[:, lanes] = dch[c, 0:1, lanes] * st + fresh[c, :, lanes]
        return carry

    lax.fori_loop(0, NJ, enter, 0)

    HB = RB // 2

    def cbx(h, k, slot, dev):
        rows = pl.ds(pl.multiple_of(lax.rem(dev, GROUP) * RB + h * HB, 16), HB)
        return rcopy(
            comb_s.at[rows, :], comb_r.at[slot, pl.ds(h * HB, HB), :],
            cb_s.at[h, k], cb_r.at[h, k], at(i, dev),
        )

    chunks = HB // SR
    for h in range(2):

        def finish(n, carry):
            c = (n // chunks) * (2 * chunks) + h * chunks + lax.rem(n, chunks)
            rows = pl.ds(pl.multiple_of(c * SR, 16), SR)
            y = yacc[rows, :]
            for d in range(2):
                lanes = slice(d * CW, (d + 1) * CW)
                z = mm(cc[c, :, d * N:(d + 1) * N], sbs[c, :, lanes])
                y = y + grown[c, :, lanes] * z
            comb_s[rows, :] = (y * gain_ref[...]).astype(BF16)
            return carry

        lax.fori_loop(0, NJ // 2, finish, 0)
        for k in far_first:
            cbx(h, k, j, to(k)).start()
    comb_r[j] = comb_s[pl.ds(pl.multiple_of(yy * RB, 16), RB), :]
    ring_wait(3)
    half = pl.ds(pl.multiple_of(core * (CW // 2), 16), CW // 2)
    rest = pl.ds(pl.multiple_of((1 - core) * (CW // 2), 16), CW // 2)
    share = rcopy(wbuf.at[:, half, :], wbuf.at[:, half, :], sb_s.at[4], sb_r.at[4], at(sib, j))
    share.start()
    for k in range(1, NJ):
        s = frm(k)
        rcopy(gall.at[s], gall.at[s], g_s.at[k], g_r.at[k], at(i, s)).wait_recv()
    rcopy(
        wbuf.at[:, rest, :], wbuf.at[:, rest, :], sb_s.at[4], sb_r.at[4], at(sib, j)
    ).wait_recv()

    def obx(h, k, slot, dest):
        rows = pl.ds(h * HB, HB)
        return rcopy(
            obs.at[dest, rows, :], obr.at[slot, rows, :], ob_s.at[h, k], ob_r.at[h, k],
            at(i, xh * GROUP + dest),
        )

    for h in range(2):
        rows = slice(h * HB, (h + 1) * HB)
        acc[...] = jnp.zeros((HB, WC), F32)
        sqs[...] = jnp.zeros((HB, CW), F32)

        def project(k, carry):
            @pl.when(k > 0)
            def _():
                cbx(h, k, frm(k), frm(k)).wait_recv()

            b = frm(k)
            piece = comb_r[b, rows, :]
            acc[...] += mm(piece, wbuf[b])
            value = piece.astype(F32)
            sqs[...] += value * value * gall[b, 0:1, :]
            return carry

        lax.fori_loop(0, NJ, project, 0)
        scale = lax.rsqrt(jnp.sum(sqs[...], axis=1, keepdims=True) / D + EPS)
        for q in range(GROUP):
            obs[q, rows, :] = (acc[:, q * CW:(q + 1) * CW] * scale).astype(BF16)
        for k in range(1, GROUP):
            obx(h, k, yy, lax.rem(yy + k, GROUP)).start()
    def place_out(n, src, s, h, size):
        rows = pl.ds(pl.multiple_of(s * RB + h * HB, 16), size)
        return pltpu.make_async_copy(src, out_ref.at[rows, :], oc.at[n])

    outs = [place_out(0, obs.at[yy], yy, 0, RB)]
    outs[0].start()
    for h in range(2):
        for k in range(1, GROUP):
            s = lax.rem(yy + GROUP - k, GROUP)
            obx(h, k, s, s).wait_recv()
            outs.append(
                place_out(h * GROUP + k, obr.at[s, pl.ds(h * HB, HB), :], s, h, HB)
            )
            outs[-1].start()
    for h in outs:
        h.wait()

    slab_pre.wait_send()
    slab_post.wait_send()
    for h in halo:
        h.wait_send()
    for g in gains:
        g.wait_send()
    for k in range(1, NJ):
        xa(k, to(k)).wait_send()
        dtx(k, j, to(k)).wait_send()
        if k <= GROUP:
            bbx(k, j, to(k)).wait_send()
        else:
            relay(k - GROUP, to(GROUP), to(k - GROUP)).wait_send()
        ccx(k, j, to(k)).wait_send()
        wx(k, j, to(k)).wait_send()
        for h in range(2):
            cbx(h, k, j, to(k)).wait_send()

    for k in range(1, ZC):
        zx(k, zi, zto(k)).wait_send()
        zy(k, zi, zto(k)).wait_send()
    if XL > 1:
        cross.wait_send()
    halves.wait_send()
    share.wait_send()
    for d in range(ZC // 2):
        up_ring(d, zfrm(d)).wait_send()
    for d in range(ZC // 2):
        down_ring(d, zto(d)).wait_send()
    for h in range(2):
        for k in range(1, GROUP):
            obx(h, k, yy, lax.rem(yy + k, GROUP)).wait_send()


def shards(x_in, conv_weight, proj_weight, dt_bias, decay_log, skip_gain, norm_gain, out_weight):
    T, CW = x_in.shape
    D = conv_weight.shape[1]
    H = dt_bias.shape[0]
    N = (proj_weight.shape[1] - H) // 2
    NC, NJ = lax.axis_size("ctx"), lax.axis_size("chan")
    HL = H // NJ
    SR = T // NJ
    XL = 2 if NC >= 4 else 1
    ZC = NC // (2 * XL)
    PR, LB = N // 2 // ZC, 2 * CW // 128
    RB, WC = T // GROUP, GROUP * CW
    dma = pltpu.SemaphoreType.DMA
    vm = pltpu.VMEM
    scratch = [
        vm((T + 32, CW), BF16), vm((NJ, SR + 64, CW), BF16), vm((SR + 32, CW), F32),
        vm((4, D), F32), vm((T, CW), BF16), vm((T, CW), BF16),
        vm((NJ, SR, 2 * N), BF16), vm((NJ, SR, 2 * N), BF16),
        vm((NJ, 2 * HL, SR), F32), vm((NJ, 2 * HL, SR), F32),
        vm((NJ, 2 * HL, SR), F32),
        vm((NJ, N, 2 * CW), F32), vm((NJ, 8, 2 * CW), F32), vm((T, CW), F32),
        vm((SR, HL * SR), BF16), vm((HL * SR, CW), BF16), vm((6 * HL, 2 * CW), BF16),
        vm((ZC, LB * PR + 16, 128), BF16), vm((ZC, LB * PR + 16, 128), BF16),
        vm((ZC, LB * PR, 128), BF16), vm((ZC, LB * PR, 128), BF16),
        vm((LB * PR, 128), F32), vm((LB * PR, 128), F32),
        vm((N, 2 * CW), F32), vm((N, 2 * CW), F32), vm((8, 2 * CW), F32), vm((8, 2 * CW), F32),
        vm((N, 2 * CW), F32),
        vm((T, CW), BF16), vm((NJ, RB, CW), BF16), vm((NJ, 8, CW), F32),
        vm((NJ, CW, WC), BF16), vm((RB // 2, WC), F32),
        vm((GROUP, RB, CW), BF16), vm((GROUP, RB, CW), BF16),
        vm((RB // 2, CW), F32), vm((NJ, SR, 2 * CW), F32), vm((NJ, N, 2 * CW), BF16),
        dma((NJ,)), dma((NJ,)), dma((4,)), dma((2 + NJ,)), dma((NJ,)), dma((NJ,)),
        dma((NJ,)), dma((NJ,)), dma((4,)), dma((4,)), dma((4,)), dma((4,)),
        dma((NJ,)), dma((NJ,)), dma((NJ,)), dma((NJ,)), dma((NJ,)), dma((NJ,)),
        dma((ZC,)), dma((ZC,)), dma((ZC,)), dma((ZC,)), dma((5,)), dma((5,)),
        dma((2, NJ)), dma((2, NJ)), dma((2, GROUP)), dma((2, GROUP)),
        vm(proj_weight.shape, BF16), vm(proj_weight.shape, BF16),
        vm(proj_weight.shape[::-1], BF16), vm((3, H, 128), F32), dma((9,)),
        vm((4, D), F32), vm((1, H), F32), vm((1, H), F32), vm((1, H), F32), vm((1, CW), F32), dma((2 * GROUP,)),
    ]
    return pl.pallas_call(
        functools.partial(kernel, (NC, NJ, T, CW, D, N, HL, XL, ZC)),
        out_shape=jax.ShapeDtypeStruct((T, CW), BF16),
        in_specs=[pl.BlockSpec(memory_space=pl.ANY)] * 8,
        out_specs=pl.BlockSpec(memory_space=pl.ANY),
        scratch_shapes=scratch,
        compiler_params=pltpu.CompilerParams(
            collective_id=0, has_side_effects=True, vmem_limit_bytes=62 * 1024 * 1024
        ),
        cost_estimate=pl.CostEstimate(
            flops=4 * T * D * CW, bytes_accessed=8 * T * CW, transcendentals=16 * T * SR
        ),
    )(
        x_in, conv_weight, proj_weight.T, dt_bias[None], decay_log[None], skip_gain[None],
        norm_gain[None], out_weight,
    )


def solution(mesh):
    in_specs = (P("ctx", "chan"), P(), P(), P(), P(), P(), P("chan"), P("chan", None))
    out_specs = P("ctx", "chan")
    return jax.shard_map(shards, mesh=mesh, in_specs=in_specs, out_specs=out_specs, check_vma=False)
```

```python
import functools

import jax
import jax.numpy as jnp
from jax import lax
from jax.experimental import pallas as pl
from jax.experimental.pallas import tpu as pltpu
from jax.sharding import PartitionSpec as P

F32 = jnp.float32
BF16 = jnp.bfloat16
MESH = pl.DeviceIdType.MESH
EPS = 1e-05
GROUP = 4


def mm(a, b, dims=((1,), (0,)), **kw):
    return lax.dot_general(a, b, (dims, ((), ())), preferred_element_type=F32, **kw)


def silu(v):
    return v / (1.0 + jnp.exp(-v))


def iota(shape, axis):
    return lax.broadcasted_iota(jnp.int32, shape, axis)


def kernel(
    dims,
    x_ref, cw_hbm, pw_ref, bias_hbm, decay_hbm, skip_hbm, gain_hbm, w_ref, out_ref,
    xpad, xe, cbuf, cwr, xf, xr, bb, cc, dtout, dtin, cumr, fresh, dch, yacc,
    mcat, xbd, emat, zs, zr, es, er, xs_, xr_, st_o, ech, dec_me, dec_o, stin, comb_s, comb_r, gall, wbuf, acc, obs, obr, sqs, grown, sbs,
    xa_s, xa_r, ha_s, ha_r, g_s, g_r, w_s, w_r, up_s, up_r, dn_s, dn_r, bb_s, bb_r, cc_s, cc_r, dt_s, dt_r,
    zx_s, zx_r, zy_s, zy_r, sb_s, sb_r, cb_s, cb_r, ob_s, ob_r, pwv, pwr, pwt, prm, lc,
    cw_ref, bias_ref, decay_ref, skip_ref, gain_ref, oc,
):
    NC, NJ, T, CW, D, N, HL, XL, ZC = dims
    SR = T // NJ
    PR = N // 2 // ZC
    LB = 2 * CW // 128
    WR = CW // 2 // ZC
    RB = T // GROUP
    WC = GROUP * CW
    i = lax.axis_index("ctx")
    j = lax.axis_index("chan")
    prev_i = lax.rem(i + NC - 1, NC)
    next_i = lax.rem(i + 1, NC)
    core = lax.rem(i, 2)
    sib = i + 1 - 2 * core
    xlo = i // (2 * ZC)
    zi = lax.rem(i // 2, ZC)
    xh = j // GROUP
    yy = lax.rem(j, GROUP)

    def at(ci, cj):
        return {"ctx": ci, "chan": cj}

    def to(k):
        return lax.rem(xh + k // GROUP, 2) * GROUP + lax.rem(yy + lax.rem(k, GROUP), GROUP)

    def frm(k):
        return (
            lax.rem(xh + k // GROUP, 2) * GROUP
            + lax.rem(yy + GROUP - lax.rem(k, GROUP), GROUP)
        )

    far_first = (6, 5, 7, 4, 2, 1, 3)

    def rcopy(src, dst, ss, rs, dev):
        return pltpu.make_async_remote_copy(
            src_ref=src, dst_ref=dst, send_sem=ss, recv_sem=rs, device_id=dev, device_id_type=MESH
        )

    def win(jd):
        return pl.multiple_of(jnp.clip(SR * jd - 16, 0, T - SR - 32), 16)

    def wrows(z):
        return pl.ds(pl.multiple_of(core * (CW // 2) + z * WR, 16), WR)

    own_wide = pl.ds(pl.multiple_of(xh * WC, 128), WC)
    here = [
        pltpu.make_async_copy(x_ref, xpad.at[pl.ds(16, T), :], lc.at[0]),
        pltpu.make_async_copy(
            x_ref.at[pl.ds(win(j), SR + 32), :], xe.at[j, pl.ds(16, SR + 32), :], lc.at[1]
        ),
        pltpu.make_async_copy(pw_ref, pwt, lc.at[2]),
        pltpu.make_async_copy(
            w_ref.at[wrows(zi), own_wide], wbuf.at[j, wrows(zi), :], lc.at[3]
        ),
    ]
    small = [
        pltpu.make_async_copy(src, dst, lc.at[4 + q])
        for q, (src, dst) in enumerate((
            (cw_hbm, cw_ref), (bias_hbm, bias_ref), (decay_hbm, decay_ref),
            (skip_hbm, skip_ref), (gain_hbm, gain_ref),
        ))
    ]
    for h in small + here:
        h.start()

    barrier = pltpu.get_barrier_semaphore()

    def hail(dev):
        pl.semaphore_signal(barrier, inc=1, device_id=dev, device_id_type=MESH)

    for k in range(1, NJ):
        hail(at(i, to(k)))

    def zpos(z):
        return xlo * (2 * ZC) + z * 2 + core

    def zto(k):
        return lax.rem(zi + k, ZC)

    def zfrm(k):
        return lax.rem(zi + ZC - k, ZC)

    for k in range(1, ZC):
        hail(at(zpos(zto(k)), j))
    across = lax.rem(i + 2 * ZC, NC)
    if XL > 1:
        hail(at(across, j))
    for c in (sib, prev_i, next_i):
        hail(at(c, j))

    @pl.when(j == 0)
    def _():
        for q in range(NJ):
            hail(at(prev_i, q))

    @pl.when(j == NJ - 1)
    def _():
        for q in range(NJ):
            hail(at(next_i, q))

    for h in small:
        h.wait()
    gall[j] = jnp.broadcast_to(1.0 / (gain_ref[...] * gain_ref[...]), (8, CW))
    heads = HL * NJ
    eye = iota((heads, heads), 0) == iota((heads, heads), 1)
    for q, ref in enumerate((bias_ref, decay_ref, skip_ref)):
        row = jnp.broadcast_to(ref[...], (heads, heads))
        column = jnp.sum(jnp.where(eye, row, 0.0), axis=1, keepdims=True)
        prm[q] = jnp.broadcast_to(column, (heads, 128))
    anti = iota((CW, CW), 0) + iota((CW, CW), 1) == CW - 1
    anti_f = jnp.where(anti, 1.0, 0.0).astype(F32)
    anti_b = anti_f.astype(BF16)
    for b in range(NJ):
        cwr[:, b * CW:(b + 1) * CW] = mm(
            cw_ref[:, (NJ - 1 - b) * CW:(NJ - b) * CW], anti_f, precision=lax.Precision.HIGHEST
        )
    head_row = lax.rem(iota((6 * HL, 2 * CW), 0), 2 * HL)
    ec = iota((6 * HL, 2 * CW), 1)
    head_of = ec // (CW // HL)
    target = jnp.where(head_of < HL, head_of, 3 * HL - 1 - head_of)
    emat[...] = jnp.where(head_row == target, 1.0, 0.0).astype(BF16)

    def terms(rows):
        hi = rows.astype(BF16)
        rest = rows - hi.astype(F32)
        mid = rest.astype(BF16)
        low = (rest - mid.astype(F32)).astype(BF16)
        return jnp.concatenate([hi, mid, low], axis=0)

    def expand(rows):
        return mm(terms(rows), emat[...], ((0,), (0,)))

    pl.semaphore_wait(barrier, NJ - 1 + ZC - 1 + XL - 1 + 3 + 2)

    def xa(k, jd):
        return rcopy(
            x_ref.at[pl.ds(win(jd), SR + 32), :], xe.at[j, pl.ds(16, SR + 32), :],
            xa_s.at[k], xa_r.at[k], at(i, jd),
        )

    def xa_in(k):
        return rcopy(
            x_ref.at[pl.ds(0, SR + 32), :], xe.at[frm(k), pl.ds(16, SR + 32), :],
            xa_s.at[k], xa_r.at[k], at(i, frm(k)),
        )

    lastrows, firstrows = x_ref.at[pl.ds(T - 16, 16), :], x_ref.at[pl.ds(0, 16), :]
    halo = [
        rcopy(lastrows, xpad.at[pl.ds(0, 16), :], ha_s.at[0], ha_r.at[0], at(next_i, j)),
        rcopy(firstrows, xpad.at[pl.ds(16 + T, 16), :], ha_s.at[1], ha_r.at[1], at(prev_i, j)),
    ]
    slab_pre = rcopy(
        lastrows, xe.at[j, pl.ds(0, 16), :], ha_s.at[2], ha_r.at[2 + j], at(next_i, 0)
    )
    slab_post = rcopy(
        firstrows, xe.at[j, pl.ds(SR + 48, 16), :], ha_s.at[3], ha_r.at[2 + j], at(prev_i, NJ - 1)
    )
    slab_pre.start()
    slab_post.start()
    for k in far_first:
        xa(k, to(k)).start()
    def wx(k, slot, dev):
        cols = pl.ds(pl.multiple_of((dev // GROUP) * WC, 128), WC)
        return rcopy(
            w_ref.at[wrows(zi), cols], wbuf.at[slot, wrows(zi), :], w_s.at[k], w_r.at[k],
            at(i, dev),
        )

    def wrelay(k, slot, dev):
        part = wbuf.at[slot, wrows(zi), :]
        return rcopy(part, part, w_s.at[GROUP + k], w_r.at[GROUP + k], at(i, dev))

    def halfway(d):
        return ZC % 2 == 0 and d == ZC // 2 - 1

    def up_ring(d, z):
        part = wbuf.at[pl.ds(0, NJ // 2 if halfway(d) else NJ), wrows(z), :]
        return rcopy(part, part, up_s.at[d], up_r.at[d], at(zpos(zto(1)), j))

    def down_ring(d, z):
        first = NJ // 2 if halfway(d) else 0
        part = wbuf.at[pl.ds(first, NJ - first), wrows(z), :]
        return rcopy(part, part, dn_s.at[d], dn_r.at[d], at(zpos(zfrm(1)), j))

    def ring_start(d):
        if d < ZC // 2:
            up_ring(d, zfrm(d)).start()
        if d < ZC // 2:
            down_ring(d, zto(d)).start()

    def ring_wait(d):
        if d < ZC // 2:
            up_ring(d, zfrm(d + 1)).wait_recv()
        if d < ZC // 2:
            down_ring(d, zto(d + 1)).wait_recv()

    for k in (GROUP, 2, 1, 3):
        wx(k, j, to(k)).start()
    for h in halo:
        h.start()
    gains = [
        rcopy(gall.at[j], gall.at[j], g_s.at[k], g_r.at[k], at(i, to(k))) for k in range(1, NJ)
    ]
    for g in gains:
        g.start()

    def conv_pair(taps, rtaps):
        vf = taps[0:1, :] * cbuf[13:13 + SR, :]
        vr = rtaps[0:1, :] * cbuf[19:19 + SR, :]
        for k in range(1, 4):
            vf = vf + taps[k:k + 1, :] * cbuf[13 + k:13 + k + SR, :]
            vr = vr + rtaps[k:k + 1, :] * cbuf[19 - k:19 - k + SR, :]
        return silu(vf).astype(BF16), silu(vr).astype(BF16)

    here[2].wait()
    for b in range(NJ):
        block = pwt[:, b * CW:(b + 1) * CW].T
        pwv[b * CW:(b + 1) * CW, :] = block
        pwr[(NJ - 1 - b) * CW:(NJ - b) * CW, :] = mm(anti_b, block).astype(BF16)

    own_cols = pl.ds(pl.multiple_of(j * CW, 128), CW)

    def own_conv(c, carry):
        rows = pl.ds(pl.multiple_of(c * SR, 16), SR)
        cbuf[...] = xpad[pl.ds(pl.multiple_of(c * SR, 16), SR + 32), :].astype(F32)
        f, r = conv_pair(cw_ref[:, own_cols], cwr[:, own_cols])
        xf[rows, :] = f
        xr[rows, :] = r
        return carry

    here[0].wait()
    lax.fori_loop(1, NJ - 1, own_conv, 0)

    @pl.when(j == 0)
    def _():
        for q in range(NJ):
            rcopy(
                lastrows, xe.at[q, pl.ds(0, 16), :], ha_s.at[2], ha_r.at[2 + q], at(prev_i, q)
            ).wait_recv()

    @pl.when(j == NJ - 1)
    def _():
        for q in range(NJ):
            rcopy(
                firstrows, xe.at[q, pl.ds(SR + 48, 16), :], ha_s.at[3], ha_r.at[2 + q],
                at(next_i, q),
            ).wait_recv()

    @pl.when(jnp.logical_and(i == 0, j == 0))
    def _():
        for q in range(NJ):
            xe[q, 0:16, :] = jnp.zeros((16, CW), BF16)

    @pl.when(jnp.logical_and(i == NC - 1, j == NJ - 1))
    def _():
        for q in range(NJ):
            xe[q, SR + 48:SR + 64, :] = jnp.zeros((16, CW), BF16)

    start = pl.multiple_of(SR * j - win(j), 16)
    here[1].wait()

    def slab(k, carry):
        pf, pr = carry

        @pl.when(k == GROUP)
        def _():
            wx(GROUP, frm(GROUP), frm(GROUP)).wait_recv()
            for q in (2, 1, 3):
                wrelay(q, to(GROUP), to(q)).start()

        @pl.when(k > 0)
        def _():
            xa_in(k).wait_recv()

        b = frm(k)
        cols = pl.ds(pl.multiple_of(b * CW, 128), CW)
        cbuf[...] = xe[b, pl.ds(start, SR + 32), :].astype(F32)
        f, r = conv_pair(cw_ref[:, cols], cwr[:, cols])
        pf = pf + mm(f, pwv[cols, :])
        pr = pr + mm(r, pwr[cols, :])
        return pf, pr

    wide = pwv.shape[1]
    pf, pr = lax.fori_loop(
        0, NJ, slab, (jnp.zeros((SR, wide), F32), jnp.zeros((SR, wide), F32))
    )
    def bbx(k, slot, dev):
        return rcopy(bb.at[slot], bb.at[slot], bb_s.at[k], bb_r.at[k], at(i, dev))

    def relay(k, slot, dev):
        return rcopy(bb.at[slot], bb.at[slot], bb_s.at[GROUP + k], bb_r.at[GROUP + k], at(i, dev))

    def ccx(k, slot, dev):
        return rcopy(cc.at[slot], cc.at[slot], cc_s.at[k], cc_r.at[k], at(i, dev))

    def dtx(k, slot, dev):
        return rcopy(dtout.at[dev], dtin.at[slot], dt_s.at[k], dt_r.at[k], at(i, dev))

    bb[j, :, 0:N] = pf[:, 0:N].astype(BF16)
    bb[j, :, N:2 * N] = pr[:, 0:N].astype(BF16)
    for k in (GROUP, 2, 1, 3):
        bbx(k, j, to(k)).start()
    raw = jnp.concatenate([pf[:, 2 * N:], pr[:, 2 * N:]], axis=1).T
    bias = jnp.concatenate([prm[0], prm[0]], axis=0)
    v = raw + bias
    dts = jnp.maximum(v, 0.0) + jnp.log1p(jnp.exp(-jnp.abs(v)))
    for q in range(NJ):
        dtout[q, 0:HL, :] = dts[q * HL:(q + 1) * HL, :]
        dtout[q, HL:2 * HL, :] = dts[heads + (NJ - 1 - q) * HL:heads + (NJ - q) * HL, :]
    for k in far_first:
        dtx(k, j, to(k)).start()
    dtin[j] = dtout[j]
    cc[j, :, 0:N] = pf[:, N:2 * N].astype(BF16)
    cc[j, :, N:2 * N] = pr[:, N:2 * N].astype(BF16)

    for h in halo:
        h.wait_recv()

    @pl.when(i == 0)
    def _():
        xpad[0:16, :] = jnp.zeros((16, CW), BF16)

    @pl.when(i == NC - 1)
    def _():
        xpad[16 + T:32 + T, :] = jnp.zeros((16, CW), BF16)

    own_conv(0, 0)
    own_conv(NJ - 1, 0)

    for k in range(1, GROUP):
        wx(k, frm(k), frm(k)).wait_recv()
        wrelay(k, frm(GROUP + k), frm(k)).wait_recv()
    here[3].wait()
    ring_start(0)

    bbx(GROUP, frm(GROUP), frm(GROUP)).wait_recv()
    for k in (2, 1, 3):
        relay(k, to(GROUP), to(k)).start()

    own = pl.ds(pl.multiple_of(j * HL, 8), HL)
    mirror = pl.ds(pl.multiple_of((NJ - 1 - j) * HL, 8), HL)

    def own_rows(which):
        return jnp.concatenate([prm[which, own, :], prm[which, mirror, :]], axis=0)

    rate = -jnp.exp(own_rows(1))
    src, dst = iota((SR, 2 * SR), 0), iota((SR, 2 * SR), 1)
    sums = jnp.where(dst < SR, dst - src, src - dst + SR) >= 0
    sums = jnp.where(sums, 1.0, 0.0).astype(BF16)
    is_fwd = iota((2 * HL, SR), 0) < HL
    chunk_lane = iota((2 * HL, SR), 1)

    def states(k, ends):
        c = frm(k)

        @pl.when(k > 0)
        def _():
            dtx(k, c, c).wait_recv()

        @pl.when(jnp.logical_and(k > 0, k < GROUP))
        def _():
            bbx(k, c, c).wait_recv()

        @pl.when(k > GROUP)
        def _():
            relay(k - GROUP, c, c).wait_recv()

        @pl.when(k == GROUP + 2)
        def _():
            ring_wait(0)
            ring_start(1)

        @pl.when(k == 1)
        def _():
            for q in range(1, GROUP):
                ccx(q, j, to(q)).start()

        @pl.when(k == GROUP + 1)
        def _():
            for q in range(GROUP, NJ):
                ccx(q, j, to(q)).start()

        rows = pl.ds(pl.multiple_of(c * SR, 16), SR)
        dt = dtin[c]
        a = dt * rate
        run = mm(terms(a), sums)
        run = run[0:2 * HL] + run[2 * HL:4 * HL] + run[4 * HL:6 * HL]
        cum = jnp.where(is_fwd, run[:, 0:SR], run[:, SR:2 * SR])
        end = jnp.sum(a, axis=1, keepdims=True)
        cumr[c] = cum
        tail = expand(jnp.exp(end - cum) * dt)
        tf = (xf[rows, :].astype(F32) * tail[:, 0:CW]).astype(BF16)
        tr = (xr[rows, :].astype(F32) * tail[:, CW:2 * CW]).astype(BF16)
        fresh[c, :, 0:CW] = mm(bb[c, :, 0:N], tf, ((0,), (0,)))
        fresh[c, :, CW:2 * CW] = mm(bb[c, :, N:2 * N], tr, ((0,), (0,)))
        return jnp.where(chunk_lane == c, end, ends)

    ends = lax.fori_loop(0, NJ, states, jnp.zeros((2 * HL, SR), F32))
    ends = jnp.where(chunk_lane == NJ, jnp.sum(ends, axis=1, keepdims=True), ends)
    whole = expand(jnp.exp(ends))
    for c in range(NJ):
        dch[c] = jnp.broadcast_to(whole[c:c + 1, :], (8, 2 * CW))
    dec_me[...] = jnp.broadcast_to(whole[NJ:NJ + 1, :], (8, 2 * CW))

    stin[...] = jnp.zeros((N, 2 * CW), F32)

    def fold(c, carry):
        r = NJ - 1 - c
        stin[:, 0:CW] = dch[c, 0:1, 0:CW] * stin[:, 0:CW] + fresh[c, :, 0:CW]
        stin[:, CW:2 * CW] = (
            dch[r, 0:1, CW:2 * CW] * stin[:, CW:2 * CW] + fresh[r, :, CW:2 * CW]
        )
        return carry

    lax.fori_loop(0, NJ, fold, 0)

    swap = [
        rcopy(stin, st_o, sb_s.at[0], sb_r.at[0], at(sib, j)),
        rcopy(dec_me, dec_o, sb_s.at[1], sb_r.at[1], at(sib, j)),
    ]
    for h in swap:
        h.start()
    for h in swap:
        h.wait_recv()
    mine = pl.ds(pl.multiple_of(core * (N // 2), 8), N // 2)
    s_me, s_o = stin[mine, :], st_o[mine, :]
    d_me, d_o = dec_me[0:1, :], dec_o[0:1, :]
    fwd_lane = jnp.where(iota((8, 2 * CW), 1) < CW, 1, 0)[0:1, :]
    other_last = fwd_lane == 1 - core
    pair = jnp.where(other_last, d_o * s_me + s_o, d_me * s_o + s_me)
    d_pair = jnp.broadcast_to(d_me * d_o, (8, 2 * CW))
    place = iota((16, 128), 0)
    d_tile = jnp.zeros((16, 128), F32)
    for q in range(LB):
        d = d_pair[:, q * 128:(q + 1) * 128][0:1, :]
        hi = d.astype(BF16).astype(F32)
        mid = (d - hi).astype(BF16).astype(F32)
        for t, term in enumerate((hi, mid, d - hi - mid)):
            d_tile = jnp.where(place == t * LB + q, term, d_tile)
    d_tile = d_tile.astype(BF16)
    for p in range(ZC):
        blocks = [pair[p * PR:(p + 1) * PR, q * 128:(q + 1) * 128] for q in range(LB)]
        zs[p, 0:LB * PR, :] = jnp.concatenate(blocks, axis=0).astype(BF16)
        zs[p, LB * PR:LB * PR + 16, :] = d_tile
    zr[zi] = zs[zi]

    def zx(k, slot, z):
        return rcopy(zs.at[z], zr.at[slot], zx_s.at[k], zx_r.at[k], at(zpos(z), j))

    def zy(k, slot, z):
        return rcopy(es.at[z], er.at[slot], zy_s.at[k], zy_r.at[k], at(zpos(z), j))

    for k in range(1, ZC):
        zx(k, zi, zto(k)).start()

    low = iota((SR, SR), 0) >= iota((SR, SR), 1)
    upp = iota((SR, SR), 0) <= iota((SR, SR), 1)
    lane_head = iota((8, CW), 1) // (CW // HL)
    skips = expand(own_rows(2))[0:8, :]

    def inner(k, carry):
        c = frm(k)

        @pl.when(k > 0)
        def _():
            ccx(k, c, c).wait_recv()

        rows = pl.ds(pl.multiple_of(c * SR, 16), SR)
        cum = cumr[c]
        cols = jnp.concatenate([cum, jnp.zeros((SR - 2 * HL, SR), F32)], axis=0).T
        lds = cum - jnp.log(dtin[c])
        y = jnp.zeros((SR, CW), F32)
        for d, (xs, mask) in enumerate(((xf, low), (xr, upp))):
            xv = xs[rows, :]
            part = slice(d * N, (d + 1) * N)
            score = mm(cc[c, :, part], bb[c, :, part], ((1,), (1,)))
            for q in range(HL):
                row = q if d == 0 else 2 * HL - 1 - q
                seg = jnp.where(mask, cols[:, row:row + 1] - lds[row:row + 1, :], -1e30)
                mcat[:, q * SR:(q + 1) * SR] = (score * jnp.exp(seg)).astype(BF16)
                keep = jnp.where(lane_head == q, 1.0, 0.0)[0:1, :].astype(BF16)
                xbd[q * SR:(q + 1) * SR, :] = xv * keep
            y = y + mm(mcat[...], xbd[...])
            y = y + skips[0:1, d * CW:(d + 1) * CW] * xv.astype(F32)
        yacc[rows, :] = y
        grown[c] = expand(jnp.exp(cum))
        return carry

    lax.fori_loop(0, 3, inner, 0)

    for k in range(1, ZC):
        zx(k, zfrm(k), zfrm(k)).wait_recv()

    pieces, decays = [], []
    for z in range(ZC):
        whole = zr[z].astype(F32)
        pieces.append(whole[0:LB * PR])
        tile = whole[LB * PR:LB * PR + 16]
        decays.append([
            tile[q:q + 1] + tile[LB + q:LB + q + 1] + tile[2 * LB + q:2 * LB + q + 1]
            for q in range(LB)
        ])

    def chain(q, e):
        order = range(ZC) if q < LB // 2 else range(ZC - 1, -1, -1)
        before = [None] * ZC
        for z in order:
            before[z] = e
            e = decays[z][q] * e + pieces[z][q * PR:(q + 1) * PR]
        return before, e

    zero = jnp.zeros((PR, 128), F32)
    if XL > 1:
        for q in range(LB):
            xs_[q * PR:(q + 1) * PR, :] = chain(q, zero)[1]
        cross = rcopy(xs_, xr_, sb_s.at[2], sb_r.at[2], at(across, j))
        cross.start()
        lax.fori_loop(3, 4, inner, 0)
        cross.wait_recv()
    before = []
    for q in range(LB):
        start_from = zero
        if XL > 1:
            takes = xlo == 1 if q < LB // 2 else xlo == 0
            start_from = jnp.where(takes, xr_[q * PR:(q + 1) * PR, :], 0.0)
        before.append(chain(q, start_from)[0])
    for z in range(ZC):
        es[z] = jnp.concatenate([before[q][z] for q in range(LB)], axis=0).astype(BF16)
    er[zi] = es[zi]
    for k in range(1, ZC):
        zy(k, zi, zto(k)).start()
    lax.fori_loop(4 if XL > 1 else 3, NJ, inner, 0)
    for k in range(1, ZC):
        zy(k, zfrm(k), zfrm(k)).wait_recv()
    ring_wait(1)
    ring_start(2)
    for p in range(ZC):
        piece = er[p].astype(F32)
        for q in range(LB):
            ech[pl.ds(pl.multiple_of(core * (N // 2) + p * PR, 8), PR), q * 128:(q + 1) * 128] = (
                piece[q * PR:(q + 1) * PR, :]
            )
    halves = rcopy(ech.at[mine, :], ech.at[mine, :], sb_s.at[3], sb_r.at[3], at(sib, j))
    halves.start()
    for h in swap:
        h.wait_send()
    theirs = pl.ds(pl.multiple_of((1 - core) * (N // 2), 8), N // 2)
    rcopy(ech.at[theirs, :], ech.at[theirs, :], sb_s.at[3], sb_r.at[3], at(sib, j)).wait_recv()
    other_first = fwd_lane == core
    stin[...] = jnp.where(other_first, dec_o[0:1, :] * ech[...] + st_o[...], ech[...])

    def enter(s, carry):
        for d in range(2):
            c = s if d == 0 else NJ - 1 - s
            lanes = slice(d * CW, (d + 1) * CW)
            st = stin[:, lanes]
            sbs[c, :, lanes] = st.astype(BF16)
            stin[:, lanes] = dch[c, 0:1, lanes] * st + fresh[c, :, lanes]
        return carry

    lax.fori_loop(0, NJ, enter, 0)

    HB = RB // 2

    def cbx(h, k, slot, dev):
        rows = pl.ds(pl.multiple_of(lax.rem(dev, GROUP) * RB + h * HB, 16), HB)
        return rcopy(
            comb_s.at[rows, :], comb_r.at[slot, pl.ds(h * HB, HB), :],
            cb_s.at[h, k], cb_r.at[h, k], at(i, dev),
        )

    chunks = HB // SR
    for h in range(2):

        def finish(n, carry):
            c = (n // chunks) * (2 * chunks) + h * chunks + lax.rem(n, chunks)
            rows = pl.ds(pl.multiple_of(c * SR, 16), SR)
            y = yacc[rows, :]
            for d in range(2):
                lanes = slice(d * CW, (d + 1) * CW)
                z = mm(cc[c, :, d * N:(d + 1) * N], sbs[c, :, lanes])
                y = y + grown[c, :, lanes] * z
            comb_s[rows, :] = (y * gain_ref[...]).astype(BF16)
            return carry

        lax.fori_loop(0, NJ // 2, finish, 0)
        for k in far_first:
            cbx(h, k, j, to(k)).start()
    comb_r[j] = comb_s[pl.ds(pl.multiple_of(yy * RB, 16), RB), :]
    ring_wait(2)
    ring_start(3)
    ring_wait(3)
    half = pl.ds(pl.multiple_of(core * (CW // 2), 16), CW // 2)
    rest = pl.ds(pl.multiple_of((1 - core) * (CW // 2), 16), CW // 2)
    share = rcopy(wbuf.at[:, half, :], wbuf.at[:, half, :], sb_s.at[4], sb_r.at[4], at(sib, j))
    share.start()
    for k in range(1, NJ):
        s = frm(k)
        rcopy(gall.at[s], gall.at[s], g_s.at[k], g_r.at[k], at(i, s)).wait_recv()
    rcopy(
        wbuf.at[:, rest, :], wbuf.at[:, rest, :], sb_s.at[4], sb_r.at[4], at(sib, j)
    ).wait_recv()

    def obx(h, k, slot, dest):
        rows = pl.ds(h * HB, HB)
        return rcopy(
            obs.at[dest, rows, :], obr.at[slot, rows, :], ob_s.at[h, k], ob_r.at[h, k],
            at(i, xh * GROUP + dest),
        )

    for h in range(2):
        rows = slice(h * HB, (h + 1) * HB)
        acc[...] = jnp.zeros((HB, WC), F32)
        sqs[...] = jnp.zeros((HB, CW), F32)

        def project(k, carry):
            @pl.when(k > 0)
            def _():
                cbx(h, k, frm(k), frm(k)).wait_recv()

            b = frm(k)
            piece = comb_r[b, rows, :]
            acc[...] += mm(piece, wbuf[b])
            value = piece.astype(F32)
            sqs[...] += value * value * gall[b, 0:1, :]
            return carry

        lax.fori_loop(0, NJ, project, 0)
        scale = lax.rsqrt(jnp.sum(sqs[...], axis=1, keepdims=True) / D + EPS)
        for q in range(GROUP):
            obs[q, rows, :] = (acc[:, q * CW:(q + 1) * CW] * scale).astype(BF16)
        for k in range(1, GROUP):
            obx(h, k, yy, lax.rem(yy + k, GROUP)).start()
    def place_out(n, src, s, h, size):
        rows = pl.ds(pl.multiple_of(s * RB + h * HB, 16), size)
        return pltpu.make_async_copy(src, out_ref.at[rows, :], oc.at[n])

    outs = [place_out(0, obs.at[yy], yy, 0, RB)]
    outs[0].start()
    for h in range(2):
        for k in range(1, GROUP):
            s = lax.rem(yy + GROUP - k, GROUP)
            obx(h, k, s, s).wait_recv()
            outs.append(
                place_out(h * GROUP + k, obr.at[s, pl.ds(h * HB, HB), :], s, h, HB)
            )
            outs[-1].start()
    for h in outs:
        h.wait()

    slab_pre.wait_send()
    slab_post.wait_send()
    for h in halo:
        h.wait_send()
    for g in gains:
        g.wait_send()
    for k in range(1, NJ):
        xa(k, to(k)).wait_send()
        dtx(k, j, to(k)).wait_send()
        if k <= GROUP:
            bbx(k, j, to(k)).wait_send()
        else:
            relay(k - GROUP, to(GROUP), to(k - GROUP)).wait_send()
        ccx(k, j, to(k)).wait_send()
        if k <= GROUP:
            wx(k, j, to(k)).wait_send()
        else:
            wrelay(k - GROUP, to(GROUP), to(k - GROUP)).wait_send()
        for h in range(2):
            cbx(h, k, j, to(k)).wait_send()

    for k in range(1, ZC):
        zx(k, zi, zto(k)).wait_send()
        zy(k, zi, zto(k)).wait_send()
    if XL > 1:
        cross.wait_send()
    halves.wait_send()
    share.wait_send()
    for d in range(ZC // 2):
        up_ring(d, zfrm(d)).wait_send()
    for d in range(ZC // 2):
        down_ring(d, zto(d)).wait_send()
    for h in range(2):
        for k in range(1, GROUP):
            obx(h, k, yy, lax.rem(yy + k, GROUP)).wait_send()


def shards(x_in, conv_weight, proj_weight, dt_bias, decay_log, skip_gain, norm_gain, out_weight):
    T, CW = x_in.shape
    D = conv_weight.shape[1]
    H = dt_bias.shape[0]
    N = (proj_weight.shape[1] - H) // 2
    NC, NJ = lax.axis_size("ctx"), lax.axis_size("chan")
    HL = H // NJ
    SR = T // NJ
    XL = 2 if NC >= 4 else 1
    ZC = NC // (2 * XL)
    PR, LB = N // 2 // ZC, 2 * CW // 128
    RB, WC = T // GROUP, GROUP * CW
    dma = pltpu.SemaphoreType.DMA
    vm = pltpu.VMEM
    scratch = [
        vm((T + 32, CW), BF16), vm((NJ, SR + 64, CW), BF16), vm((SR + 32, CW), F32),
        vm((4, D), F32), vm((T, CW), BF16), vm((T, CW), BF16),
        vm((NJ, SR, 2 * N), BF16), vm((NJ, SR, 2 * N), BF16),
        vm((NJ, 2 * HL, SR), F32), vm((NJ, 2 * HL, SR), F32),
        vm((NJ, 2 * HL, SR), F32),
        vm((NJ, N, 2 * CW), F32), vm((NJ, 8, 2 * CW), F32), vm((T, CW), F32),
        vm((SR, HL * SR), BF16), vm((HL * SR, CW), BF16), vm((6 * HL, 2 * CW), BF16),
        vm((ZC, LB * PR + 16, 128), BF16), vm((ZC, LB * PR + 16, 128), BF16),
        vm((ZC, LB * PR, 128), BF16), vm((ZC, LB * PR, 128), BF16),
        vm((LB * PR, 128), F32), vm((LB * PR, 128), F32),
        vm((N, 2 * CW), F32), vm((N, 2 * CW), F32), vm((8, 2 * CW), F32), vm((8, 2 * CW), F32),
        vm((N, 2 * CW), F32),
        vm((T, CW), BF16), vm((NJ, RB, CW), BF16), vm((NJ, 8, CW), F32),
        vm((NJ, CW, WC), BF16), vm((RB // 2, WC), F32),
        vm((GROUP, RB, CW), BF16), vm((GROUP, RB, CW), BF16),
        vm((RB // 2, CW), F32), vm((NJ, SR, 2 * CW), F32), vm((NJ, N, 2 * CW), BF16),
        dma((NJ,)), dma((NJ,)), dma((4,)), dma((2 + NJ,)), dma((NJ,)), dma((NJ,)),
        dma((NJ,)), dma((NJ,)), dma((4,)), dma((4,)), dma((4,)), dma((4,)),
        dma((NJ,)), dma((NJ,)), dma((NJ,)), dma((NJ,)), dma((NJ,)), dma((NJ,)),
        dma((ZC,)), dma((ZC,)), dma((ZC,)), dma((ZC,)), dma((5,)), dma((5,)),
        dma((2, NJ)), dma((2, NJ)), dma((2, GROUP)), dma((2, GROUP)),
        vm(proj_weight.shape, BF16), vm(proj_weight.shape, BF16),
        vm(proj_weight.shape[::-1], BF16), vm((3, H, 128), F32), dma((9,)),
        vm((4, D), F32), vm((1, H), F32), vm((1, H), F32), vm((1, H), F32), vm((1, CW), F32), dma((2 * GROUP,)),
    ]
    return pl.pallas_call(
        functools.partial(kernel, (NC, NJ, T, CW, D, N, HL, XL, ZC)),
        out_shape=jax.ShapeDtypeStruct((T, CW), BF16),
        in_specs=[pl.BlockSpec(memory_space=pl.ANY)] * 8,
        out_specs=pl.BlockSpec(memory_space=pl.ANY),
        scratch_shapes=scratch,
        compiler_params=pltpu.CompilerParams(
            collective_id=0, has_side_effects=True, vmem_limit_bytes=62 * 1024 * 1024
        ),
        cost_estimate=pl.CostEstimate(
            flops=4 * T * D * CW, bytes_accessed=8 * T * CW, transcendentals=16 * T * SR
        ),
    )(
        x_in, conv_weight, proj_weight.T, dt_bias[None], decay_log[None], skip_gain[None],
        norm_gain[None], out_weight,
    )


def solution(mesh):
    in_specs = (P("ctx", "chan"), P(), P(), P(), P(), P(), P("chan"), P("chan", None))
    out_specs = P("ctx", "chan")
    return jax.shard_map(shards, mesh=mesh, in_specs=in_specs, out_specs=out_specs, check_vma=False)
```

```python
import functools

import jax
import jax.numpy as jnp
from jax import lax
from jax.experimental import pallas as pl
from jax.experimental.pallas import tpu as pltpu
from jax.sharding import PartitionSpec as P

F32 = jnp.float32
BF16 = jnp.bfloat16
MESH = pl.DeviceIdType.MESH
EPS = 1e-05
GROUP = 4


def mm(a, b, dims=((1,), (0,)), **kw):
    return lax.dot_general(a, b, (dims, ((), ())), preferred_element_type=F32, **kw)


def silu(v):
    return v / (1.0 + jnp.exp(-v))


def iota(shape, axis):
    return lax.broadcasted_iota(jnp.int32, shape, axis)


def kernel(
    dims,
    x_ref, cw_hbm, pw_ref, bias_hbm, decay_hbm, skip_hbm, gain_hbm, w_ref, out_ref,
    xpad, xe, cbuf, cwr, xf, xr, bb, cc, dtout, dtin, cumr, fresh, dch, yacc,
    mcat, xbd, emat, zs, zr, es, er, xs_, xr_, st_o, ech, dec_me, dec_o, stin, comb_s, comb_r, gall, wbuf, acc, obs, obr, sqs, grown, sbs,
    xa_s, xa_r, ha_s, ha_r, g_s, g_r, w_s, w_r, up_s, up_r, dn_s, dn_r, bb_s, bb_r, cc_s, cc_r, dt_s, dt_r,
    zx_s, zx_r, zy_s, zy_r, sb_s, sb_r, cb_s, cb_r, ob_s, ob_r, pwv, pwr, pwt, prm, lc,
    cw_ref, bias_ref, decay_ref, skip_ref, gain_ref, oc,
):
    NC, NJ, T, CW, D, N, HL, XL, ZC = dims
    SR = T // NJ
    PR = N // 2 // ZC
    LB = 2 * CW // 128
    WR = CW // 2 // ZC
    RB = T // GROUP
    WC = GROUP * CW
    i = lax.axis_index("ctx")
    j = lax.axis_index("chan")
    prev_i = lax.rem(i + NC - 1, NC)
    next_i = lax.rem(i + 1, NC)
    core = lax.rem(i, 2)
    sib = i + 1 - 2 * core
    xlo = i // (2 * ZC)
    zi = lax.rem(i // 2, ZC)
    xh = j // GROUP
    yy = lax.rem(j, GROUP)

    def at(ci, cj):
        return {"ctx": ci, "chan": cj}

    def to(k):
        return lax.rem(xh + k // GROUP, 2) * GROUP + lax.rem(yy + lax.rem(k, GROUP), GROUP)

    def frm(k):
        return (
            lax.rem(xh + k // GROUP, 2) * GROUP
            + lax.rem(yy + GROUP - lax.rem(k, GROUP), GROUP)
        )

    far_first = (6, 5, 7, 4, 2, 1, 3)

    def rcopy(src, dst, ss, rs, dev):
        return pltpu.make_async_remote_copy(
            src_ref=src, dst_ref=dst, send_sem=ss, recv_sem=rs, device_id=dev, device_id_type=MESH
        )

    def win(jd):
        return pl.multiple_of(jnp.clip(SR * jd - 16, 0, T - SR - 32), 16)

    def wrows(z):
        return pl.ds(pl.multiple_of(core * (CW // 2) + z * WR, 16), WR)

    own_wide = pl.ds(pl.multiple_of(xh * WC, 128), WC)
    here = [
        pltpu.make_async_copy(x_ref, xpad.at[pl.ds(16, T), :], lc.at[0]),
        pltpu.make_async_copy(
            x_ref.at[pl.ds(win(j), SR + 32), :], xe.at[j, pl.ds(16, SR + 32), :], lc.at[1]
        ),
        pltpu.make_async_copy(pw_ref, pwt, lc.at[2]),
        pltpu.make_async_copy(
            w_ref.at[wrows(zi), own_wide], wbuf.at[j, wrows(zi), :], lc.at[3]
        ),
    ]
    small = [
        pltpu.make_async_copy(src, dst, lc.at[4 + q])
        for q, (src, dst) in enumerate((
            (cw_hbm, cw_ref), (bias_hbm, bias_ref), (decay_hbm, decay_ref),
            (skip_hbm, skip_ref), (gain_hbm, gain_ref),
        ))
    ]
    for h in small + here:
        h.start()

    barrier = pltpu.get_barrier_semaphore()

    def hail(dev):
        pl.semaphore_signal(barrier, inc=1, device_id=dev, device_id_type=MESH)

    for k in range(1, NJ):
        hail(at(i, to(k)))

    def zpos(z):
        return xlo * (2 * ZC) + z * 2 + core

    def zto(k):
        return lax.rem(zi + k, ZC)

    def zfrm(k):
        return lax.rem(zi + ZC - k, ZC)

    for k in range(1, ZC):
        hail(at(zpos(zto(k)), j))
    across = lax.rem(i + 2 * ZC, NC)
    if XL > 1:
        hail(at(across, j))
    for c in (sib, prev_i, next_i):
        hail(at(c, j))

    @pl.when(j == 0)
    def _():
        for q in range(NJ):
            hail(at(prev_i, q))

    @pl.when(j == NJ - 1)
    def _():
        for q in range(NJ):
            hail(at(next_i, q))

    for h in small:
        h.wait()
    gall[j] = jnp.broadcast_to(1.0 / (gain_ref[...] * gain_ref[...]), (8, CW))
    heads = HL * NJ
    eye = iota((heads, heads), 0) == iota((heads, heads), 1)
    for q, ref in enumerate((bias_ref, decay_ref, skip_ref)):
        row = jnp.broadcast_to(ref[...], (heads, heads))
        column = jnp.sum(jnp.where(eye, row, 0.0), axis=1, keepdims=True)
        prm[q] = jnp.broadcast_to(column, (heads, 128))
    anti = iota((CW, CW), 0) + iota((CW, CW), 1) == CW - 1
    anti_f = jnp.where(anti, 1.0, 0.0).astype(F32)
    anti_b = anti_f.astype(BF16)
    for b in range(NJ):
        cwr[:, b * CW:(b + 1) * CW] = mm(
            cw_ref[:, (NJ - 1 - b) * CW:(NJ - b) * CW], anti_f, precision=lax.Precision.HIGHEST
        )
    head_row = lax.rem(iota((6 * HL, 2 * CW), 0), 2 * HL)
    ec = iota((6 * HL, 2 * CW), 1)
    head_of = ec // (CW // HL)
    target = jnp.where(head_of < HL, head_of, 3 * HL - 1 - head_of)
    emat[...] = jnp.where(head_row == target, 1.0, 0.0).astype(BF16)

    def terms(rows):
        hi = rows.astype(BF16)
        rest = rows - hi.astype(F32)
        mid = rest.astype(BF16)
        low = (rest - mid.astype(F32)).astype(BF16)
        return jnp.concatenate([hi, mid, low], axis=0)

    def expand(rows):
        return mm(terms(rows), emat[...], ((0,), (0,)))

    pl.semaphore_wait(barrier, NJ - 1 + ZC - 1 + XL - 1 + 3 + 2)

    def xa(k, jd):
        return rcopy(
            x_ref.at[pl.ds(win(jd), SR + 32), :], xe.at[j, pl.ds(16, SR + 32), :],
            xa_s.at[k], xa_r.at[k], at(i, jd),
        )

    def xa_in(k):
        return rcopy(
            x_ref.at[pl.ds(0, SR + 32), :], xe.at[frm(k), pl.ds(16, SR + 32), :],
            xa_s.at[k], xa_r.at[k], at(i, frm(k)),
        )

    lastrows, firstrows = x_ref.at[pl.ds(T - 16, 16), :], x_ref.at[pl.ds(0, 16), :]
    halo = [
        rcopy(lastrows, xpad.at[pl.ds(0, 16), :], ha_s.at[0], ha_r.at[0], at(next_i, j)),
        rcopy(firstrows, xpad.at[pl.ds(16 + T, 16), :], ha_s.at[1], ha_r.at[1], at(prev_i, j)),
    ]
    slab_pre = rcopy(
        lastrows, xe.at[j, pl.ds(0, 16), :], ha_s.at[2], ha_r.at[2 + j], at(next_i, 0)
    )
    slab_post = rcopy(
        firstrows, xe.at[j, pl.ds(SR + 48, 16), :], ha_s.at[3], ha_r.at[2 + j], at(prev_i, NJ - 1)
    )
    slab_pre.start()
    slab_post.start()
    for k in far_first:
        xa(k, to(k)).start()
    def wx(k, slot, dev):
        cols = pl.ds(pl.multiple_of((dev // GROUP) * WC, 128), WC)
        return rcopy(
            w_ref.at[wrows(zi), cols], wbuf.at[slot, wrows(zi), :], w_s.at[k], w_r.at[k],
            at(i, dev),
        )

    def wrelay(k, slot, dev):
        part = wbuf.at[slot, wrows(zi), :]
        return rcopy(part, part, w_s.at[GROUP + k], w_r.at[GROUP + k], at(i, dev))

    def halfway(d):
        return ZC % 2 == 0 and d == ZC // 2 - 1

    def up_ring(d, z):
        part = wbuf.at[pl.ds(0, NJ // 2 if halfway(d) else NJ), wrows(z), :]
        return rcopy(part, part, up_s.at[d], up_r.at[d], at(zpos(zto(1)), j))

    def down_ring(d, z):
        first = NJ // 2 if halfway(d) else 0
        part = wbuf.at[pl.ds(first, NJ - first), wrows(z), :]
        return rcopy(part, part, dn_s.at[d], dn_r.at[d], at(zpos(zfrm(1)), j))

    def ring_start(d):
        if d < ZC // 2:
            up_ring(d, zfrm(d)).start()
        if d < ZC // 2:
            down_ring(d, zto(d)).start()

    def ring_wait(d):
        if d < ZC // 2:
            up_ring(d, zfrm(d + 1)).wait_recv()
        if d < ZC // 2:
            down_ring(d, zto(d + 1)).wait_recv()

    for k in (GROUP, 2, 1, 3):
        wx(k, j, to(k)).start()
    for h in halo:
        h.start()
    gains = [
        rcopy(gall.at[j], gall.at[j], g_s.at[k], g_r.at[k], at(i, to(k))) for k in range(1, NJ)
    ]
    for g in gains:
        g.start()

    def conv_pair(taps, rtaps, slot=0):
        vf = taps[0:1, :] * cbuf[slot, 13:13 + SR, :]
        vr = rtaps[0:1, :] * cbuf[slot, 19:19 + SR, :]
        for k in range(1, 4):
            vf = vf + taps[k:k + 1, :] * cbuf[slot, 13 + k:13 + k + SR, :]
            vr = vr + rtaps[k:k + 1, :] * cbuf[slot, 19 - k:19 - k + SR, :]
        return silu(vf).astype(BF16), silu(vr).astype(BF16)

    here[2].wait()
    for b in range(NJ):
        block = pwt[:, b * CW:(b + 1) * CW].T
        pwv[b * CW:(b + 1) * CW, :] = block
        pwr[(NJ - 1 - b) * CW:(NJ - b) * CW, :] = mm(anti_b, block).astype(BF16)

    own_cols = pl.ds(pl.multiple_of(j * CW, 128), CW)

    def own_conv(c, carry):
        rows = pl.ds(pl.multiple_of(c * SR, 16), SR)
        cbuf[0] = xpad[pl.ds(pl.multiple_of(c * SR, 16), SR + 32), :].astype(F32)
        f, r = conv_pair(cw_ref[:, own_cols], cwr[:, own_cols])
        xf[rows, :] = f
        xr[rows, :] = r
        return carry

    here[0].wait()
    lax.fori_loop(1, NJ - 1, own_conv, 0)

    @pl.when(j == 0)
    def _():
        for q in range(NJ):
            rcopy(
                lastrows, xe.at[q, pl.ds(0, 16), :], ha_s.at[2], ha_r.at[2 + q], at(prev_i, q)
            ).wait_recv()

    @pl.when(j == NJ - 1)
    def _():
        for q in range(NJ):
            rcopy(
                firstrows, xe.at[q, pl.ds(SR + 48, 16), :], ha_s.at[3], ha_r.at[2 + q],
                at(next_i, q),
            ).wait_recv()

    @pl.when(jnp.logical_and(i == 0, j == 0))
    def _():
        for q in range(NJ):
            xe[q, 0:16, :] = jnp.zeros((16, CW), BF16)

    @pl.when(jnp.logical_and(i == NC - 1, j == NJ - 1))
    def _():
        for q in range(NJ):
            xe[q, SR + 48:SR + 64, :] = jnp.zeros((16, CW), BF16)

    start = pl.multiple_of(SR * j - win(j), 16)
    here[1].wait()

    def block_proj(k, slot, carry):
        pf, pr = carry
        b = frm(k)
        cols = pl.ds(pl.multiple_of(b * CW, 128), CW)
        cbuf[slot] = xe[b, pl.ds(start, SR + 32), :].astype(F32)
        f, r = conv_pair(cw_ref[:, cols], cwr[:, cols], slot)
        pf = pf + mm(f, pwv[cols, :])
        pr = pr + mm(r, pwr[cols, :])
        return pf, pr

    def slab(k, carry):
        @pl.when(k > 0)
        def _():
            xa_in(k).wait_recv()

        return block_proj(k, 0, carry)

    wide = pwv.shape[1]
    pf, pr = lax.fori_loop(
        0, GROUP, slab, (jnp.zeros((SR, wide), F32), jnp.zeros((SR, wide), F32))
    )
    wx(GROUP, frm(GROUP), frm(GROUP)).wait_recv()
    for q in (2, 1, 3):
        wrelay(q, to(GROUP), to(q)).start()
    for k in range(GROUP, NJ):
        xa_in(k).wait_recv()
    for k in range(GROUP, NJ):
        pf, pr = block_proj(k, k % 2, (pf, pr))
    def bbx(k, slot, dev):
        return rcopy(bb.at[slot], bb.at[slot], bb_s.at[k], bb_r.at[k], at(i, dev))

    def relay(k, slot, dev):
        return rcopy(bb.at[slot], bb.at[slot], bb_s.at[GROUP + k], bb_r.at[GROUP + k], at(i, dev))

    def ccx(k, slot, dev):
        return rcopy(cc.at[slot], cc.at[slot], cc_s.at[k], cc_r.at[k], at(i, dev))

    def dtx(k, slot, dev):
        return rcopy(dtout.at[dev], dtin.at[slot], dt_s.at[k], dt_r.at[k], at(i, dev))

    bb[j, :, 0:N] = pf[:, 0:N].astype(BF16)
    bb[j, :, N:2 * N] = pr[:, 0:N].astype(BF16)
    for k in (GROUP, 2, 1, 3):
        bbx(k, j, to(k)).start()
    raw = jnp.concatenate([pf[:, 2 * N:], pr[:, 2 * N:]], axis=1).T
    bias = jnp.concatenate([prm[0], prm[0]], axis=0)
    v = raw + bias
    dts = jnp.maximum(v, 0.0) + jnp.log1p(jnp.exp(-jnp.abs(v)))
    for q in range(NJ):
        dtout[q, 0:HL, :] = dts[q * HL:(q + 1) * HL, :]
        dtout[q, HL:2 * HL, :] = dts[heads + (NJ - 1 - q) * HL:heads + (NJ - q) * HL, :]
    for k in far_first:
        dtx(k, j, to(k)).start()
    dtin[j] = dtout[j]
    cc[j, :, 0:N] = pf[:, N:2 * N].astype(BF16)
    cc[j, :, N:2 * N] = pr[:, N:2 * N].astype(BF16)

    for h in halo:
        h.wait_recv()

    @pl.when(i == 0)
    def _():
        xpad[0:16, :] = jnp.zeros((16, CW), BF16)

    @pl.when(i == NC - 1)
    def _():
        xpad[16 + T:32 + T, :] = jnp.zeros((16, CW), BF16)

    own_conv(0, 0)
    own_conv(NJ - 1, 0)

    for k in range(1, GROUP):
        wx(k, frm(k), frm(k)).wait_recv()
        wrelay(k, frm(GROUP + k), frm(k)).wait_recv()
    here[3].wait()
    ring_start(0)

    bbx(GROUP, frm(GROUP), frm(GROUP)).wait_recv()
    for k in (2, 1, 3):
        relay(k, to(GROUP), to(k)).start()

    own = pl.ds(pl.multiple_of(j * HL, 8), HL)
    mirror = pl.ds(pl.multiple_of((NJ - 1 - j) * HL, 8), HL)

    def own_rows(which):
        return jnp.concatenate([prm[which, own, :], prm[which, mirror, :]], axis=0)

    rate = -jnp.exp(own_rows(1))
    src, dst = iota((SR, 2 * SR), 0), iota((SR, 2 * SR), 1)
    sums = jnp.where(dst < SR, dst - src, src - dst + SR) >= 0
    sums = jnp.where(sums, 1.0, 0.0).astype(BF16)
    is_fwd = iota((2 * HL, SR), 0) < HL
    chunk_lane = iota((2 * HL, SR), 1)

    def states(k, ends):
        c = frm(k)

        @pl.when(k > 0)
        def _():
            dtx(k, c, c).wait_recv()

        @pl.when(jnp.logical_and(k > 0, k < GROUP))
        def _():
            bbx(k, c, c).wait_recv()

        @pl.when(k > GROUP)
        def _():
            relay(k - GROUP, c, c).wait_recv()

        @pl.when(k == GROUP + 2)
        def _():
            ring_wait(0)
            ring_start(1)

        @pl.when(k == 1)
        def _():
            for q in range(1, GROUP):
                ccx(q, j, to(q)).start()

        @pl.when(k == GROUP + 1)
        def _():
            for q in range(GROUP, NJ):
                ccx(q, j, to(q)).start()

        rows = pl.ds(pl.multiple_of(c * SR, 16), SR)
        dt = dtin[c]
        a = dt * rate
        run = mm(terms(a), sums)
        run = run[0:2 * HL] + run[2 * HL:4 * HL] + run[4 * HL:6 * HL]
        cum = jnp.where(is_fwd, run[:, 0:SR], run[:, SR:2 * SR])
        end = jnp.sum(a, axis=1, keepdims=True)
        cumr[c] = cum
        tail = expand(jnp.exp(end - cum) * dt)
        tf = (xf[rows, :].astype(F32) * tail[:, 0:CW]).astype(BF16)
        tr = (xr[rows, :].astype(F32) * tail[:, CW:2 * CW]).astype(BF16)
        fresh[c, :, 0:CW] = mm(bb[c, :, 0:N], tf, ((0,), (0,)))
        fresh[c, :, CW:2 * CW] = mm(bb[c, :, N:2 * N], tr, ((0,), (0,)))
        return jnp.where(chunk_lane == c, end, ends)

    ends = lax.fori_loop(0, NJ, states, jnp.zeros((2 * HL, SR), F32))
    ends = jnp.where(chunk_lane == NJ, jnp.sum(ends, axis=1, keepdims=True), ends)
    whole = expand(jnp.exp(ends))
    for c in range(NJ):
        dch[c] = jnp.broadcast_to(whole[c:c + 1, :], (8, 2 * CW))
    dec_me[...] = jnp.broadcast_to(whole[NJ:NJ + 1, :], (8, 2 * CW))

    stin[...] = jnp.zeros((N, 2 * CW), F32)

    def fold(c, carry):
        r = NJ - 1 - c
        stin[:, 0:CW] = dch[c, 0:1, 0:CW] * stin[:, 0:CW] + fresh[c, :, 0:CW]
        stin[:, CW:2 * CW] = (
            dch[r, 0:1, CW:2 * CW] * stin[:, CW:2 * CW] + fresh[r, :, CW:2 * CW]
        )
        return carry

    lax.fori_loop(0, NJ, fold, 0)

    swap = [
        rcopy(stin, st_o, sb_s.at[0], sb_r.at[0], at(sib, j)),
        rcopy(dec_me, dec_o, sb_s.at[1], sb_r.at[1], at(sib, j)),
    ]
    for h in swap:
        h.start()
    for h in swap:
        h.wait_recv()
    mine = pl.ds(pl.multiple_of(core * (N // 2), 8), N // 2)
    s_me, s_o = stin[mine, :], st_o[mine, :]
    d_me, d_o = dec_me[0:1, :], dec_o[0:1, :]
    fwd_lane = jnp.where(iota((8, 2 * CW), 1) < CW, 1, 0)[0:1, :]
    other_last = fwd_lane == 1 - core
    pair = jnp.where(other_last, d_o * s_me + s_o, d_me * s_o + s_me)
    d_pair = jnp.broadcast_to(d_me * d_o, (8, 2 * CW))
    place = iota((16, 128), 0)
    d_tile = jnp.zeros((16, 128), F32)
    for q in range(LB):
        d = d_pair[:, q * 128:(q + 1) * 128][0:1, :]
        hi = d.astype(BF16).astype(F32)
        mid = (d - hi).astype(BF16).astype(F32)
        for t, term in enumerate((hi, mid, d - hi - mid)):
            d_tile = jnp.where(place == t * LB + q, term, d_tile)
    d_tile = d_tile.astype(BF16)
    for p in range(ZC):
        blocks = [pair[p * PR:(p + 1) * PR, q * 128:(q + 1) * 128] for q in range(LB)]
        zs[p, 0:LB * PR, :] = jnp.concatenate(blocks, axis=0).astype(BF16)
        zs[p, LB * PR:LB * PR + 16, :] = d_tile
    zr[zi] = zs[zi]

    def zx(k, slot, z):
        return rcopy(zs.at[z], zr.at[slot], zx_s.at[k], zx_r.at[k], at(zpos(z), j))

    def zy(k, slot, z):
        return rcopy(es.at[z], er.at[slot], zy_s.at[k], zy_r.at[k], at(zpos(z), j))

    for k in range(1, ZC):
        zx(k, zi, zto(k)).start()

    low = iota((SR, SR), 0) >= iota((SR, SR), 1)
    upp = iota((SR, SR), 0) <= iota((SR, SR), 1)
    lane_head = iota((8, CW), 1) // (CW // HL)
    skips = expand(own_rows(2))[0:8, :]

    def inner(k, carry):
        c = frm(k)

        @pl.when(k > 0)
        def _():
            ccx(k, c, c).wait_recv()

        rows = pl.ds(pl.multiple_of(c * SR, 16), SR)
        cum = cumr[c]
        cols = jnp.concatenate([cum, jnp.zeros((SR - 2 * HL, SR), F32)], axis=0).T
        lds = cum - jnp.log(dtin[c])
        y = jnp.zeros((SR, CW), F32)
        for d, (xs, mask) in enumerate(((xf, low), (xr, upp))):
            xv = xs[rows, :]
            part = slice(d * N, (d + 1) * N)
            score = mm(cc[c, :, part], bb[c, :, part], ((1,), (1,)))
            for q in range(HL):
                row = q if d == 0 else 2 * HL - 1 - q
                seg = jnp.where(mask, cols[:, row:row + 1] - lds[row:row + 1, :], -1e30)
                mcat[:, q * SR:(q + 1) * SR] = (score * jnp.exp(seg)).astype(BF16)
                keep = jnp.where(lane_head == q, 1.0, 0.0)[0:1, :].astype(BF16)
                xbd[q * SR:(q + 1) * SR, :] = xv * keep
            y = y + mm(mcat[...], xbd[...])
            y = y + skips[0:1, d * CW:(d + 1) * CW] * xv.astype(F32)
        yacc[rows, :] = y
        grown[c] = expand(jnp.exp(cum))
        return carry

    lax.fori_loop(0, 3, inner, 0)

    for k in range(1, ZC):
        zx(k, zfrm(k), zfrm(k)).wait_recv()

    pieces, decays = [], []
    for z in range(ZC):
        whole = zr[z].astype(F32)
        pieces.append(whole[0:LB * PR])
        tile = whole[LB * PR:LB * PR + 16]
        decays.append([
            tile[q:q + 1] + tile[LB + q:LB + q + 1] + tile[2 * LB + q:2 * LB + q + 1]
            for q in range(LB)
        ])

    def chain(q, e):
        order = range(ZC) if q < LB // 2 else range(ZC - 1, -1, -1)
        before = [None] * ZC
        for z in order:
            before[z] = e
            e = decays[z][q] * e + pieces[z][q * PR:(q + 1) * PR]
        return before, e

    zero = jnp.zeros((PR, 128), F32)
    if XL > 1:
        for q in range(LB):
            xs_[q * PR:(q + 1) * PR, :] = chain(q, zero)[1]
        cross = rcopy(xs_, xr_, sb_s.at[2], sb_r.at[2], at(across, j))
        cross.start()
        lax.fori_loop(3, 4, inner, 0)
        cross.wait_recv()
    before = []
    for q in range(LB):
        start_from = zero
        if XL > 1:
            takes = xlo == 1 if q < LB // 2 else xlo == 0
            start_from = jnp.where(takes, xr_[q * PR:(q + 1) * PR, :], 0.0)
        before.append(chain(q, start_from)[0])
    for z in range(ZC):
        es[z] = jnp.concatenate([before[q][z] for q in range(LB)], axis=0).astype(BF16)
    er[zi] = es[zi]
    for k in range(1, ZC):
        zy(k, zi, zto(k)).start()
    lax.fori_loop(4 if XL > 1 else 3, NJ, inner, 0)
    for k in range(1, ZC):
        zy(k, zfrm(k), zfrm(k)).wait_recv()
    ring_wait(1)
    ring_start(2)
    for p in range(ZC):
        piece = er[p].astype(F32)
        for q in range(LB):
            ech[pl.ds(pl.multiple_of(core * (N // 2) + p * PR, 8), PR), q * 128:(q + 1) * 128] = (
                piece[q * PR:(q + 1) * PR, :]
            )
    halves = rcopy(ech.at[mine, :], ech.at[mine, :], sb_s.at[3], sb_r.at[3], at(sib, j))
    halves.start()
    for h in swap:
        h.wait_send()
    theirs = pl.ds(pl.multiple_of((1 - core) * (N // 2), 8), N // 2)
    rcopy(ech.at[theirs, :], ech.at[theirs, :], sb_s.at[3], sb_r.at[3], at(sib, j)).wait_recv()
    other_first = fwd_lane == core
    stin[...] = jnp.where(other_first, dec_o[0:1, :] * ech[...] + st_o[...], ech[...])

    def enter(s, carry):
        for d in range(2):
            c = s if d == 0 else NJ - 1 - s
            lanes = slice(d * CW, (d + 1) * CW)
            st = stin[:, lanes]
            top = st.astype(BF16)
            sbs[c, 0:N, lanes] = top
            sbs[c, N:2 * N, lanes] = (st - top.astype(F32)).astype(BF16)
            stin[:, lanes] = dch[c, 0:1, lanes] * st + fresh[c, :, lanes]
        return carry

    lax.fori_loop(0, NJ, enter, 0)

    HB = RB // 2

    def cbx(h, k, slot, dev):
        rows = pl.ds(pl.multiple_of(lax.rem(dev, GROUP) * RB + h * HB, 16), HB)
        return rcopy(
            comb_s.at[rows, :], comb_r.at[slot, pl.ds(h * HB, HB), :],
            cb_s.at[h, k], cb_r.at[h, k], at(i, dev),
        )

    chunks = HB // SR
    for h in range(2):

        def finish(n, carry):
            c = (n // chunks) * (2 * chunks) + h * chunks + lax.rem(n, chunks)
            rows = pl.ds(pl.multiple_of(c * SR, 16), SR)
            y = yacc[rows, :]
            for d in range(2):
                lanes = slice(d * CW, (d + 1) * CW)
                cv = cc[c, :, d * N:(d + 1) * N]
                z = mm(jnp.concatenate([cv, cv], axis=1), sbs[c, :, lanes])
                y = y + grown[c, :, lanes] * z
            comb_s[rows, :] = (y * gain_ref[...]).astype(BF16)
            return carry

        lax.fori_loop(0, NJ // 2, finish, 0)
        for k in far_first:
            cbx(h, k, j, to(k)).start()
    comb_r[j] = comb_s[pl.ds(pl.multiple_of(yy * RB, 16), RB), :]
    ring_wait(2)
    ring_start(3)
    ring_wait(3)
    half = pl.ds(pl.multiple_of(core * (CW // 2), 16), CW // 2)
    rest = pl.ds(pl.multiple_of((1 - core) * (CW // 2), 16), CW // 2)
    share = rcopy(wbuf.at[:, half, :], wbuf.at[:, half, :], sb_s.at[4], sb_r.at[4], at(sib, j))
    share.start()
    for k in range(1, NJ):
        s = frm(k)
        rcopy(gall.at[s], gall.at[s], g_s.at[k], g_r.at[k], at(i, s)).wait_recv()
    rcopy(
        wbuf.at[:, rest, :], wbuf.at[:, rest, :], sb_s.at[4], sb_r.at[4], at(sib, j)
    ).wait_recv()

    def obx(h, k, slot, dest):
        rows = pl.ds(h * HB, HB)
        return rcopy(
            obs.at[dest, rows, :], obr.at[slot, rows, :], ob_s.at[h, k], ob_r.at[h, k],
            at(i, xh * GROUP + dest),
        )

    for h in range(2):
        rows = slice(h * HB, (h + 1) * HB)
        acc[...] = jnp.zeros((HB, WC), F32)
        sqs[...] = jnp.zeros((HB, CW), F32)

        def project(k, carry):
            @pl.when(k > 0)
            def _():
                cbx(h, k, frm(k), frm(k)).wait_recv()

            b = frm(k)
            piece = comb_r[b, rows, :]
            acc[...] += mm(piece, wbuf[b])
            value = piece.astype(F32)
            sqs[...] += value * value * gall[b, 0:1, :]
            return carry

        lax.fori_loop(0, NJ, project, 0)
        scale = lax.rsqrt(jnp.sum(sqs[...], axis=1, keepdims=True) / D + EPS)
        for q in range(GROUP):
            obs[q, rows, :] = (acc[:, q * CW:(q + 1) * CW] * scale).astype(BF16)
        for k in range(1, GROUP):
            obx(h, k, yy, lax.rem(yy + k, GROUP)).start()
    def place_out(n, src, s, h, size):
        rows = pl.ds(pl.multiple_of(s * RB + h * HB, 16), size)
        return pltpu.make_async_copy(src, out_ref.at[rows, :], oc.at[n])

    outs = [place_out(0, obs.at[yy], yy, 0, RB)]
    outs[0].start()
    for h in range(2):
        for k in range(1, GROUP):
            s = lax.rem(yy + GROUP - k, GROUP)
            obx(h, k, s, s).wait_recv()
            outs.append(
                place_out(h * GROUP + k, obr.at[s, pl.ds(h * HB, HB), :], s, h, HB)
            )
            outs[-1].start()
    for h in outs:
        h.wait()

    slab_pre.wait_send()
    slab_post.wait_send()
    for h in halo:
        h.wait_send()
    for g in gains:
        g.wait_send()
    for k in range(1, NJ):
        xa(k, to(k)).wait_send()
        dtx(k, j, to(k)).wait_send()
        if k <= GROUP:
            bbx(k, j, to(k)).wait_send()
        else:
            relay(k - GROUP, to(GROUP), to(k - GROUP)).wait_send()
        ccx(k, j, to(k)).wait_send()
        if k <= GROUP:
            wx(k, j, to(k)).wait_send()
        else:
            wrelay(k - GROUP, to(GROUP), to(k - GROUP)).wait_send()
        for h in range(2):
            cbx(h, k, j, to(k)).wait_send()

    for k in range(1, ZC):
        zx(k, zi, zto(k)).wait_send()
        zy(k, zi, zto(k)).wait_send()
    if XL > 1:
        cross.wait_send()
    halves.wait_send()
    share.wait_send()
    for d in range(ZC // 2):
        up_ring(d, zfrm(d)).wait_send()
    for d in range(ZC // 2):
        down_ring(d, zto(d)).wait_send()
    for h in range(2):
        for k in range(1, GROUP):
            obx(h, k, yy, lax.rem(yy + k, GROUP)).wait_send()


def shards(x_in, conv_weight, proj_weight, dt_bias, decay_log, skip_gain, norm_gain, out_weight):
    T, CW = x_in.shape
    D = conv_weight.shape[1]
    H = dt_bias.shape[0]
    N = (proj_weight.shape[1] - H) // 2
    NC, NJ = lax.axis_size("ctx"), lax.axis_size("chan")
    HL = H // NJ
    SR = T // NJ
    XL = 2 if NC >= 4 else 1
    ZC = NC // (2 * XL)
    PR, LB = N // 2 // ZC, 2 * CW // 128
    RB, WC = T // GROUP, GROUP * CW
    dma = pltpu.SemaphoreType.DMA
    vm = pltpu.VMEM
    scratch = [
        vm((T + 32, CW), BF16), vm((NJ, SR + 64, CW), BF16), vm((2, SR + 32, CW), F32),
        vm((4, D), F32), vm((T, CW), BF16), vm((T, CW), BF16),
        vm((NJ, SR, 2 * N), BF16), vm((NJ, SR, 2 * N), BF16),
        vm((NJ, 2 * HL, SR), F32), vm((NJ, 2 * HL, SR), F32),
        vm((NJ, 2 * HL, SR), F32),
        vm((NJ, N, 2 * CW), F32), vm((NJ, 8, 2 * CW), F32), vm((T, CW), F32),
        vm((SR, HL * SR), BF16), vm((HL * SR, CW), BF16), vm((6 * HL, 2 * CW), BF16),
        vm((ZC, LB * PR + 16, 128), BF16), vm((ZC, LB * PR + 16, 128), BF16),
        vm((ZC, LB * PR, 128), BF16), vm((ZC, LB * PR, 128), BF16),
        vm((LB * PR, 128), F32), vm((LB * PR, 128), F32),
        vm((N, 2 * CW), F32), vm((N, 2 * CW), F32), vm((8, 2 * CW), F32), vm((8, 2 * CW), F32),
        vm((N, 2 * CW), F32),
        vm((T, CW), BF16), vm((NJ, RB, CW), BF16), vm((NJ, 8, CW), F32),
        vm((NJ, CW, WC), BF16), vm((RB // 2, WC), F32),
        vm((GROUP, RB, CW), BF16), vm((GROUP, RB, CW), BF16),
        vm((RB // 2, CW), F32), vm((NJ, SR, 2 * CW), F32), vm((NJ, 2 * N, 2 * CW), BF16),
        dma((NJ,)), dma((NJ,)), dma((4,)), dma((2 + NJ,)), dma((NJ,)), dma((NJ,)),
        dma((NJ,)), dma((NJ,)), dma((4,)), dma((4,)), dma((4,)), dma((4,)),
        dma((NJ,)), dma((NJ,)), dma((NJ,)), dma((NJ,)), dma((NJ,)), dma((NJ,)),
        dma((ZC,)), dma((ZC,)), dma((ZC,)), dma((ZC,)), dma((5,)), dma((5,)),
        dma((2, NJ)), dma((2, NJ)), dma((2, GROUP)), dma((2, GROUP)),
        vm(proj_weight.shape, BF16), vm(proj_weight.shape, BF16),
        vm(proj_weight.shape[::-1], BF16), vm((3, H, 128), F32), dma((9,)),
        vm((4, D), F32), vm((1, H), F32), vm((1, H), F32), vm((1, H), F32), vm((1, CW), F32), dma((2 * GROUP,)),
    ]
    return pl.pallas_call(
        functools.partial(kernel, (NC, NJ, T, CW, D, N, HL, XL, ZC)),
        out_shape=jax.ShapeDtypeStruct((T, CW), BF16),
        in_specs=[pl.BlockSpec(memory_space=pl.ANY)] * 8,
        out_specs=pl.BlockSpec(memory_space=pl.ANY),
        scratch_shapes=scratch,
        compiler_params=pltpu.CompilerParams(
            collective_id=0, has_side_effects=True, vmem_limit_bytes=62 * 1024 * 1024
        ),
        cost_estimate=pl.CostEstimate(
            flops=4 * T * D * CW, bytes_accessed=8 * T * CW, transcendentals=16 * T * SR
        ),
    )(
        x_in, conv_weight, proj_weight.T, dt_bias[None], decay_log[None], skip_gain[None],
        norm_gain[None], out_weight,
    )


def solution(mesh):
    in_specs = (P("ctx", "chan"), P(), P(), P(), P(), P(), P("chan"), P("chan", None))
    out_specs = P("ctx", "chan")
    return jax.shard_map(shards, mesh=mesh, in_specs=in_specs, out_specs=out_specs, check_vma=False)
```

```python
import functools

import jax
import jax.numpy as jnp
from jax import lax
from jax.experimental import pallas as pl
from jax.experimental.pallas import tpu as pltpu
from jax.sharding import PartitionSpec as P

F32 = jnp.float32
BF16 = jnp.bfloat16
MESH = pl.DeviceIdType.MESH
EPS = 1e-05
GROUP = 4


def mm(a, b, dims=((1,), (0,)), **kw):
    return lax.dot_general(a, b, (dims, ((), ())), preferred_element_type=F32, **kw)


def silu(v):
    return v / (1.0 + jnp.exp(-v))


def iota(shape, axis):
    return lax.broadcasted_iota(jnp.int32, shape, axis)


def kernel(
    dims,
    x_ref, cw_hbm, pw_ref, bias_hbm, decay_hbm, skip_hbm, gain_hbm, w_ref, out_ref,
    xpad, xe, cbuf, cwr, xf, xr, bb, cc, dtout, dtin, cumr, fresh, dch, yacc,
    mcat, xbd, emat, zs, zr, es, er, xs_, xr_, st_o, ech, dec_me, dec_o, stin, comb_s, comb_r, gall, wbuf, acc, obs, obr, sqs, grown, sbs,
    xa_s, xa_r, ha_s, ha_r, g_s, g_r, w_s, w_r, up_s, up_r, dn_s, dn_r, bb_s, bb_r, cc_s, cc_r, dt_s, dt_r,
    zx_s, zx_r, zy_s, zy_r, sb_s, sb_r, cb_s, cb_r, ob_s, ob_r, pwv, pwr, pwt, prm, lc,
    cw_ref, bias_ref, decay_ref, skip_ref, gain_ref, oc,
):
    NC, NJ, T, CW, D, N, HL, XL, ZC = dims
    SR = T // NJ
    PR = N // 2 // ZC
    LB = 2 * CW // 128
    WR = CW // 2 // ZC
    RB = T // GROUP
    WC = GROUP * CW
    i = lax.axis_index("ctx")
    j = lax.axis_index("chan")
    prev_i = lax.rem(i + NC - 1, NC)
    next_i = lax.rem(i + 1, NC)
    core = lax.rem(i, 2)
    sib = i + 1 - 2 * core
    xlo = i // (2 * ZC)
    zi = lax.rem(i // 2, ZC)
    xh = j // GROUP
    yy = lax.rem(j, GROUP)

    def at(ci, cj):
        return {"ctx": ci, "chan": cj}

    def to(k):
        return lax.rem(xh + k // GROUP, 2) * GROUP + lax.rem(yy + lax.rem(k, GROUP), GROUP)

    def frm(k):
        return (
            lax.rem(xh + k // GROUP, 2) * GROUP
            + lax.rem(yy + GROUP - lax.rem(k, GROUP), GROUP)
        )

    far_first = (6, 5, 7, 4, 2, 1, 3)

    def rcopy(src, dst, ss, rs, dev):
        return pltpu.make_async_remote_copy(
            src_ref=src, dst_ref=dst, send_sem=ss, recv_sem=rs, device_id=dev, device_id_type=MESH
        )

    def win(jd):
        return pl.multiple_of(jnp.clip(SR * jd - 16, 0, T - SR - 32), 16)

    def wrows(z):
        return pl.ds(pl.multiple_of(core * (CW // 2) + z * WR, 16), WR)

    own_wide = pl.ds(pl.multiple_of(xh * WC, 128), WC)
    here = [
        pltpu.make_async_copy(x_ref, xpad.at[pl.ds(16, T), :], lc.at[0]),
        pltpu.make_async_copy(
            x_ref.at[pl.ds(win(j), SR + 32), :], xe.at[j, pl.ds(16, SR + 32), :], lc.at[1]
        ),
        pltpu.make_async_copy(pw_ref, pwt, lc.at[2]),
        pltpu.make_async_copy(
            w_ref.at[wrows(zi), own_wide], wbuf.at[j, wrows(zi), :], lc.at[3]
        ),
    ]
    small = [
        pltpu.make_async_copy(src, dst, lc.at[4 + q])
        for q, (src, dst) in enumerate((
            (cw_hbm, cw_ref), (bias_hbm, bias_ref), (decay_hbm, decay_ref),
            (skip_hbm, skip_ref), (gain_hbm, gain_ref),
        ))
    ]
    for h in small + here:
        h.start()

    barrier = pltpu.get_barrier_semaphore()

    def hail(dev):
        pl.semaphore_signal(barrier, inc=1, device_id=dev, device_id_type=MESH)

    for k in range(1, NJ):
        hail(at(i, to(k)))

    def zpos(z):
        return xlo * (2 * ZC) + z * 2 + core

    def zto(k):
        return lax.rem(zi + k, ZC)

    def zfrm(k):
        return lax.rem(zi + ZC - k, ZC)

    for k in range(1, ZC):
        hail(at(zpos(zto(k)), j))
    across = lax.rem(i + 2 * ZC, NC)
    if XL > 1:
        hail(at(across, j))
    for c in (sib, prev_i, next_i):
        hail(at(c, j))

    @pl.when(j == 0)
    def _():
        for q in range(NJ):
            hail(at(prev_i, q))

    @pl.when(j == NJ - 1)
    def _():
        for q in range(NJ):
            hail(at(next_i, q))

    for h in small:
        h.wait()
    gall[j] = jnp.broadcast_to(1.0 / (gain_ref[...] * gain_ref[...]), (8, CW))
    heads = HL * NJ
    eye = iota((heads, heads), 0) == iota((heads, heads), 1)
    for q, ref in enumerate((bias_ref, decay_ref, skip_ref)):
        row = jnp.broadcast_to(ref[...], (heads, heads))
        column = jnp.sum(jnp.where(eye, row, 0.0), axis=1, keepdims=True)
        prm[q] = jnp.broadcast_to(column, (heads, 128))
    anti = iota((CW, CW), 0) + iota((CW, CW), 1) == CW - 1
    anti_f = jnp.where(anti, 1.0, 0.0).astype(F32)
    anti_b = anti_f.astype(BF16)
    for b in range(NJ):
        cwr[:, b * CW:(b + 1) * CW] = mm(
            cw_ref[:, (NJ - 1 - b) * CW:(NJ - b) * CW], anti_f, precision=lax.Precision.HIGHEST
        )
    head_row = lax.rem(iota((6 * HL, 2 * CW), 0), 2 * HL)
    ec = iota((6 * HL, 2 * CW), 1)
    head_of = ec // (CW // HL)
    target = jnp.where(head_of < HL, head_of, 3 * HL - 1 - head_of)
    emat[...] = jnp.where(head_row == target, 1.0, 0.0).astype(BF16)

    def terms(rows):
        hi = rows.astype(BF16)
        rest = rows - hi.astype(F32)
        mid = rest.astype(BF16)
        low = (rest - mid.astype(F32)).astype(BF16)
        return jnp.concatenate([hi, mid, low], axis=0)

    def expand(rows):
        return mm(terms(rows), emat[...], ((0,), (0,)))

    pl.semaphore_wait(barrier, NJ - 1 + ZC - 1 + XL - 1 + 3 + 2)

    def xa(k, jd):
        return rcopy(
            x_ref.at[pl.ds(win(jd), SR + 32), :], xe.at[j, pl.ds(16, SR + 32), :],
            xa_s.at[k], xa_r.at[k], at(i, jd),
        )

    def xa_in(k):
        return rcopy(
            x_ref.at[pl.ds(0, SR + 32), :], xe.at[frm(k), pl.ds(16, SR + 32), :],
            xa_s.at[k], xa_r.at[k], at(i, frm(k)),
        )

    lastrows, firstrows = x_ref.at[pl.ds(T - 16, 16), :], x_ref.at[pl.ds(0, 16), :]
    halo = [
        rcopy(lastrows, xpad.at[pl.ds(0, 16), :], ha_s.at[0], ha_r.at[0], at(next_i, j)),
        rcopy(firstrows, xpad.at[pl.ds(16 + T, 16), :], ha_s.at[1], ha_r.at[1], at(prev_i, j)),
    ]
    slab_pre = rcopy(
        lastrows, xe.at[j, pl.ds(0, 16), :], ha_s.at[2], ha_r.at[2 + j], at(next_i, 0)
    )
    slab_post = rcopy(
        firstrows, xe.at[j, pl.ds(SR + 48, 16), :], ha_s.at[3], ha_r.at[2 + j], at(prev_i, NJ - 1)
    )
    slab_pre.start()
    slab_post.start()
    for k in far_first:
        xa(k, to(k)).start()
    def wx(k, slot, dev):
        cols = pl.ds(pl.multiple_of((dev // GROUP) * WC, 128), WC)
        return rcopy(
            w_ref.at[wrows(zi), cols], wbuf.at[slot, wrows(zi), :], w_s.at[k], w_r.at[k],
            at(i, dev),
        )

    def wrelay(k, slot, dev):
        part = wbuf.at[slot, wrows(zi), :]
        return rcopy(part, part, w_s.at[GROUP + k], w_r.at[GROUP + k], at(i, dev))

    def halfway(d):
        return ZC % 2 == 0 and d == ZC // 2 - 1

    def up_ring(d, z):
        part = wbuf.at[pl.ds(0, NJ // 2 if halfway(d) else NJ), wrows(z), :]
        return rcopy(part, part, up_s.at[d], up_r.at[d], at(zpos(zto(1)), j))

    def down_ring(d, z):
        first = NJ // 2 if halfway(d) else 0
        part = wbuf.at[pl.ds(first, NJ - first), wrows(z), :]
        return rcopy(part, part, dn_s.at[d], dn_r.at[d], at(zpos(zfrm(1)), j))

    def ring_start(d):
        if d < ZC // 2:
            up_ring(d, zfrm(d)).start()
        if d < ZC // 2:
            down_ring(d, zto(d)).start()

    def ring_wait(d):
        if d < ZC // 2:
            up_ring(d, zfrm(d + 1)).wait_recv()
        if d < ZC // 2:
            down_ring(d, zto(d + 1)).wait_recv()

    for k in (GROUP, 2, 1, 3):
        wx(k, j, to(k)).start()
    for h in halo:
        h.start()
    gains = [
        rcopy(gall.at[j], gall.at[j], g_s.at[k], g_r.at[k], at(i, to(k))) for k in range(1, NJ)
    ]
    for g in gains:
        g.start()

    def conv_pair(taps, rtaps, slot=0):
        vf = taps[0:1, :] * cbuf[slot, 13:13 + SR, :]
        vr = rtaps[0:1, :] * cbuf[slot, 19:19 + SR, :]
        for k in range(1, 4):
            vf = vf + taps[k:k + 1, :] * cbuf[slot, 13 + k:13 + k + SR, :]
            vr = vr + rtaps[k:k + 1, :] * cbuf[slot, 19 - k:19 - k + SR, :]
        return silu(vf).astype(BF16), silu(vr).astype(BF16)

    here[2].wait()
    for b in range(NJ):
        block = pwt[:, b * CW:(b + 1) * CW].T
        pwv[b * CW:(b + 1) * CW, :] = block
        pwr[(NJ - 1 - b) * CW:(NJ - b) * CW, :] = mm(anti_b, block).astype(BF16)

    own_cols = pl.ds(pl.multiple_of(j * CW, 128), CW)

    def own_conv(c, carry):
        rows = pl.ds(pl.multiple_of(c * SR, 16), SR)
        cbuf[0] = xpad[pl.ds(pl.multiple_of(c * SR, 16), SR + 32), :].astype(F32)
        f, r = conv_pair(cw_ref[:, own_cols], cwr[:, own_cols])
        xf[rows, :] = f
        xr[rows, :] = r
        return carry

    here[0].wait()
    lax.fori_loop(1, NJ - 1, own_conv, 0)

    @pl.when(j == 0)
    def _():
        for q in range(NJ):
            rcopy(
                lastrows, xe.at[q, pl.ds(0, 16), :], ha_s.at[2], ha_r.at[2 + q], at(prev_i, q)
            ).wait_recv()

    @pl.when(j == NJ - 1)
    def _():
        for q in range(NJ):
            rcopy(
                firstrows, xe.at[q, pl.ds(SR + 48, 16), :], ha_s.at[3], ha_r.at[2 + q],
                at(next_i, q),
            ).wait_recv()

    @pl.when(jnp.logical_and(i == 0, j == 0))
    def _():
        for q in range(NJ):
            xe[q, 0:16, :] = jnp.zeros((16, CW), BF16)

    @pl.when(jnp.logical_and(i == NC - 1, j == NJ - 1))
    def _():
        for q in range(NJ):
            xe[q, SR + 48:SR + 64, :] = jnp.zeros((16, CW), BF16)

    start = pl.multiple_of(SR * j - win(j), 16)
    here[1].wait()

    def block_proj(k, slot, carry):
        pf, pr = carry
        b = frm(k)
        cols = pl.ds(pl.multiple_of(b * CW, 128), CW)
        cbuf[slot] = xe[b, pl.ds(start, SR + 32), :].astype(F32)
        f, r = conv_pair(cw_ref[:, cols], cwr[:, cols], slot)
        pf = pf + mm(f, pwv[cols, :])
        pr = pr + mm(r, pwr[cols, :])
        return pf, pr

    def slab(k, carry):
        @pl.when(k > 0)
        def _():
            xa_in(k).wait_recv()

        return block_proj(k, 0, carry)

    wide = pwv.shape[1]
    pf, pr = lax.fori_loop(
        0, GROUP, slab, (jnp.zeros((SR, wide), F32), jnp.zeros((SR, wide), F32))
    )
    wx(GROUP, frm(GROUP), frm(GROUP)).wait_recv()
    for q in (2, 1, 3):
        wrelay(q, to(GROUP), to(q)).start()
    for k in range(GROUP, NJ):
        xa_in(k).wait_recv()
    for k in range(GROUP, NJ):
        pf, pr = block_proj(k, k % 2, (pf, pr))
    def bbx(k, slot, dev):
        return rcopy(bb.at[slot], bb.at[slot], bb_s.at[k], bb_r.at[k], at(i, dev))

    def relay(k, slot, dev):
        return rcopy(bb.at[slot], bb.at[slot], bb_s.at[GROUP + k], bb_r.at[GROUP + k], at(i, dev))

    def ccx(k, slot, dev):
        return rcopy(cc.at[slot], cc.at[slot], cc_s.at[k], cc_r.at[k], at(i, dev))

    def dtx(k, slot, dev):
        return rcopy(dtout.at[dev], dtin.at[slot], dt_s.at[k], dt_r.at[k], at(i, dev))

    bb[j, :, 0:N] = pf[:, 0:N].astype(BF16)
    bb[j, :, N:2 * N] = pr[:, 0:N].astype(BF16)
    for k in (GROUP, 2, 1, 3):
        bbx(k, j, to(k)).start()
    raw = jnp.concatenate([pf[:, 2 * N:], pr[:, 2 * N:]], axis=1).T
    bias = jnp.concatenate([prm[0], prm[0]], axis=0)
    v = raw + bias
    dts = jnp.maximum(v, 0.0) + jnp.log1p(jnp.exp(-jnp.abs(v)))
    for q in range(NJ):
        dtout[q, 0:HL, :] = dts[q * HL:(q + 1) * HL, :]
        dtout[q, HL:2 * HL, :] = dts[heads + (NJ - 1 - q) * HL:heads + (NJ - q) * HL, :]
    for k in far_first:
        dtx(k, j, to(k)).start()
    dtin[j] = dtout[j]
    cc[j, :, 0:N] = pf[:, N:2 * N].astype(BF16)
    cc[j, :, N:2 * N] = pr[:, N:2 * N].astype(BF16)

    for h in halo:
        h.wait_recv()

    @pl.when(i == 0)
    def _():
        xpad[0:16, :] = jnp.zeros((16, CW), BF16)

    @pl.when(i == NC - 1)
    def _():
        xpad[16 + T:32 + T, :] = jnp.zeros((16, CW), BF16)

    own_conv(0, 0)
    own_conv(NJ - 1, 0)

    for k in range(1, GROUP):
        wx(k, frm(k), frm(k)).wait_recv()
        wrelay(k, frm(GROUP + k), frm(k)).wait_recv()
    here[3].wait()
    ring_start(0)

    bbx(GROUP, frm(GROUP), frm(GROUP)).wait_recv()
    for k in (2, 1, 3):
        relay(k, to(GROUP), to(k)).start()

    own = pl.ds(pl.multiple_of(j * HL, 8), HL)
    mirror = pl.ds(pl.multiple_of((NJ - 1 - j) * HL, 8), HL)

    def own_rows(which):
        return jnp.concatenate([prm[which, own, :], prm[which, mirror, :]], axis=0)

    rate = -jnp.exp(own_rows(1))
    src, dst = iota((SR, 2 * SR), 0), iota((SR, 2 * SR), 1)
    sums = jnp.where(dst < SR, dst - src, src - dst + SR) >= 0
    sums = jnp.where(sums, 1.0, 0.0).astype(BF16)
    is_fwd = iota((2 * HL, SR), 0) < HL
    chunk_lane = iota((2 * HL, SR), 1)

    def chunk_state(c, ends):
        rows = pl.ds(pl.multiple_of(c * SR, 16), SR)
        dt = dtin[c]
        a = dt * rate
        run = mm(terms(a), sums)
        run = run[0:2 * HL] + run[2 * HL:4 * HL] + run[4 * HL:6 * HL]
        cum = jnp.where(is_fwd, run[:, 0:SR], run[:, SR:2 * SR])
        end = jnp.sum(a, axis=1, keepdims=True)
        cumr[c] = cum
        tail = expand(jnp.exp(end - cum) * dt)
        tf = (xf[rows, :].astype(F32) * tail[:, 0:CW]).astype(BF16)
        tr = (xr[rows, :].astype(F32) * tail[:, CW:2 * CW]).astype(BF16)
        fresh[c, :, 0:CW] = mm(bb[c, :, 0:N], tf, ((0,), (0,)))
        fresh[c, :, CW:2 * CW] = mm(bb[c, :, N:2 * N], tr, ((0,), (0,)))
        return jnp.where(chunk_lane == c, end, ends)

    def states(k, ends):
        c = frm(k)

        @pl.when(k > 0)
        def _():
            dtx(k, c, c).wait_recv()
            bbx(k, c, c).wait_recv()

        @pl.when(k == 1)
        def _():
            for q in range(1, GROUP):
                ccx(q, j, to(q)).start()

        return chunk_state(c, ends)

    ends = lax.fori_loop(0, GROUP, states, jnp.zeros((2 * HL, SR), F32))
    for k in range(GROUP, NJ):
        dtx(k, frm(k), frm(k)).wait_recv()
        if k > GROUP:
            relay(k - GROUP, frm(k), frm(k)).wait_recv()
    for k in range(GROUP, NJ):
        ccx(k, j, to(k)).start()
    for k in range(GROUP, NJ):
        if k == GROUP + 2:
            ring_wait(0)
            ring_start(1)
        ends = chunk_state(frm(k), ends)
    ends = jnp.where(chunk_lane == NJ, jnp.sum(ends, axis=1, keepdims=True), ends)
    whole = expand(jnp.exp(ends))
    for c in range(NJ):
        dch[c] = jnp.broadcast_to(whole[c:c + 1, :], (8, 2 * CW))
    dec_me[...] = jnp.broadcast_to(whole[NJ:NJ + 1, :], (8, 2 * CW))

    stin[...] = jnp.zeros((N, 2 * CW), F32)

    def fold(c, carry):
        r = NJ - 1 - c
        stin[:, 0:CW] = dch[c, 0:1, 0:CW] * stin[:, 0:CW] + fresh[c, :, 0:CW]
        stin[:, CW:2 * CW] = (
            dch[r, 0:1, CW:2 * CW] * stin[:, CW:2 * CW] + fresh[r, :, CW:2 * CW]
        )
        return carry

    lax.fori_loop(0, NJ, fold, 0)

    swap = [
        rcopy(stin, st_o, sb_s.at[0], sb_r.at[0], at(sib, j)),
        rcopy(dec_me, dec_o, sb_s.at[1], sb_r.at[1], at(sib, j)),
    ]
    for h in swap:
        h.start()
    for h in swap:
        h.wait_recv()
    mine = pl.ds(pl.multiple_of(core * (N // 2), 8), N // 2)
    s_me, s_o = stin[mine, :], st_o[mine, :]
    d_me, d_o = dec_me[0:1, :], dec_o[0:1, :]
    fwd_lane = jnp.where(iota((8, 2 * CW), 1) < CW, 1, 0)[0:1, :]
    other_last = fwd_lane == 1 - core
    pair = jnp.where(other_last, d_o * s_me + s_o, d_me * s_o + s_me)
    d_pair = jnp.broadcast_to(d_me * d_o, (8, 2 * CW))
    place = iota((16, 128), 0)
    d_tile = jnp.zeros((16, 128), F32)
    for q in range(LB):
        d = d_pair[:, q * 128:(q + 1) * 128][0:1, :]
        hi = d.astype(BF16).astype(F32)
        mid = (d - hi).astype(BF16).astype(F32)
        for t, term in enumerate((hi, mid, d - hi - mid)):
            d_tile = jnp.where(place == t * LB + q, term, d_tile)
    d_tile = d_tile.astype(BF16)
    for p in range(ZC):
        blocks = [pair[p * PR:(p + 1) * PR, q * 128:(q + 1) * 128] for q in range(LB)]
        zs[p, 0:LB * PR, :] = jnp.concatenate(blocks, axis=0).astype(BF16)
        zs[p, LB * PR:LB * PR + 16, :] = d_tile
    zr[zi] = zs[zi]

    def zx(k, slot, z):
        return rcopy(zs.at[z], zr.at[slot], zx_s.at[k], zx_r.at[k], at(zpos(z), j))

    def zy(k, slot, z):
        return rcopy(es.at[z], er.at[slot], zy_s.at[k], zy_r.at[k], at(zpos(z), j))

    for k in range(1, ZC):
        zx(k, zi, zto(k)).start()

    low = iota((SR, SR), 0) >= iota((SR, SR), 1)
    upp = iota((SR, SR), 0) <= iota((SR, SR), 1)
    lane_head = iota((8, CW), 1) // (CW // HL)
    skips = expand(own_rows(2))[0:8, :]

    def inner(k, carry):
        c = frm(k)

        @pl.when(k > 0)
        def _():
            ccx(k, c, c).wait_recv()

        rows = pl.ds(pl.multiple_of(c * SR, 16), SR)
        cum = cumr[c]
        cols = jnp.concatenate([cum, jnp.zeros((SR - 2 * HL, SR), F32)], axis=0).T
        lds = cum - jnp.log(dtin[c])
        y = jnp.zeros((SR, CW), F32)
        for d, (xs, mask) in enumerate(((xf, low), (xr, upp))):
            xv = xs[rows, :]
            part = slice(d * N, (d + 1) * N)
            score = mm(cc[c, :, part], bb[c, :, part], ((1,), (1,)))
            for q in range(HL):
                row = q if d == 0 else 2 * HL - 1 - q
                seg = jnp.where(mask, cols[:, row:row + 1] - lds[row:row + 1, :], -1e30)
                mcat[:, q * SR:(q + 1) * SR] = (score * jnp.exp(seg)).astype(BF16)
                keep = jnp.where(lane_head == q, 1.0, 0.0)[0:1, :].astype(BF16)
                xbd[q * SR:(q + 1) * SR, :] = xv * keep
            y = y + mm(mcat[...], xbd[...])
            y = y + skips[0:1, d * CW:(d + 1) * CW] * xv.astype(F32)
        yacc[rows, :] = y
        grown[c] = expand(jnp.exp(cum))
        return carry

    lax.fori_loop(0, 3, inner, 0)

    for k in range(1, ZC):
        zx(k, zfrm(k), zfrm(k)).wait_recv()

    pieces, decays = [], []
    for z in range(ZC):
        whole = zr[z].astype(F32)
        pieces.append(whole[0:LB * PR])
        tile = whole[LB * PR:LB * PR + 16]
        decays.append([
            tile[q:q + 1] + tile[LB + q:LB + q + 1] + tile[2 * LB + q:2 * LB + q + 1]
            for q in range(LB)
        ])

    def chain(q, e):
        order = range(ZC) if q < LB // 2 else range(ZC - 1, -1, -1)
        before = [None] * ZC
        for z in order:
            before[z] = e
            e = decays[z][q] * e + pieces[z][q * PR:(q + 1) * PR]
        return before, e

    zero = jnp.zeros((PR, 128), F32)
    if XL > 1:
        for q in range(LB):
            xs_[q * PR:(q + 1) * PR, :] = chain(q, zero)[1]
        cross = rcopy(xs_, xr_, sb_s.at[2], sb_r.at[2], at(across, j))
        cross.start()
        lax.fori_loop(3, 4, inner, 0)
        cross.wait_recv()
    before = []
    for q in range(LB):
        start_from = zero
        if XL > 1:
            takes = xlo == 1 if q < LB // 2 else xlo == 0
            start_from = jnp.where(takes, xr_[q * PR:(q + 1) * PR, :], 0.0)
        before.append(chain(q, start_from)[0])
    for z in range(ZC):
        es[z] = jnp.concatenate([before[q][z] for q in range(LB)], axis=0).astype(BF16)
    er[zi] = es[zi]
    for k in range(1, ZC):
        zy(k, zi, zto(k)).start()
    lax.fori_loop(4 if XL > 1 else 3, NJ, inner, 0)
    for k in range(1, ZC):
        zy(k, zfrm(k), zfrm(k)).wait_recv()
    ring_wait(1)
    ring_start(2)
    for p in range(ZC):
        piece = er[p].astype(F32)
        for q in range(LB):
            ech[pl.ds(pl.multiple_of(core * (N // 2) + p * PR, 8), PR), q * 128:(q + 1) * 128] = (
                piece[q * PR:(q + 1) * PR, :]
            )
    halves = rcopy(ech.at[mine, :], ech.at[mine, :], sb_s.at[3], sb_r.at[3], at(sib, j))
    halves.start()
    for h in swap:
        h.wait_send()
    theirs = pl.ds(pl.multiple_of((1 - core) * (N // 2), 8), N // 2)
    rcopy(ech.at[theirs, :], ech.at[theirs, :], sb_s.at[3], sb_r.at[3], at(sib, j)).wait_recv()
    other_first = fwd_lane == core
    stin[...] = jnp.where(other_first, dec_o[0:1, :] * ech[...] + st_o[...], ech[...])

    def enter(s, carry):
        for d in range(2):
            c = s if d == 0 else NJ - 1 - s
            lanes = slice(d * CW, (d + 1) * CW)
            st = stin[:, lanes]
            top = st.astype(BF16)
            sbs[c, 0:N, lanes] = top
            sbs[c, N:2 * N, lanes] = (st - top.astype(F32)).astype(BF16)
            stin[:, lanes] = dch[c, 0:1, lanes] * st + fresh[c, :, lanes]
        return carry

    lax.fori_loop(0, NJ, enter, 0)

    HB = RB // 2

    def cbx(h, k, slot, dev):
        rows = pl.ds(pl.multiple_of(lax.rem(dev, GROUP) * RB + h * HB, 16), HB)
        return rcopy(
            comb_s.at[rows, :], comb_r.at[slot, pl.ds(h * HB, HB), :],
            cb_s.at[h, k], cb_r.at[h, k], at(i, dev),
        )

    chunks = HB // SR
    for h in range(2):

        def finish(n, carry):
            c = (n // chunks) * (2 * chunks) + h * chunks + lax.rem(n, chunks)
            rows = pl.ds(pl.multiple_of(c * SR, 16), SR)
            y = yacc[rows, :]
            for d in range(2):
                lanes = slice(d * CW, (d + 1) * CW)
                cv = cc[c, :, d * N:(d + 1) * N]
                z = mm(jnp.concatenate([cv, cv], axis=1), sbs[c, :, lanes])
                y = y + grown[c, :, lanes] * z
            comb_s[rows, :] = (y * gain_ref[...]).astype(BF16)
            return carry

        lax.fori_loop(0, NJ // 2, finish, 0)
        for k in far_first:
            cbx(h, k, j, to(k)).start()
    comb_r[j] = comb_s[pl.ds(pl.multiple_of(yy * RB, 16), RB), :]
    ring_wait(2)
    ring_start(3)
    ring_wait(3)
    half = pl.ds(pl.multiple_of(core * (CW // 2), 16), CW // 2)
    rest = pl.ds(pl.multiple_of((1 - core) * (CW // 2), 16), CW // 2)
    share = rcopy(wbuf.at[:, half, :], wbuf.at[:, half, :], sb_s.at[4], sb_r.at[4], at(sib, j))
    share.start()
    for k in range(1, NJ):
        s = frm(k)
        rcopy(gall.at[s], gall.at[s], g_s.at[k], g_r.at[k], at(i, s)).wait_recv()
    rcopy(
        wbuf.at[:, rest, :], wbuf.at[:, rest, :], sb_s.at[4], sb_r.at[4], at(sib, j)
    ).wait_recv()

    def obx(h, k, slot, dest):
        rows = pl.ds(h * HB, HB)
        return rcopy(
            obs.at[dest, rows, :], obr.at[slot, rows, :], ob_s.at[h, k], ob_r.at[h, k],
            at(i, xh * GROUP + dest),
        )

    for h in range(2):
        rows = slice(h * HB, (h + 1) * HB)
        acc[...] = jnp.zeros((HB, WC), F32)
        sqs[...] = jnp.zeros((HB, CW), F32)

        def multiply(b):
            piece = comb_r[b, rows, :]
            value = piece.astype(F32)
            return mm(piece, wbuf[b]), value * value * gall[b, 0:1, :]

        def project(k, carry):
            @pl.when(k > 0)
            def _():
                cbx(h, k, frm(k), frm(k)).wait_recv()

            product, square = multiply(frm(k))
            acc[...] += product
            sqs[...] += square
            return carry

        lax.fori_loop(0, GROUP, project, 0)
        for k in range(GROUP, NJ):
            cbx(h, k, frm(k), frm(k)).wait_recv()
        for k in range(GROUP, NJ):
            product, square = multiply(frm(k))
            acc[...] += product
            sqs[...] += square
        scale = lax.rsqrt(jnp.sum(sqs[...], axis=1, keepdims=True) / D + EPS)
        for q in range(GROUP):
            obs[q, rows, :] = (acc[:, q * CW:(q + 1) * CW] * scale).astype(BF16)
        for k in range(1, GROUP):
            obx(h, k, yy, lax.rem(yy + k, GROUP)).start()
    def place_out(n, src, s, h, size):
        rows = pl.ds(pl.multiple_of(s * RB + h * HB, 16), size)
        return pltpu.make_async_copy(src, out_ref.at[rows, :], oc.at[n])

    outs = [place_out(0, obs.at[yy], yy, 0, RB)]
    outs[0].start()
    for h in range(2):
        for k in range(1, GROUP):
            s = lax.rem(yy + GROUP - k, GROUP)
            obx(h, k, s, s).wait_recv()
            outs.append(
                place_out(h * GROUP + k, obr.at[s, pl.ds(h * HB, HB), :], s, h, HB)
            )
            outs[-1].start()
    for h in outs:
        h.wait()

    slab_pre.wait_send()
    slab_post.wait_send()
    for h in halo:
        h.wait_send()
    for g in gains:
        g.wait_send()
    for k in range(1, NJ):
        xa(k, to(k)).wait_send()
        dtx(k, j, to(k)).wait_send()
        if k <= GROUP:
            bbx(k, j, to(k)).wait_send()
        else:
            relay(k - GROUP, to(GROUP), to(k - GROUP)).wait_send()
        ccx(k, j, to(k)).wait_send()
        if k <= GROUP:
            wx(k, j, to(k)).wait_send()
        else:
            wrelay(k - GROUP, to(GROUP), to(k - GROUP)).wait_send()
        for h in range(2):
            cbx(h, k, j, to(k)).wait_send()

    for k in range(1, ZC):
        zx(k, zi, zto(k)).wait_send()
        zy(k, zi, zto(k)).wait_send()
    if XL > 1:
        cross.wait_send()
    halves.wait_send()
    share.wait_send()
    for d in range(ZC // 2):
        up_ring(d, zfrm(d)).wait_send()
    for d in range(ZC // 2):
        down_ring(d, zto(d)).wait_send()
    for h in range(2):
        for k in range(1, GROUP):
            obx(h, k, yy, lax.rem(yy + k, GROUP)).wait_send()


def shards(x_in, conv_weight, proj_weight, dt_bias, decay_log, skip_gain, norm_gain, out_weight):
    T, CW = x_in.shape
    D = conv_weight.shape[1]
    H = dt_bias.shape[0]
    N = (proj_weight.shape[1] - H) // 2
    NC, NJ = lax.axis_size("ctx"), lax.axis_size("chan")
    HL = H // NJ
    SR = T // NJ
    XL = 2 if NC >= 4 else 1
    ZC = NC // (2 * XL)
    PR, LB = N // 2 // ZC, 2 * CW // 128
    RB, WC = T // GROUP, GROUP * CW
    dma = pltpu.SemaphoreType.DMA
    vm = pltpu.VMEM
    scratch = [
        vm((T + 32, CW), BF16), vm((NJ, SR + 64, CW), BF16), vm((2, SR + 32, CW), F32),
        vm((4, D), F32), vm((T, CW), BF16), vm((T, CW), BF16),
        vm((NJ, SR, 2 * N), BF16), vm((NJ, SR, 2 * N), BF16),
        vm((NJ, 2 * HL, SR), F32), vm((NJ, 2 * HL, SR), F32),
        vm((NJ, 2 * HL, SR), F32),
        vm((NJ, N, 2 * CW), F32), vm((NJ, 8, 2 * CW), F32), vm((T, CW), F32),
        vm((SR, HL * SR), BF16), vm((HL * SR, CW), BF16), vm((6 * HL, 2 * CW), BF16),
        vm((ZC, LB * PR + 16, 128), BF16), vm((ZC, LB * PR + 16, 128), BF16),
        vm((ZC, LB * PR, 128), BF16), vm((ZC, LB * PR, 128), BF16),
        vm((LB * PR, 128), F32), vm((LB * PR, 128), F32),
        vm((N, 2 * CW), F32), vm((N, 2 * CW), F32), vm((8, 2 * CW), F32), vm((8, 2 * CW), F32),
        vm((N, 2 * CW), F32),
        vm((T, CW), BF16), vm((NJ, RB, CW), BF16), vm((NJ, 8, CW), F32),
        vm((NJ, CW, WC), BF16), vm((RB // 2, WC), F32),
        vm((GROUP, RB, CW), BF16), vm((GROUP, RB, CW), BF16),
        vm((RB // 2, CW), F32), vm((NJ, SR, 2 * CW), F32), vm((NJ, 2 * N, 2 * CW), BF16),
        dma((NJ,)), dma((NJ,)), dma((4,)), dma((2 + NJ,)), dma((NJ,)), dma((NJ,)),
        dma((NJ,)), dma((NJ,)), dma((4,)), dma((4,)), dma((4,)), dma((4,)),
        dma((NJ,)), dma((NJ,)), dma((NJ,)), dma((NJ,)), dma((NJ,)), dma((NJ,)),
        dma((ZC,)), dma((ZC,)), dma((ZC,)), dma((ZC,)), dma((5,)), dma((5,)),
        dma((2, NJ)), dma((2, NJ)), dma((2, GROUP)), dma((2, GROUP)),
        vm(proj_weight.shape, BF16), vm(proj_weight.shape, BF16),
        vm(proj_weight.shape[::-1], BF16), vm((3, H, 128), F32), dma((9,)),
        vm((4, D), F32), vm((1, H), F32), vm((1, H), F32), vm((1, H), F32), vm((1, CW), F32), dma((2 * GROUP,)),
    ]
    return pl.pallas_call(
        functools.partial(kernel, (NC, NJ, T, CW, D, N, HL, XL, ZC)),
        out_shape=jax.ShapeDtypeStruct((T, CW), BF16),
        in_specs=[pl.BlockSpec(memory_space=pl.ANY)] * 8,
        out_specs=pl.BlockSpec(memory_space=pl.ANY),
        scratch_shapes=scratch,
        compiler_params=pltpu.CompilerParams(
            collective_id=0, has_side_effects=True, vmem_limit_bytes=62 * 1024 * 1024
        ),
        cost_estimate=pl.CostEstimate(
            flops=4 * T * D * CW, bytes_accessed=8 * T * CW, transcendentals=16 * T * SR
        ),
    )(
        x_in, conv_weight, proj_weight.T, dt_bias[None], decay_log[None], skip_gain[None],
        norm_gain[None], out_weight,
    )


def solution(mesh):
    in_specs = (P("ctx", "chan"), P(), P(), P(), P(), P(), P("chan"), P("chan", None))
    out_specs = P("ctx", "chan")
    return jax.shard_map(shards, mesh=mesh, in_specs=in_specs, out_specs=out_specs, check_vma=False)
```
